512 devices in a mesh: rows: 32 (over y, x), cols: 16 (over z, core).
Axes of the slice: x: 4, y: 8, z: 8, core: 2. Of those that a mesh axis runs over, the one named last changes fastest.
Arguments:
- micrograph: float32 [2048, 32768], P('rows', 'cols'), may hold values from -6 to 6
- thresholds: float32 [4, 3], replicated, may hold values from 0.2 to 1.5
Outputs:
- denoised: float32 [2048, 32768], P('rows', 'cols')
The draws below stay inside these ranges and needn't reach their ends.
All inputs are finite; a program needn't handle non-finite values.
Results may differ from the reference program's by a relative error of at most 0.00002.
Values sent between devices are 32-bit elements; how exact they have to be, the bound alone decides.
No kernel may reach another device: no remote copies, remote signals or barrier semaphores. Data moves between devices by JAX's collectives and lax.ppermute only.
A program may use at most 64 MiB of HBM per device.

```python
import math
import jax
import jax.numpy as jnp
from jax import lax

LEVELS = 4
NR = 2048
NC = 32768


def levels(rng, shape, split, smallest, top_value):
    gain = 1.0
    for position, shards_of in split:
        heights = jax.random.uniform(jax.random.fold_in(jax.random.fold_in(rng, 6), position), (shards_of,), jnp.float32, smallest / len(split), top_value / len(split))
        gain = gain * jnp.repeat(jnp.exp(heights), shape[position] // shards_of).reshape((-1,) + (1,) * (len(shape) - 1 - position))
    return gain


def noise(own_key, shape, scale, reach, shards=(), held_as=jnp.bfloat16):
    factor_of = levels(own_key, shape, shards, -0.22, 0.18) if shards else 1.0
    values = jax.random.normal(own_key, shape, jnp.float32) * scale * factor_of
    return jnp.minimum(jnp.maximum(values, -reach), reach).astype(held_as)


def setup_inputs(seed: int = 0) -> dict:
    streams_of = jax.random.split(jax.random.key(seed), 3)
    return {
        "micrograph": noise(streams_of[0], (NR, NC), 1.0, 6.0, ((0, 32), (1, 16)), jnp.float32),
        "thresholds": jnp.clip(jnp.exp(jax.random.uniform(streams_of[1], (LEVELS, 3), jnp.float32, math.log(0.2), math.log(1.5))), 0.2, 1.5),
    }


step_one = -1.586134342
step_two = -0.05298011854
step_three = 0.8829110762
step_four = 0.4435068522
band_gain = 1.149604398


def section(array, start, stop, direction):
    return lax.slice_in_dim(array, start, stop, 1, direction)


def alternate(leading, trailing, direction):
    stacked = jnp.stack([leading, trailing], direction + 1)
    new_shape = list(leading.shape)
    new_shape[direction] = new_shape[direction] * 2
    return stacked.reshape(new_shape)


def forward_lift(padded, direction):
    length = padded.shape[direction] - 8
    half_len = length // 2
    even_part = lax.slice_in_dim(padded, 0, length + 8, 2, direction)
    odd_part = lax.slice_in_dim(padded, 1, length + 8, 2, direction)
    odd_one = section(odd_part, 0, half_len + 3, direction) + step_one * (section(even_part, 0, half_len + 3, direction) + section(even_part, 1, half_len + 4, direction))
    even_one = section(even_part, 1, half_len + 3, direction) + step_two * (section(odd_one, 0, half_len + 2, direction) + section(odd_one, 1, half_len + 3, direction))
    odd_two = section(odd_one, 1, half_len + 2, direction) + step_three * (section(even_one, 0, half_len + 1, direction) + section(even_one, 1, half_len + 2, direction))
    even_two = section(even_one, 1, half_len + 1, direction) + step_four * (section(odd_two, 0, half_len, direction) + section(odd_two, 1, half_len + 1, direction))
    return even_two * band_gain, section(odd_two, 1, half_len + 1, direction) / band_gain


def inverse_lift(padded, direction):
    length = padded.shape[direction] - 8
    half_len = length // 2
    even_two = lax.slice_in_dim(padded, 0, length + 8, 2, direction) / band_gain
    odd_two = lax.slice_in_dim(padded, 1, length + 8, 2, direction) * band_gain
    even_one = section(even_two, 1, half_len + 4, direction) - step_four * (section(odd_two, 0, half_len + 3, direction) + section(odd_two, 1, half_len + 4, direction))
    odd_one = section(odd_two, 1, half_len + 3, direction) - step_three * (section(even_one, 0, half_len + 2, direction) + section(even_one, 1, half_len + 3, direction))
    even_zero = section(even_one, 1, half_len + 2, direction) - step_two * (section(odd_one, 0, half_len + 1, direction) + section(odd_one, 1, half_len + 2, direction))
    odd_zero = section(odd_one, 1, half_len + 1, direction) - step_one * (section(even_zero, 0, half_len, direction) + section(even_zero, 1, half_len + 1, direction))
    return alternate(section(even_zero, 0, half_len, direction), odd_zero, direction)


def mirror(current, direction):
    widths = [(0, 0), (0, 0)]
    widths[direction] = (4, 4)
    return jnp.pad(current, widths, mode="reflect")


def soften(coeffs, limit):
    return coeffs - jnp.clip(coeffs, -limit, limit)


def reference(micrograph, thresholds):
    current = micrograph
    details = []
    for level_index in range(LEVELS):
        width_now = current.shape[1] // 2
        low_cols, high_cols = forward_lift(mirror(current, 1), 1)
        joined = jnp.concatenate([low_cols, high_cols], 1)
        low_band, high_band = forward_lift(mirror(joined, 0), 0)
        band_right = soften(low_band[:, width_now:], thresholds[level_index, 0])
        lower_left = soften(high_band[:, :width_now], thresholds[level_index, 1])
        lower_right = soften(high_band[:, width_now:], thresholds[level_index, 2])
        details.append((band_right, lower_left, lower_right))
        current = low_band[:, :width_now]
    for level_index in range(LEVELS - 1, -1, -1):
        band_right, lower_left, lower_right = details[level_index]
        upper_half = jnp.concatenate([current, band_right], 1)
        bottom = jnp.concatenate([lower_left, lower_right], 1)
        rows_mixed = alternate(upper_half, bottom, 0)
        half_cols = rows_mixed.shape[1] // 2
        full_grid = alternate(rows_mixed[:, :half_cols], rows_mixed[:, half_cols:], 1)
        current = inverse_lift(mirror(full_grid, 0), 0)
        current = inverse_lift(mirror(current, 1), 1)
    return current
```

```python
import functools

import jax
import jax.numpy as jnp
from jax import lax
from jax.experimental import pallas as pl
from jax.experimental.pallas import tpu as pltpu
from jax.sharding import PartitionSpec as P

LEVELS = 4

step_one = -1.586134342
step_two = -0.05298011854
step_three = 0.8829110762
step_four = 0.4435068522
band_gain = 1.149604398
inv_gain = 1.0 / band_gain

ROWS, COLS = 64, 2048
WIDE = (1152, 640, 384, 256)
EDGE = (64, 32, 16, 8)
TALL = (96, 48, 24, 16)
OWN = (32, 16, 8, 4)


def soften(coeffs, limit):
    return coeffs - jnp.clip(coeffs, -limit, limit)


def patch(shifted, source, axis, index, flag):
    unit = 8 if axis == 0 else 128
    lo = index // unit * unit
    hi = min(lo + unit, shifted.shape[axis])
    cut = functools.partial(lax.slice_in_dim, axis=axis)
    tile = cut(shifted, lo, hi)
    here = (lax.broadcasted_iota(jnp.int32, tile.shape, axis) == index - lo) & flag
    tile = jnp.where(here, cut(source, lo, hi), tile)
    parts = [cut(shifted, 0, lo)] if lo else []
    parts.append(tile)
    if hi < shifted.shape[axis]:
        parts.append(cut(shifted, hi, shifted.shape[axis]))
    return jnp.concatenate(parts, axis) if len(parts) > 1 else tile


def neighbours(axis, first, count, at_start, at_end):
    def before(odd):
        return patch(pltpu.roll(odd, 1, axis), odd, axis, first, at_start)

    def after(even):
        rolled = pltpu.roll(even, even.shape[axis] - 1, axis)
        return patch(rolled, even, axis, first + count - 1, at_end)

    return before, after


def forward_lift(even, odd, near):
    before, after = near
    odd = odd + step_one * (even + after(even))
    even = even + step_two * (before(odd) + odd)
    odd = odd + step_three * (even + after(even))
    even = even + step_four * (before(odd) + odd)
    return even * band_gain, odd * inv_gain


def inverse_lift(low, high, near):
    before, after = near
    even = low * inv_gain
    odd = high * band_gain
    even = even - step_four * (before(odd) + odd)
    odd = odd - step_three * (even + after(even))
    even = even - step_two * (before(odd) + odd)
    odd = odd - step_one * (even + after(even))
    return even, odd


def pairing(transpose):
    a = lax.broadcasted_iota(jnp.int32, (256, 256), 1 if not transpose else 0)
    b = lax.broadcasted_iota(jnp.int32, (256, 256), 0 if not transpose else 1)
    target = jnp.where(a < 128, 2 * a, 2 * a - 255)
    return jnp.where(b == target, 1.0, 0.0).astype(jnp.bfloat16)


def permuted(x, matrix):
    rows = x.shape[0]
    high = x.astype(jnp.bfloat16)
    rest = x - high.astype(jnp.float32)
    middle = rest.astype(jnp.bfloat16)
    last = (rest - middle.astype(jnp.float32)).astype(jnp.bfloat16)
    out = jnp.dot(
        jnp.concatenate([high, middle, last], 0), matrix, preferred_element_type=jnp.float32
    )
    return (out[:rows] + out[rows : 2 * rows]) + out[2 * rows :]


def tiles(width, body):
    def step(t, carry):
        body(t, pl.ds(pl.multiple_of(t * 128, 128), 128))
        return carry

    lax.fori_loop(0, width // 128, step, 0)


def row_groups(rows, body):
    def step(t, carry):
        body(pl.ds(pl.multiple_of(t * 8, 8), 8))
        return carry

    lax.fori_loop(0, rows // 8, step, 0)


def joined(ref, rows, width):
    return jnp.concatenate([ref[k, rows] for k in range(width // 128)], 1)


def spread(ref, rows, value):
    for k in range(value.shape[1] // 128):
        ref[k, rows] = value[:, 128 * k : 128 * k + 128]


def ends(axis):
    position = lax.axis_index(axis)
    return position % 2 == 0, position == 0, position == lax.axis_size(axis) - 1


def columns_kernel(x_ref, odd_ref, even_ref, send_ref, high_ref, e_ref, o_ref):
    is_even, at_start, at_end = ends("cols")
    matrix = pairing(False)
    left = jnp.where(is_even, odd_ref[:, 128:], even_ref[:, 128:])
    right = jnp.where(is_even, even_ref[:, :128], odd_ref[:, :128])
    for k in range(9):
        if k == 0:
            chunk = jnp.concatenate([left, x_ref[:, :128]], 1)
        elif k == 8:
            chunk = jnp.concatenate([x_ref[:, COLS - 128 :], right], 1)
        else:
            chunk = x_ref[:, 256 * k - 128 : 256 * k + 128]
        both = permuted(chunk, matrix)
        e_ref[:, 128 * k : 128 * k + 128] = both[:, :128]
        o_ref[:, 128 * k : 128 * k + 128] = both[:, 128:]
    near = neighbours(1, EDGE[0], 1024, at_start, at_end)

    def lift(g):
        low, high = forward_lift(e_ref[g, :], o_ref[g, :], near)
        send_ref[g, :] = low
        high_ref[g, :] = high

    row_groups(ROWS, lift)
    send_ref[64:72, :] = high_ref[0:8, :]
    send_ref[72:80, :] = high_ref[56:64, :]


def forward_kernel(t_ref, own_ref, high_ref, odd_ref, even_ref, pack_even, pack_odd, *rest):
    outs, (l_ref, h_ref, b_ref, e_ref, o_ref) = rest[:13], rest[13:]
    is_even, at_start, at_end = ends("rows")
    _, left_end, right_end = ends("cols")
    matrix = pairing(False)

    def gather(t, s):
        l_ref[t, 0:64] = jnp.where(is_even, odd_ref[0:64, s], even_ref[0:64, s])
        l_ref[t, 64:128] = own_ref[0:64, s]
        l_ref[t, 128:192] = jnp.where(is_even, even_ref[0:64, s], odd_ref[0:64, s])
        h_ref[t, 8:16] = jnp.where(is_even, odd_ref[72:80, s], even_ref[72:80, s])
        h_ref[t, 16:80] = high_ref[:, s]
        h_ref[t, 80:88] = jnp.where(is_even, even_ref[64:72, s], odd_ref[64:72, s])

    tiles(WIDE[0], gather)

    def share(level, kind, s, coeffs):
        own = OWN[level]
        outs[3 * level + kind][4 : 4 + own, s] = coeffs
        edge = 2 if level == 0 else 4
        first, last = coeffs[:edge], coeffs[own - edge :]
        at = 2 * kind if level == 0 else 8 + 4 * kind
        lanes = s
        shift = (0, 0, 640, 1024)[level]
        if shift:
            lanes = pl.ds(pl.multiple_of(s.start + shift, 128), 128)
        pack_even[at : at + edge, lanes] = jnp.where(is_even, last, first)
        pack_odd[at : at + edge, lanes] = jnp.where(is_even, first, last)

    for level in range(LEVELS):
        tall, own = TALL[level], OWN[level]
        begin = (32, 16, 8, 4)[level]
        near = neighbours(0, begin, own, at_start, at_end)
        h_tall, h_begin = (48, 8) if level == 0 else (tall, begin)
        h_near = neighbours(0, h_begin, own, at_start, at_end)

        def lift_low(t, s, level=level, tall=tall, own=own, begin=begin, near=near):
            low, high = forward_lift(
                l_ref[t, pl.ds(0, tall, stride=2)], l_ref[t, pl.ds(1, tall, stride=2)], near
            )
            share(level, 1, s, soften(high[begin : begin + own], t_ref[level, 1]))
            if level < LEVELS - 1:
                b_ref[0:tall, s] = low
            else:
                share(level, 3, s, low[begin : begin + own])

        def lift_high(t, s, level=level, own=own, tall=h_tall, begin=h_begin, near=h_near):
            low, high = forward_lift(
                h_ref[t, pl.ds(0, tall, stride=2)], h_ref[t, pl.ds(1, tall, stride=2)], near
            )
            share(level, 0, s, soften(low[begin : begin + own], t_ref[level, 0]))
            share(level, 2, s, soften(high[begin : begin + own], t_ref[level, 2]))

        tiles(WIDE[level], lift_low)
        tiles(WIDE[level], lift_high)
        if level == LEVELS - 1:
            break
        rows = max(tall, 32)
        if tall < rows:
            b_ref[tall:rows, : WIDE[level]] = jnp.zeros((rows - tall, WIDE[level]), jnp.float32)
        wide = WIDE[level + 1]
        if 2 * wide > WIDE[level]:
            b_ref[0:rows, WIDE[level] : 2 * wide] = jnp.zeros((rows, 2 * wide - WIDE[level]), jnp.float32)
        for k in range(wide // 128):
            both = permuted(b_ref[0:rows, 256 * k : 256 * k + 256], matrix)
            e_ref[0:rows, 128 * k : 128 * k + 128] = both[:, :128]
            o_ref[0:rows, 128 * k : 128 * k + 128] = both[:, 128:]
        along = neighbours(1, EDGE[level + 1], 1024 >> (level + 1), left_end, right_end)

        def lift_across(g, wide=wide, along=along):
            low, high = forward_lift(e_ref[g, :wide], o_ref[g, :wide], along)
            spread(l_ref, g, low)
            spread(h_ref, g, high)

        row_groups(rows, lift_across)


def inverse_kernel(odd_ref, even_ref, *rest):
    ins, out_ref, (p_ref, v_ref, w_ref, r_ref), kept = rest[:13], rest[13], rest[14:18], rest[18:]
    is_even, at_start, at_end = ends("rows")
    _, left_end, right_end = ends("cols")
    matrix = pairing(True)

    def choose(t, s):
        up = jnp.where(is_even, odd_ref[:, s], even_ref[:, s])
        down = jnp.where(is_even, even_ref[:, s], odd_ref[:, s])
        p_ref[0:24, s] = up
        p_ref[24:48, s] = down

    tiles(1280, choose)
    for level in range(LEVELS - 1, -1, -1):
        own = OWN[level]
        long = max(own + 8, 16)
        near = neighbours(0, 4, own, at_start, at_end)
        shift = (0, 0, 640, 1024)[level]
        edge = 2 if level == 0 else 4

        def halo(kind, s, level=level, own=own, edge=edge, shift=shift):
            source, target = ins[3 * level + kind], kept[kind]
            at = 2 * kind if level == 0 else 8 + 4 * kind
            lanes = s
            if shift:
                lanes = pl.ds(pl.multiple_of(s.start + shift, 128), 128)
            target[0 : own + 8, s] = source[0 : own + 8, s]
            target[4 - edge : 4, s] = p_ref[at : at + edge, lanes]
            target[4 + own : 4 + own + edge, s] = p_ref[24 + at : 24 + at + edge, lanes]

        def lift_down(t, s, level=level, long=long, near=near, halo=halo):
            for kind in range(4 if level == LEVELS - 1 else 3):
                halo(kind, s)
            low = kept[3][0:long, s] if level == LEVELS - 1 else r_ref[4 : 4 + long, s]
            even, odd = inverse_lift(low, kept[1][0:long, s], near)
            v_ref[t, pl.ds(0, long, stride=2)] = even
            v_ref[t, pl.ds(1, long, stride=2)] = odd
            even, odd = inverse_lift(kept[0][0:long, s], kept[2][0:long, s], near)
            w_ref[t, pl.ds(0, long, stride=2)] = even
            w_ref[t, pl.ds(1, long, stride=2)] = odd

        wide = WIDE[level]
        tiles(wide, lift_down)
        along = neighbours(1, EDGE[level], 1024 >> level, left_end, right_end)
        first, rows = (8, 64) if level == 0 else (0, 2 * long)

        def lift_across(g, wide=wide, along=along, first=first):
            at = pl.ds(pl.multiple_of(g.start + first, 8), 8)
            even, odd = inverse_lift(joined(v_ref, at, wide), joined(w_ref, at, wide), along)
            spread(v_ref, at, even)
            spread(w_ref, at, odd)

        row_groups(rows, lift_across)
        for k in range(wide // 128):
            cut = slice(first, first + rows)
            both = permuted(jnp.concatenate([v_ref[k, cut], w_ref[k, cut]], 1), matrix)
            if level:
                r_ref[0:rows, 256 * k : 256 * k + 256] = both
            elif k == 0:
                out_ref[:, :128] = both[:, 128:]
            elif k == 8:
                out_ref[:, COLS - 128 :] = both[:, :128]
            else:
                out_ref[:, 256 * k - 128 : 256 * k + 128] = both


def swaps(axis, offset):
    count = lax.axis_size(axis)
    pairs = []
    for i in range(offset, count - 1, 2):
        pairs += [(i, i + 1), (i + 1, i)]
    return pairs


def exchange(for_even, for_odd, axis):
    even = lax.ppermute(for_even, axis, swaps(axis, 0))
    odd = lax.ppermute(for_odd, axis, swaps(axis, 1))
    return odd, even


def f32(*shape):
    return jax.ShapeDtypeStruct(shape, jnp.float32)


def scratch(*shape):
    return pltpu.VMEM(shape, jnp.float32)


def call(kernel, outs, scratches, *args, scalars=0):
    vmem = pl.BlockSpec(memory_space=pltpu.VMEM)
    smem = pl.BlockSpec(memory_space=pltpu.SMEM)
    return pl.pallas_call(
        kernel,
        out_shape=outs,
        in_specs=[smem] * scalars + [vmem] * (len(args) - scalars),
        out_specs=jax.tree.map(lambda _: vmem, outs),
        scratch_shapes=scratches,
        compiler_params=pltpu.CompilerParams(vmem_limit_bytes=16 * 2**20),
    )(*args)


def local(micrograph, thresholds):
    edges = jnp.concatenate([micrograph[:, :128], micrograph[:, COLS - 128 :]], 1)
    odd, even = exchange(edges, edges, "cols")
    block, high = call(
        columns_kernel,
        (f32(80, 1152), f32(64, 1152)),
        [scratch(64, 1152), scratch(64, 1152)],
        micrograph,
        odd,
        even,
    )
    odd, even = exchange(block, block, "rows")
    shapes = [f32(OWN[level] + 8, WIDE[level]) for level in range(LEVELS) for _ in range(3)]
    shapes.append(shapes[-1])
    pack_even, pack_odd, *bands = call(
        forward_kernel,
        (f32(24, 1280), f32(24, 1280), *shapes),
        [
            scratch(9, 192, 128),
            scratch(9, 96, 128),
            scratch(96, 1280),
            scratch(96, 640),
            scratch(96, 640),
        ],
        thresholds,
        block,
        high,
        odd,
        even,
        scalars=1,
    )
    odd, even = exchange(pack_even, pack_odd, "rows")
    return call(
        inverse_kernel,
        f32(ROWS, COLS),
        [scratch(48, 1280), scratch(9, 80, 128), scratch(9, 80, 128), scratch(48, 1280)]
        + [scratch(40, 1152)] * 3
        + [scratch(16, 256)],
        odd,
        even,
        *bands,
    )


def solution(mesh):
    placed = (P("rows", "cols"), P())
    return jax.shard_map(
        local, mesh=mesh, in_specs=placed, out_specs=P("rows", "cols"), check_vma=False
    )
```

```python
import functools

import jax
import jax.numpy as jnp
from jax import lax
from jax.experimental import pallas as pl
from jax.experimental.pallas import tpu as pltpu
from jax.sharding import PartitionSpec as P

LEVELS = 4

step_one = -1.586134342
step_two = -0.05298011854
step_three = 0.8829110762
step_four = 0.4435068522
band_gain = 1.149604398
inv_gain = 1.0 / band_gain

ROWS, COLS = 64, 2048
WIDE = (1152, 640, 384, 256)
EDGE = (64, 32, 16, 8)
TALL = (96, 48, 24, 16)
OWN = (32, 16, 8, 4)


def soften(coeffs, limit):
    return coeffs - jnp.clip(coeffs, -limit, limit)


def patch(shifted, source, axis, index, flag):
    unit = 8 if axis == 0 else 128
    lo = index // unit * unit
    hi = min(lo + unit, shifted.shape[axis])
    cut = functools.partial(lax.slice_in_dim, axis=axis)
    tile = cut(shifted, lo, hi)
    here = (lax.broadcasted_iota(jnp.int32, tile.shape, axis) == index - lo) & flag
    tile = jnp.where(here, cut(source, lo, hi), tile)
    parts = [cut(shifted, 0, lo)] if lo else []
    parts.append(tile)
    if hi < shifted.shape[axis]:
        parts.append(cut(shifted, hi, shifted.shape[axis]))
    return jnp.concatenate(parts, axis) if len(parts) > 1 else tile


def neighbours(axis, first, count, at_start, at_end):
    def before(odd):
        return patch(pltpu.roll(odd, 1, axis), odd, axis, first, at_start)

    def after(even):
        rolled = pltpu.roll(even, even.shape[axis] - 1, axis)
        return patch(rolled, even, axis, first + count - 1, at_end)

    return before, after


def forward_lift(even, odd, near):
    before, after = near
    odd = odd + step_one * (even + after(even))
    even = even + step_two * (before(odd) + odd)
    odd = odd + step_three * (even + after(even))
    even = even + step_four * (before(odd) + odd)
    return even * band_gain, odd * inv_gain


def inverse_lift(low, high, near):
    before, after = near
    even = low * inv_gain
    odd = high * band_gain
    even = even - step_four * (before(odd) + odd)
    odd = odd - step_three * (even + after(even))
    even = even - step_two * (before(odd) + odd)
    odd = odd - step_one * (even + after(even))
    return even, odd


def pairing(transpose):
    a = lax.broadcasted_iota(jnp.int32, (256, 256), 1 if not transpose else 0)
    b = lax.broadcasted_iota(jnp.int32, (256, 256), 0 if not transpose else 1)
    target = jnp.where(a < 128, 2 * a, 2 * a - 255)
    return jnp.where(b == target, 1.0, 0.0).astype(jnp.bfloat16)


def permuted(x, matrix):
    rows = x.shape[0]
    high = x.astype(jnp.bfloat16)
    rest = x - high.astype(jnp.float32)
    middle = rest.astype(jnp.bfloat16)
    last = (rest - middle.astype(jnp.float32)).astype(jnp.bfloat16)
    out = jnp.dot(
        jnp.concatenate([high, middle, last], 0), matrix, preferred_element_type=jnp.float32
    )
    return (out[:rows] + out[rows : 2 * rows]) + out[2 * rows :]


def tiles(width, body):
    def step(t, carry):
        body(t, pl.ds(pl.multiple_of(t * 128, 128), 128))
        return carry

    lax.fori_loop(0, width // 128, step, 0)


def row_groups(rows, size, body):
    def step(t, carry):
        body(pl.ds(pl.multiple_of(t * size, 8), size))
        return carry

    if size == rows:
        body(pl.ds(0, rows))
    else:
        lax.fori_loop(0, rows // size, step, 0)


def joined(ref, rows, width):
    return jnp.concatenate([ref[k, rows] for k in range(width // 128)], 1)


def spread(ref, rows, value):
    for k in range(value.shape[1] // 128):
        ref[k, rows] = value[:, 128 * k : 128 * k + 128]


def ends(axis):
    position = lax.axis_index(axis)
    return position % 2 == 0, position == 0, position == lax.axis_size(axis) - 1


def edges_kernel(x_ref, for_even, for_odd, sems):
    is_even = ends("cols")[0]
    right = jnp.where(is_even, COLS - 128, 0)
    copies = []
    for k, (at, out) in enumerate(((right, for_even), (COLS - 128 - right, for_odd))):
        lanes = pl.ds(pl.multiple_of(at, 128), 128)
        copies.append(pltpu.make_async_copy(x_ref.at[:, lanes], out, sems.at[k]))
        copies[-1].start()
    for copy in copies:
        copy.wait()


def inner_kernel(x_ref, e_ref, o_ref, edge_ref):
    matrix = pairing(False)
    for k in range(7):
        both = permuted(x_ref[:, 256 * k + 128 : 256 * k + 384], matrix)
        e_ref[:, 128 * k : 128 * k + 128] = both[:, :128]
        o_ref[:, 128 * k : 128 * k + 128] = both[:, 128:]
    edge_ref[:, :128] = x_ref[:, :128]
    edge_ref[:, 128:] = x_ref[:, COLS - 128 :]


def columns_kernel(e_ref, o_ref, edge_ref, odd_ref, even_ref, send_ref, high_ref):
    is_even, at_start, at_end = ends("cols")
    matrix = pairing(False)
    left = jnp.where(is_even, odd_ref[...], even_ref[...])
    right = jnp.where(is_even, even_ref[...], odd_ref[...])
    first = permuted(jnp.concatenate([left, edge_ref[:, :128]], 1), matrix)
    last = permuted(jnp.concatenate([edge_ref[:, 128:], right], 1), matrix)
    near = neighbours(1, EDGE[0], 1024, at_start, at_end)
    low, high = forward_lift(
        jnp.concatenate([first[:, :128], e_ref[...], last[:, :128]], 1),
        jnp.concatenate([first[:, 128:], o_ref[...], last[:, 128:]], 1),
        near,
    )
    send_ref[0:64, :] = low
    high_ref[...] = high
    send_ref[64:72, :] = high[0:8]
    send_ref[72:80, :] = high[56:64]


def forward_kernel(t_ref, own_ref, high_ref, odd_ref, even_ref, pack_even, pack_odd, *rest):
    outs, (l_ref, h_ref, b_ref, e_ref, o_ref) = rest[:13], rest[13:]
    is_even, at_start, at_end = ends("rows")
    _, left_end, right_end = ends("cols")
    matrix = pairing(False)

    def gather(t, s):
        l_ref[t, 0:64] = jnp.where(is_even, odd_ref[0:64, s], even_ref[0:64, s])
        l_ref[t, 64:128] = own_ref[0:64, s]
        l_ref[t, 128:192] = jnp.where(is_even, even_ref[0:64, s], odd_ref[0:64, s])
        h_ref[t, 8:16] = jnp.where(is_even, odd_ref[72:80, s], even_ref[72:80, s])
        h_ref[t, 16:80] = high_ref[:, s]
        h_ref[t, 80:88] = jnp.where(is_even, even_ref[64:72, s], odd_ref[64:72, s])

    tiles(WIDE[0], gather)

    def share(level, kind, s, coeffs):
        own = OWN[level]
        outs[3 * level + kind][4 : 4 + own, s] = coeffs
        edge = 2 if level == 0 else 4
        first, last = coeffs[:edge], coeffs[own - edge :]
        at = 2 * kind if level == 0 else 8 + 4 * kind
        lanes = s
        shift = (0, 0, 640, 1024)[level]
        if shift:
            lanes = pl.ds(pl.multiple_of(s.start + shift, 128), 128)
        pack_even[at : at + edge, lanes] = jnp.where(is_even, last, first)
        pack_odd[at : at + edge, lanes] = jnp.where(is_even, first, last)

    for level in range(LEVELS):
        tall, own = TALL[level], OWN[level]
        begin = (32, 16, 8, 4)[level]
        near = neighbours(0, begin, own, at_start, at_end)
        h_tall, h_begin = (48, 8) if level == 0 else (tall, begin)
        h_near = neighbours(0, h_begin, own, at_start, at_end)

        def lift_low(t, s, level=level, tall=tall, own=own, begin=begin, near=near):
            low, high = forward_lift(
                l_ref[t, pl.ds(0, tall, stride=2)], l_ref[t, pl.ds(1, tall, stride=2)], near
            )
            share(level, 1, s, soften(high[begin : begin + own], t_ref[level, 1]))
            if level < LEVELS - 1:
                b_ref[0:tall, s] = low
            else:
                share(level, 3, s, low[begin : begin + own])

        def lift_high(t, s, level=level, own=own, tall=h_tall, begin=h_begin, near=h_near):
            low, high = forward_lift(
                h_ref[t, pl.ds(0, tall, stride=2)], h_ref[t, pl.ds(1, tall, stride=2)], near
            )
            share(level, 0, s, soften(low[begin : begin + own], t_ref[level, 0]))
            share(level, 2, s, soften(high[begin : begin + own], t_ref[level, 2]))

        tiles(WIDE[level], lift_low)
        tiles(WIDE[level], lift_high)
        if level == LEVELS - 1:
            break
        rows = max(tall, 32)
        if tall < rows:
            b_ref[tall:rows, : WIDE[level]] = jnp.zeros((rows - tall, WIDE[level]), jnp.float32)
        wide = WIDE[level + 1]
        if 2 * wide > WIDE[level]:
            b_ref[0:rows, WIDE[level] : 2 * wide] = jnp.zeros((rows, 2 * wide - WIDE[level]), jnp.float32)
        for k in range(wide // 128):
            both = permuted(b_ref[0:rows, 256 * k : 256 * k + 256], matrix)
            e_ref[0:rows, 128 * k : 128 * k + 128] = both[:, :128]
            o_ref[0:rows, 128 * k : 128 * k + 128] = both[:, 128:]
        along = neighbours(1, EDGE[level + 1], 1024 >> (level + 1), left_end, right_end)

        def lift_across(g, wide=wide, along=along):
            low, high = forward_lift(e_ref[g, :wide], o_ref[g, :wide], along)
            spread(l_ref, g, low)
            spread(h_ref, g, high)

        row_groups(rows, rows, lift_across)


def inverse_kernel(odd_ref, even_ref, *rest):
    ins, out_ref, (p_ref, v_ref, w_ref, r_ref), kept = rest[:13], rest[13], rest[14:18], rest[18:]
    is_even, at_start, at_end = ends("rows")
    _, left_end, right_end = ends("cols")
    matrix = pairing(True)

    def choose(t, s):
        up = jnp.where(is_even, odd_ref[:, s], even_ref[:, s])
        down = jnp.where(is_even, even_ref[:, s], odd_ref[:, s])
        p_ref[0:24, s] = up
        p_ref[24:48, s] = down

    tiles(1280, choose)
    for level in range(LEVELS - 1, -1, -1):
        own = OWN[level]
        long = max(own + 8, 16)
        near = neighbours(0, 4, own, at_start, at_end)
        shift = (0, 0, 640, 1024)[level]
        edge = 2 if level == 0 else 4

        def halo(kind, s, level=level, own=own, edge=edge, shift=shift):
            source, target = ins[3 * level + kind], kept[kind]
            at = 2 * kind if level == 0 else 8 + 4 * kind
            lanes = s
            if shift:
                lanes = pl.ds(pl.multiple_of(s.start + shift, 128), 128)
            target[0 : own + 8, s] = source[0 : own + 8, s]
            target[4 - edge : 4, s] = p_ref[at : at + edge, lanes]
            target[4 + own : 4 + own + edge, s] = p_ref[24 + at : 24 + at + edge, lanes]

        def lift_down(t, s, level=level, long=long, near=near, halo=halo):
            for kind in range(4 if level == LEVELS - 1 else 3):
                halo(kind, s)
            low = kept[3][0:long, s] if level == LEVELS - 1 else r_ref[4 : 4 + long, s]
            even, odd = inverse_lift(low, kept[1][0:long, s], near)
            v_ref[t, pl.ds(0, long, stride=2)] = even
            v_ref[t, pl.ds(1, long, stride=2)] = odd
            even, odd = inverse_lift(kept[0][0:long, s], kept[2][0:long, s], near)
            w_ref[t, pl.ds(0, long, stride=2)] = even
            w_ref[t, pl.ds(1, long, stride=2)] = odd

        wide = WIDE[level]
        tiles(wide, lift_down)
        along = neighbours(1, EDGE[level], 1024 >> level, left_end, right_end)
        first, rows = (8, 64) if level == 0 else (0, 2 * long)

        def lift_across(g, wide=wide, along=along, first=first):
            at = pl.ds(g.start + first, g.size)
            even, odd = inverse_lift(joined(v_ref, at, wide), joined(w_ref, at, wide), along)
            spread(v_ref, at, even)
            spread(w_ref, at, odd)

        row_groups(rows, rows, lift_across)
        for k in range(wide // 128):
            cut = slice(first, first + rows)
            both = permuted(jnp.concatenate([v_ref[k, cut], w_ref[k, cut]], 1), matrix)
            if level:
                r_ref[0:rows, 256 * k : 256 * k + 256] = both
            elif k == 0:
                out_ref[:, :128] = both[:, 128:]
            elif k == 8:
                out_ref[:, COLS - 128 :] = both[:, :128]
            else:
                out_ref[:, 256 * k - 128 : 256 * k + 128] = both


def swaps(axis, offset):
    count = lax.axis_size(axis)
    pairs = []
    for i in range(offset, count - 1, 2):
        pairs += [(i, i + 1), (i + 1, i)]
    return pairs


def exchange(for_even, for_odd, axis):
    even = lax.ppermute(for_even, axis, swaps(axis, 0))
    odd = lax.ppermute(for_odd, axis, swaps(axis, 1))
    return odd, even


def f32(*shape):
    return jax.ShapeDtypeStruct(shape, jnp.float32)


def scratch(*shape):
    return pltpu.VMEM(shape, jnp.float32)


def call(kernel, outs, scratches, *args, scalars=0, space=pltpu.VMEM, cost=None):
    vmem = pl.BlockSpec(memory_space=pltpu.VMEM)
    smem = pl.BlockSpec(memory_space=pltpu.SMEM)
    return pl.pallas_call(
        kernel,
        out_shape=outs,
        in_specs=[smem] * scalars + [pl.BlockSpec(memory_space=space)] * (len(args) - scalars),
        out_specs=jax.tree.map(lambda _: vmem, outs),
        scratch_shapes=scratches,
        compiler_params=pltpu.CompilerParams(vmem_limit_bytes=16 * 2**20),
        cost_estimate=cost,
    )(*args)


def local(micrograph, thresholds):
    for_even, for_odd = call(
        edges_kernel,
        (f32(ROWS, 128), f32(ROWS, 128)),
        [pltpu.SemaphoreType.DMA((2,))],
        micrograph,
        space=pltpu.HBM,
    )
    odd, even = exchange(for_even, for_odd, "cols")
    inner = call(
        inner_kernel,
        (f32(ROWS, 896), f32(ROWS, 896), f32(ROWS, 256)),
        [],
        micrograph,
        cost=pl.CostEstimate(flops=2 * 10**9, bytes_accessed=4 * 10**6, transcendentals=0),
    )
    block, high = call(columns_kernel, (f32(80, 1152), f32(64, 1152)), [], *inner, odd, even)
    odd, even = exchange(block, block, "rows")
    shapes = [f32(OWN[level] + 8, WIDE[level]) for level in range(LEVELS) for _ in range(3)]
    shapes.append(shapes[-1])
    pack_even, pack_odd, *bands = call(
        forward_kernel,
        (f32(24, 1280), f32(24, 1280), *shapes),
        [
            scratch(9, 192, 128),
            scratch(9, 96, 128),
            scratch(96, 1280),
            scratch(96, 640),
            scratch(96, 640),
        ],
        thresholds,
        block,
        high,
        odd,
        even,
        scalars=1,
    )
    odd, even = exchange(pack_even, pack_odd, "rows")
    return call(
        inverse_kernel,
        f32(ROWS, COLS),
        [scratch(48, 1280), scratch(9, 80, 128), scratch(9, 80, 128), scratch(48, 1280)]
        + [scratch(40, 1152)] * 3
        + [scratch(16, 256)],
        odd,
        even,
        *bands,
    )


def solution(mesh):
    placed = (P("rows", "cols"), P())
    return jax.shard_map(
        local, mesh=mesh, in_specs=placed, out_specs=P("rows", "cols"), check_vma=False
    )
```

```python
import functools

import jax
import jax.numpy as jnp
from jax import lax
from jax.experimental import pallas as pl
from jax.experimental.pallas import tpu as pltpu
from jax.sharding import PartitionSpec as P

LEVELS = 4

step_one = -1.586134342
step_two = -0.05298011854
step_three = 0.8829110762
step_four = 0.4435068522
band_gain = 1.149604398
inv_gain = 1.0 / band_gain

ROWS, COLS = 64, 2048
WIDE = (1152, 640, 384, 256)
EDGE = (64, 32, 16, 8)
TALL = (96, 48, 24, 12)
OWN = (32, 16, 8, 4)


def soften(coeffs, limit):
    return coeffs - jnp.minimum(jnp.maximum(coeffs, -limit), limit)


def patch(shifted, source, axis, index, flag):
    unit = 8 if axis == 0 else 128
    lo = index // unit * unit
    hi = min(lo + unit, shifted.shape[axis])
    cut = functools.partial(lax.slice_in_dim, axis=axis)
    tile = cut(shifted, lo, hi)
    here = (lax.broadcasted_iota(jnp.int32, tile.shape, axis) == index - lo) & flag
    tile = jnp.where(here, cut(source, lo, hi), tile)
    parts = [cut(shifted, 0, lo)] if lo else []
    parts.append(tile)
    if hi < shifted.shape[axis]:
        parts.append(cut(shifted, hi, shifted.shape[axis]))
    return jnp.concatenate(parts, axis) if len(parts) > 1 else tile


def neighbours(axis, first, count, at_start, at_end):
    def before(odd):
        return patch(pltpu.roll(odd, 1, axis), odd, axis, first, at_start)

    def after(even):
        rolled = pltpu.roll(even, even.shape[axis] - 1, axis)
        return patch(rolled, even, axis, first + count - 1, at_end)

    return before, after


def forward_lift(even, odd, near):
    before, after = near
    odd = odd + step_one * (even + after(even))
    even = even + step_two * (before(odd) + odd)
    odd = odd + step_three * (even + after(even))
    even = even + step_four * (before(odd) + odd)
    return even * band_gain, odd * inv_gain


def inverse_lift(low, high, near):
    before, after = near
    even = low * inv_gain
    odd = high * band_gain
    even = even - step_four * (before(odd) + odd)
    odd = odd - step_three * (even + after(even))
    even = even - step_two * (before(odd) + odd)
    odd = odd - step_one * (even + after(even))
    return even, odd


def pairing(transpose):
    a = lax.broadcasted_iota(jnp.int32, (256, 256), 1 if not transpose else 0)
    b = lax.broadcasted_iota(jnp.int32, (256, 256), 0 if not transpose else 1)
    target = jnp.where(a < 128, 2 * a, 2 * a - 255)
    return jnp.where(b == target, 1.0, 0.0).astype(jnp.bfloat16)


def permuted(x, matrix):
    rows = x.shape[0]
    high = x.astype(jnp.bfloat16)
    rest = x - high.astype(jnp.float32)
    middle = rest.astype(jnp.bfloat16)
    last = (rest - middle.astype(jnp.float32)).astype(jnp.bfloat16)
    out = jnp.dot(
        jnp.concatenate([high, middle, last], 0), matrix, preferred_element_type=jnp.float32
    )
    return (out[:rows] + out[rows : 2 * rows]) + out[2 * rows :]


def tiles(width, body):
    def step(t, carry):
        body(t, pl.ds(pl.multiple_of(t * 128, 128), 128))
        return carry

    lax.fori_loop(0, width // 128, step, 0)


def row_groups(rows, size, body):
    def step(t, carry):
        body(pl.ds(pl.multiple_of(t * size, 8), size))
        return carry

    if size == rows:
        body(pl.ds(0, rows))
    else:
        lax.fori_loop(0, rows // size, step, 0)


def joined(ref, rows, width):
    return jnp.concatenate([ref[k, rows] for k in range(width // 128)], 1)


def spread(ref, rows, value):
    for k in range(value.shape[1] // 128):
        ref[k, rows] = value[:, 128 * k : 128 * k + 128]


def ends(axis):
    position = lax.axis_index(axis)
    return position % 2 == 0, position == 0, position == lax.axis_size(axis) - 1


def edges_kernel(x_ref, for_even, for_odd, sems):
    is_even = ends("cols")[0]
    right = jnp.where(is_even, COLS - 128, 0)
    copies = []
    for k, (at, out) in enumerate(((right, for_even), (COLS - 128 - right, for_odd))):
        lanes = pl.ds(pl.multiple_of(at, 128), 128)
        copies.append(pltpu.make_async_copy(x_ref.at[:, lanes], out, sems.at[k]))
        copies[-1].start()
    for copy in copies:
        copy.wait()


def inner_kernel(t_ref, x_ref, e_ref, o_ref, edge_ref, limit_ref):
    for level in range(LEVELS):
        for kind in range(3):
            limit_ref[3 * level + kind : 3 * level + kind + 1, :] = jnp.full((1, 128), t_ref[level, kind])
    matrix = pairing(False)
    for k in range(7):
        both = permuted(x_ref[:, 256 * k + 128 : 256 * k + 384], matrix)
        e_ref[:, 128 * k : 128 * k + 128] = both[:, :128]
        o_ref[:, 128 * k : 128 * k + 128] = both[:, 128:]
    edge_ref[:, :128] = x_ref[:, :128]
    edge_ref[:, 128:] = x_ref[:, COLS - 128 :]


def columns_kernel(
    e_ref, o_ref, edge_ref, odd_ref, even_ref, for_even, for_odd, low_ref, high_ref, low_low_ref, low_high_ref
):
    is_even, at_start, at_end = ends("cols")
    matrix = pairing(False)
    left = jnp.where(is_even, odd_ref[...], even_ref[...])
    right = jnp.where(is_even, even_ref[...], odd_ref[...])
    first = permuted(jnp.concatenate([left, edge_ref[:, :128]], 1), matrix)
    last = permuted(jnp.concatenate([edge_ref[:, 128:], right], 1), matrix)
    near = neighbours(1, EDGE[0], 1024, at_start, at_end)
    low, high = forward_lift(
        jnp.concatenate([first[:, :128], e_ref[...], last[:, :128]], 1),
        jnp.concatenate([first[:, 128:], o_ref[...], last[:, 128:]], 1),
        near,
    )
    spread(low_ref, slice(None), low)
    spread(high_ref, slice(None), high)
    wide = WIDE[1]
    low = jnp.concatenate([low, jnp.zeros((ROWS, 2 * wide - WIDE[0]), jnp.float32)], 1)
    both = [permuted(low[:, 256 * k : 256 * k + 256], matrix) for k in range(wide // 128)]
    low, high = forward_lift(
        jnp.concatenate([x[:, :128] for x in both], 1),
        jnp.concatenate([x[:, 128:] for x in both], 1),
        neighbours(1, EDGE[1], 512, at_start, at_end),
    )
    spread(low_low_ref, slice(None), low)
    spread(low_high_ref, slice(None), high)
    below = ends("rows")[0].astype(jnp.int32)
    for pack, last in ((for_even, below), (for_odd, 1 - below)):
        for t in range(wide // 128):
            pack[t, 0:60] = low_low_ref[t, pl.ds(4 * last, 60)]
            pack[t, 60:72] = low_high_ref[t, pl.ds(52 * last, 12)]
        for j in range(18):
            source = low_ref if j < 9 else high_ref
            t, row = edge_place(j)
            pack[t, row : row + 4] = source[j % 9, pl.ds(60 * last, 4)]


def edge_place(j):
    return j // 4, 72 + 4 * (j % 4)


def forward_kernel(
    limit_ref, own_low, own_high, own_low_low, own_low_high, odd_ref, even_ref, pack_even, pack_odd, *rest
):
    outs, (l_ref, h_ref, ll_ref, lh_ref, b_ref, e_ref, o_ref) = rest[:13], rest[13:]
    is_even, at_start, at_end = ends("rows")
    _, left_end, right_end = ends("cols")
    matrix = pairing(False)

    def above(t, rows):
        return jnp.where(is_even, odd_ref[t, rows], even_ref[t, rows])

    def under(t, rows):
        return jnp.where(is_even, even_ref[t, rows], odd_ref[t, rows])

    for t in range(WIDE[1] // 128):
        ll_ref[t, 4:64] = above(t, slice(0, 60))
        ll_ref[t, 64:128] = own_low_low[t]
        ll_ref[t, 128:188] = under(t, slice(0, 60))
        lh_ref[t, 4:16] = above(t, slice(60, 72))
        lh_ref[t, 16:80] = own_low_high[t]
        lh_ref[t, 80:92] = under(t, slice(60, 72))
    for j in range(18):
        target, own = (l_ref, own_low) if j < 9 else (h_ref, own_high)
        t, row = edge_place(j)
        target[j % 9, 12:16] = above(t, slice(row, row + 4))
        target[j % 9, 16:80] = own[j % 9]
        target[j % 9, 80:84] = under(t, slice(row, row + 4))

    def share(level, kind, s, coeffs):
        own = OWN[level]
        outs[3 * level + kind][4 : 4 + own, s] = coeffs
        edge = 2 if level == 0 else 4
        first, last = coeffs[:edge], coeffs[own - edge :]
        at = 2 * kind if level == 0 else 8 + 4 * kind
        lanes = s
        shift = (0, 0, 640, 1024)[level]
        if shift:
            lanes = pl.ds(pl.multiple_of(s.start + shift, 128), 128)
        pack_even[at : at + edge, lanes] = jnp.where(is_even, last, first)
        pack_odd[at : at + edge, lanes] = jnp.where(is_even, first, last)

    def lifted(ref, t, tall, begin, own):
        near = neighbours(0, begin, own, at_start, at_end)
        return forward_lift(ref[t, pl.ds(0, tall, stride=2)], ref[t, pl.ds(1, tall, stride=2)], near)

    def lift_low(t, s, level, tall, begin):
        own = OWN[level]
        low, high = lifted(l_ref, t, tall, begin, own)
        share(level, 1, s, soften(high[begin : begin + own], limit_ref[3 * level + 1 : 3 * level + 2, :]))
        if level == LEVELS - 1:
            share(level, 3, s, low[begin : begin + own])
        elif level:
            b_ref[0:tall, s] = low

    def lift_high(t, s, level, tall, begin):
        own = OWN[level]
        low, high = lifted(h_ref, t, tall, begin, own)
        share(level, 0, s, soften(low[begin : begin + own], limit_ref[3 * level + 0 : 3 * level + 1, :]))
        share(level, 2, s, soften(high[begin : begin + own], limit_ref[3 * level + 2 : 3 * level + 3, :]))

    def lift_both(level, low_tall, low_begin, high_tall, high_begin):
        tiles(WIDE[level], lambda t, s: lift_low(t, s, level, low_tall, low_begin))
        tiles(WIDE[level], lambda t, s: lift_high(t, s, level, high_tall, high_begin))

    lift_both(0, 48, 8, 48, 8)

    def lift_next(t, s):
        l_ref[t] = lifted(ll_ref, t, 96, 32, 32)[0]
        h_ref[t, 0:48] = lifted(lh_ref, t, 48, 8, 32)[0]

    tiles(WIDE[1], lift_next)
    lift_both(1, 48, 16, 24, 4)
    for level in (2, 3):
        tall, begin = TALL[level], OWN[level]
        rows = max(2 * tall, 32)
        if 2 * tall < rows:
            b_ref[2 * tall : rows, : WIDE[level - 1]] = jnp.zeros(
                (rows - 2 * tall, WIDE[level - 1]), jnp.float32
            )
        wide = WIDE[level]
        b_ref[0:rows, WIDE[level - 1] : 2 * wide] = jnp.zeros(
            (rows, 2 * wide - WIDE[level - 1]), jnp.float32
        )
        for k in range(wide // 128):
            both = permuted(b_ref[0:rows, 256 * k : 256 * k + 256], matrix)
            e_ref[0:rows, 128 * k : 128 * k + 128] = both[:, :128]
            o_ref[0:rows, 128 * k : 128 * k + 128] = both[:, 128:]
        along = neighbours(1, EDGE[level], 1024 >> level, left_end, right_end)
        low, high = forward_lift(e_ref[0:rows, :wide], o_ref[0:rows, :wide], along)
        spread(l_ref, slice(0, rows), low)
        spread(h_ref, slice(0, rows), high)
        lift_both(level, rows // 2, begin, rows // 2, begin)


def inverse_kernel(odd_ref, even_ref, *rest):
    ins, out_ref, (p_ref, v_ref, w_ref, r_ref), kept = rest[:13], rest[13], rest[14:18], rest[18:]
    is_even, at_start, at_end = ends("rows")
    _, left_end, right_end = ends("cols")
    matrix = pairing(True)

    def choose(t, s):
        up = jnp.where(is_even, odd_ref[:, s], even_ref[:, s])
        down = jnp.where(is_even, even_ref[:, s], odd_ref[:, s])
        p_ref[0:24, s] = up
        p_ref[24:48, s] = down

    tiles(1280, choose)
    for level in range(LEVELS - 1, -1, -1):
        own = OWN[level]
        long = max(own + 8, 16)
        near = neighbours(0, 4, own, at_start, at_end)
        shift = (0, 0, 640, 1024)[level]
        edge = 2 if level == 0 else 4

        def halo(kind, s, level=level, own=own, edge=edge, shift=shift):
            source, target = ins[3 * level + kind], kept[kind]
            at = 2 * kind if level == 0 else 8 + 4 * kind
            lanes = s
            if shift:
                lanes = pl.ds(pl.multiple_of(s.start + shift, 128), 128)
            target[0 : own + 8, s] = source[0 : own + 8, s]
            target[4 - edge : 4, s] = p_ref[at : at + edge, lanes]
            target[4 + own : 4 + own + edge, s] = p_ref[24 + at : 24 + at + edge, lanes]

        def lift_down(t, s, level=level, long=long, near=near, halo=halo):
            for kind in range(4 if level == LEVELS - 1 else 3):
                halo(kind, s)
            low = kept[3][0:long, s] if level == LEVELS - 1 else r_ref[4 : 4 + long, s]
            even, odd = inverse_lift(low, kept[1][0:long, s], near)
            v_ref[t, pl.ds(0, long, stride=2)] = even
            v_ref[t, pl.ds(1, long, stride=2)] = odd
            even, odd = inverse_lift(kept[0][0:long, s], kept[2][0:long, s], near)
            w_ref[t, pl.ds(0, long, stride=2)] = even
            w_ref[t, pl.ds(1, long, stride=2)] = odd

        wide = WIDE[level]
        tiles(wide, lift_down)
        along = neighbours(1, EDGE[level], 1024 >> level, left_end, right_end)
        first, rows = (8, 64) if level == 0 else (0, 2 * long)

        def lift_across(g, wide=wide, along=along, first=first):
            at = pl.ds(g.start + first, g.size)
            even, odd = inverse_lift(joined(v_ref, at, wide), joined(w_ref, at, wide), along)
            spread(v_ref, at, even)
            spread(w_ref, at, odd)

        row_groups(rows, rows, lift_across)
        for k in range(wide // 128):
            cut = slice(first, first + rows)
            both = permuted(jnp.concatenate([v_ref[k, cut], w_ref[k, cut]], 1), matrix)
            if level:
                r_ref[0:rows, 256 * k : 256 * k + 256] = both
            elif k == 0:
                out_ref[:, :128] = both[:, 128:]
            elif k == 8:
                out_ref[:, COLS - 128 :] = both[:, :128]
            else:
                out_ref[:, 256 * k - 128 : 256 * k + 128] = both


def swaps(axis, offset):
    count = lax.axis_size(axis)
    pairs = []
    for i in range(offset, count - 1, 2):
        pairs += [(i, i + 1), (i + 1, i)]
    return pairs


def exchange(for_even, for_odd, axis):
    even = lax.ppermute(for_even, axis, swaps(axis, 0))
    odd = lax.ppermute(for_odd, axis, swaps(axis, 1))
    return odd, even


def f32(*shape):
    return jax.ShapeDtypeStruct(shape, jnp.float32)


def scratch(*shape):
    return pltpu.VMEM(shape, jnp.float32)


def call(kernel, outs, scratches, *args, scalars=0, space=pltpu.VMEM, cost=None):
    vmem = pl.BlockSpec(memory_space=pltpu.VMEM)
    smem = pl.BlockSpec(memory_space=pltpu.SMEM)
    return pl.pallas_call(
        kernel,
        out_shape=outs,
        in_specs=[smem] * scalars + [pl.BlockSpec(memory_space=space)] * (len(args) - scalars),
        out_specs=jax.tree.map(lambda _: vmem, outs),
        scratch_shapes=scratches,
        compiler_params=pltpu.CompilerParams(vmem_limit_bytes=16 * 2**20),
        cost_estimate=cost,
    )(*args)


def local(micrograph, thresholds):
    for_even, for_odd = call(
        edges_kernel,
        (f32(ROWS, 128), f32(ROWS, 128)),
        [pltpu.SemaphoreType.DMA((2,))],
        micrograph,
        space=pltpu.HBM,
    )
    odd, even = exchange(for_even, for_odd, "cols")
    *inner, limits = call(
        inner_kernel,
        (f32(ROWS, 896), f32(ROWS, 896), f32(ROWS, 256), f32(16, 128)),
        [],
        thresholds,
        micrograph,
        scalars=1,
        cost=pl.CostEstimate(flops=2 * 10**9, bytes_accessed=4 * 10**6, transcendentals=0),
    )
    for_even, for_odd, *own = call(
        columns_kernel,
        (f32(5, 88, 128), f32(5, 88, 128))
        + (f32(9, ROWS, 128), f32(9, ROWS, 128), f32(5, ROWS, 128), f32(5, ROWS, 128)),
        [],
        *inner,
        odd,
        even,
    )
    odd, even = exchange(for_even, for_odd, "rows")
    shapes = [f32(OWN[level] + 8, WIDE[level]) for level in range(LEVELS) for _ in range(3)]
    shapes.append(shapes[-1])
    pack_even, pack_odd, *bands = call(
        forward_kernel,
        (f32(24, 1280), f32(24, 1280), *shapes),
        [
            scratch(9, 96, 128),
            scratch(9, 96, 128),
            scratch(5, 192, 128),
            scratch(5, 96, 128),
            scratch(48, 768),
            scratch(48, 384),
            scratch(48, 384),
        ],
        limits,
        *own,
        odd,
        even,
    )
    odd, even = exchange(pack_even, pack_odd, "rows")
    return call(
        inverse_kernel,
        f32(ROWS, COLS),
        [scratch(48, 1280), scratch(9, 80, 128), scratch(9, 80, 128), scratch(48, 1280)]
        + [scratch(40, 1152)] * 3
        + [scratch(16, 256)],
        odd,
        even,
        *bands,
    )


def solution(mesh):
    placed = (P("rows", "cols"), P())
    return jax.shard_map(
        local, mesh=mesh, in_specs=placed, out_specs=P("rows", "cols"), check_vma=False
    )
```

```python
import functools

import jax
import jax.numpy as jnp
from jax import lax
from jax.experimental import pallas as pl
from jax.experimental.pallas import tpu as pltpu
from jax.sharding import PartitionSpec as P

LEVELS = 4

step_one = -1.586134342
step_two = -0.05298011854
step_three = 0.8829110762
step_four = 0.4435068522
band_gain = 1.149604398
inv_gain = 1.0 / band_gain

ROWS, COLS = 64, 2048
WIDE = (1152, 640, 384, 256)
EDGE = (64, 32, 16, 8)
OWN = (32, 16, 8, 4)


STEPS_FROM = 1152
GROUP = 64
MATRIX_FROM = 640


def combined(*terms):
    total = {}
    for factor, taps, moved in terms:
        for (sequence, offset), tap in taps.items():
            key = (sequence, offset + moved)
            total[key] = total.get(key, 0.0) + factor * tap
    return total


def lifted_taps(inverse):
    even, odd = {("even", 0): 1.0}, {("odd", 0): 1.0}
    if inverse:
        even, odd = combined((1.0 / band_gain, even, 0)), combined((band_gain, odd, 0))
        for to_even, to_odd in ((step_four, step_three), (step_two, step_one)):
            even = combined((1.0, even, 0), (-to_even, odd, 0), (-to_even, odd, -1))
            odd = combined((1.0, odd, 0), (-to_odd, even, 0), (-to_odd, even, 1))
        return even, odd
    for to_odd, to_even in ((step_one, step_two), (step_three, step_four)):
        odd = combined((1.0, odd, 0), (to_odd, even, 0), (to_odd, even, 1))
        even = combined((1.0, even, 0), (to_even, odd, 0), (to_even, odd, -1))
    return combined((band_gain, even, 0)), combined((1.0 / band_gain, odd, 0))


def lift_lanes(even, odd, first, count, at_start, at_end, inverse=False):
    rows, width = even.shape
    if width >= STEPS_FROM:
        near = neighbours(1, first, count, at_start, at_end)
        lift = inverse_lift if inverse else forward_lift
        groups = [slice(k, min(k + GROUP, rows)) for k in range(0, rows, GROUP)]
        parts = [lift(even[g], odd[g], near) for g in groups]
        return [jnp.concatenate(x, 0) if len(x) > 1 else x[0] for x in zip(*parts)]
    last = first + count - 1
    e, o = {0: even}, {0: odd}
    for x in (e, o):
        width = x[0].shape[1]
        for offset in (-2, -1, 1, 2):
            x[offset] = pltpu.roll(x[0], -offset % width, 1)
    fixed = lambda x, source, lane, flag: patch(x, source, 1, lane, flag)
    ends_of = {
        ("even", -1): [(e[1], first, at_start)],
        ("even", -2): [(e[2], first, at_start), (e[0], first + 1, at_start)],
        ("even", 1): [(e[0], last, at_end)],
        ("even", 2): [(e[-1], last, at_end), (e[1], last - 1, at_end)],
        ("odd", -1): [(o[0], first, at_start)],
        ("odd", -2): [(o[1], first, at_start), (o[-1], first + 1, at_start)],
        ("odd", 1): [(o[-1], last, at_end)],
        ("odd", 2): [(o[-2], last, at_end), (o[0], last - 1, at_end)],
    }
    shifted = {("even", 0): even, ("odd", 0): odd}
    for (sequence, offset), patches in ends_of.items():
        x = (e if sequence == "even" else o)[offset]
        for patch_of in patches:
            x = fixed(x, *patch_of)
        shifted[sequence, offset] = x
    out = []
    for taps in lifted_taps(inverse):
        by_tap = {}
        for key, tap in sorted(taps.items()):
            by_tap.setdefault(round(tap, 9), []).append((tap, shifted[key]))
        total = None
        for group in by_tap.values():
            term = sum((x for _, x in group[1:]), group[0][1]) * group[0][0]
            total = term if total is None else total + term
        out.append(total)
    return out


def soften(coeffs, limit):
    return coeffs - jnp.minimum(jnp.maximum(coeffs, -limit), limit)


def patch(shifted, source, axis, index, flag):
    unit = 8 if axis == 0 else 128
    lo = index // unit * unit
    hi = min(lo + unit, shifted.shape[axis])
    cut = functools.partial(lax.slice_in_dim, axis=axis)
    tile = cut(shifted, lo, hi)
    here = (lax.broadcasted_iota(jnp.int32, tile.shape, axis) == index - lo) & flag
    tile = jnp.where(here, cut(source, lo, hi), tile)
    parts = [cut(shifted, 0, lo)] if lo else []
    parts.append(tile)
    if hi < shifted.shape[axis]:
        parts.append(cut(shifted, hi, shifted.shape[axis]))
    return jnp.concatenate(parts, axis) if len(parts) > 1 else tile


def neighbours(axis, first, count, at_start, at_end):
    def before(odd):
        return patch(pltpu.roll(odd, 1, axis), odd, axis, first, at_start)

    def after(even):
        rolled = pltpu.roll(even, even.shape[axis] - 1, axis)
        return patch(rolled, even, axis, first + count - 1, at_end)

    return before, after


def forward_lift(even, odd, near):
    before, after = near
    odd = odd + step_one * (even + after(even))
    even = even + step_two * (before(odd) + odd)
    odd = odd + step_three * (even + after(even))
    even = even + step_four * (before(odd) + odd)
    return even * band_gain, odd * inv_gain


def inverse_lift(low, high, near):
    before, after = near
    even = low * inv_gain
    odd = high * band_gain
    even = even - step_four * (before(odd) + odd)
    odd = odd - step_three * (even + after(even))
    even = even - step_two * (before(odd) + odd)
    odd = odd - step_one * (even + after(even))
    return even, odd


def pairing(transpose):
    a = lax.broadcasted_iota(jnp.int32, (256, 256), 1 if not transpose else 0)
    b = lax.broadcasted_iota(jnp.int32, (256, 256), 0 if not transpose else 1)
    target = jnp.where(a < 128, 2 * a, 2 * a - 255)
    return jnp.where(b == target, 1.0, 0.0).astype(jnp.bfloat16)


def permuted(x, matrix):
    rows = x.shape[0]
    high = x.astype(jnp.bfloat16)
    rest = x - high.astype(jnp.float32)
    middle = rest.astype(jnp.bfloat16)
    last = (rest - middle.astype(jnp.float32)).astype(jnp.bfloat16)
    out = jnp.dot(
        jnp.concatenate([high, middle, last], 0), matrix, preferred_element_type=jnp.float32
    )
    return (out[:rows] + out[rows : 2 * rows]) + out[2 * rows :]


def picked(x, index):
    return jnp.take_along_axis(x, index, axis=1, mode="promise_in_bounds")


def split_pairs(x):
    if x.shape[1] < 2 * MATRIX_FROM:
        return split_by_picks(x)
    matrix = pairing(False)
    both = [permuted(x[:, k : k + 256], matrix) for k in range(0, x.shape[1], 256)]
    return jnp.concatenate([y[:, :128] for y in both], 1), jnp.concatenate([y[:, 128:] for y in both], 1)


def merge_pairs(even, odd):
    if even.shape[1] < MATRIX_FROM:
        return merge_by_picks(even, odd)
    matrix = pairing(True)
    return jnp.concatenate(
        [
            permuted(jnp.concatenate([even[:, k : k + 128], odd[:, k : k + 128]], 1), matrix)
            for k in range(0, even.shape[1], 128)
        ],
        1,
    )


def split_by_picks(x):
    rows = x.shape[0]
    lane = lax.broadcasted_iota(jnp.int32, (rows, 128), 1)
    lower = lane < 64
    near = jnp.where(lower, 2 * lane, 2 * lane - 127)
    far = jnp.where(lower, 2 * lane + 1, 2 * lane - 128)
    evens, odds = [], []
    for k in range(0, x.shape[1], 256):
        first, second = picked(x[:, k : k + 128], near), picked(x[:, k + 128 : k + 256], far)
        evens.append(jnp.where(lower, first, second))
        odds.append(pltpu.roll(jnp.where(lower, second, first), 64, 1))
    return jnp.concatenate(evens, 1), jnp.concatenate(odds, 1)


def merge_by_picks(even, odd):
    rows = even.shape[0]
    lane = lax.broadcasted_iota(jnp.int32, (rows, 128), 1)
    lower = lane < 64
    is_odd = lane % 2 == 1
    half = lane // 2
    near = jnp.where(is_odd, half + 64, half)
    far = jnp.where(is_odd, half, half + 64)
    out = []
    for k in range(0, even.shape[1], 128):
        e, o = even[:, k : k + 128], pltpu.roll(odd[:, k : k + 128], 64, 1)
        out += [picked(jnp.where(lower, e, o), near), picked(jnp.where(lower, o, e), far)]
    return jnp.concatenate(out, 1)


def tiles(width, body):
    def step(t, carry):
        body(t, pl.ds(pl.multiple_of(t * 128, 128), 128))
        return carry

    if width > 640:
        lax.fori_loop(0, width // 128, step, 0)
    else:
        for t in range(width // 128):
            body(t, slice(128 * t, 128 * t + 128))


def joined(ref, rows, width):
    return jnp.concatenate([ref[k, rows] for k in range(width // 128)], 1)


def spread(ref, rows, value):
    for k in range(value.shape[1] // 128):
        ref[k, rows] = value[:, 128 * k : 128 * k + 128]


def ends(axis):
    position = lax.axis_index(axis)
    return position % 2 == 0, position == 0, position == lax.axis_size(axis) - 1


def edges_kernel(x_ref, for_even, for_odd, sems):
    is_even = ends("cols")[0]
    right = jnp.where(is_even, COLS - 128, 0)
    copies = []
    for k, (at, out) in enumerate(((right, for_even), (COLS - 128 - right, for_odd))):
        lanes = pl.ds(pl.multiple_of(at, 128), 128)
        copies.append(pltpu.make_async_copy(x_ref.at[:, lanes], out, sems.at[k]))
        copies[-1].start()
    for copy in copies:
        copy.wait()


def inner_kernel(t_ref, x_ref, e_ref, o_ref, edge_ref, limit_ref):
    for level in range(LEVELS):
        for kind in range(3):
            limit_ref[3 * level + kind : 3 * level + kind + 1, :] = jnp.full((1, 128), t_ref[level, kind])
    e_ref[...], o_ref[...] = split_pairs(x_ref[:, 128 : COLS - 128])
    edge_ref[:, :128] = x_ref[:, :128]
    edge_ref[:, 128:] = x_ref[:, COLS - 128 :]


def columns_kernel(
    e_ref, o_ref, edge_ref, odd_ref, even_ref, for_even, for_odd, low_ref, high_ref, low_low_ref, low_high_ref
):
    is_even, at_start, at_end = ends("cols")
    left = jnp.where(is_even, odd_ref[...], even_ref[...])
    right = jnp.where(is_even, even_ref[...], odd_ref[...])
    first = split_pairs(jnp.concatenate([left, edge_ref[:, :128]], 1))
    last = split_pairs(jnp.concatenate([edge_ref[:, 128:], right], 1))
    low, high = lift_lanes(
        jnp.concatenate([first[0], e_ref[...], last[0]], 1),
        jnp.concatenate([first[1], o_ref[...], last[1]], 1),
        EDGE[0],
        1024,
        at_start,
        at_end,
    )
    spread(low_ref, slice(None), low)
    spread(high_ref, slice(None), high)
    wide = WIDE[1]
    low = jnp.concatenate([low, jnp.zeros((ROWS, 2 * wide - WIDE[0]), jnp.float32)], 1)
    low, high = lift_lanes(*split_pairs(low), EDGE[1], 512, at_start, at_end)
    spread(low_low_ref, slice(None), low)
    spread(low_high_ref, slice(None), high)
    below = ends("rows")[0].astype(jnp.int32)
    for pack, last in ((for_even, below), (for_odd, 1 - below)):
        for t in range(wide // 128):
            pack[t, 0:60] = low_low_ref[t, pl.ds(4 * last, 60)]
            pack[t, 60:72] = low_high_ref[t, pl.ds(52 * last, 12)]
        for j in range(18):
            source = low_ref if j < 9 else high_ref
            t, row = edge_place(j)
            pack[t, row : row + 8] = source[j % 9, pl.ds(56 * last, 8)]


def edge_place(j):
    return j // 4, 72 + 8 * (j % 4)


def edge_at(level, kind, t):
    return 4 * (2 * kind + t) if level == 3 else 32 + 4 * (5 * (kind // 2) + t)


def sides(odd_ref, even_ref):
    is_even = ends("rows")[0]

    def above(*at):
        return jnp.where(is_even, odd_ref[at], even_ref[at])

    def under(*at):
        return jnp.where(is_even, even_ref[at], odd_ref[at])

    return above, under


def lifted(ref, t, tall, begin, own):
    _, at_start, at_end = ends("rows")
    near = neighbours(0, begin, own, at_start, at_end)
    return forward_lift(ref[t, pl.ds(0, tall, stride=2)], ref[t, pl.ds(1, tall, stride=2)], near)


def forward_kernel(limit_ref, own_low, own_high, odd_ref, even_ref, for_even, for_odd, *rest):
    outs, (l_ref, h_ref, ll_ref, lh_ref, b_ref) = rest[:10], rest[10:]
    is_even = ends("rows")[0]
    _, left_end, right_end = ends("cols")
    above, under = sides(odd_ref, even_ref)
    for t in range(WIDE[1] // 128):
        ll_ref[t, 4:64] = above(t, slice(0, 60))
        ll_ref[t, 64:128] = own_low[t]
        ll_ref[t, 128:188] = under(t, slice(0, 60))
        lh_ref[t, 4:16] = above(t, slice(60, 72))
        lh_ref[t, 16:80] = own_high[t]
        lh_ref[t, 80:92] = under(t, slice(60, 72))
        l_ref[t] = lifted(ll_ref, t, 96, 32, 32)[0]
        h_ref[t, 0:48] = lifted(lh_ref, t, 48, 8, 32)[0]

    def limited(coeffs, level, kind):
        if kind == 3:
            return coeffs
        at = 3 * level + kind
        return soften(coeffs, limit_ref[at : at + 1, :])

    def keep(level, kind, t, s, coeffs, begin):
        own = OWN[level]
        coeffs = limited(coeffs[begin - 4 : begin + own + 4], level, kind)
        outs[3 * (level - 1) + kind][:, s] = coeffs
        if level == 3 or (level == 1 and kind != 1):
            first, last = coeffs[4:8], coeffs[own : own + 4]
            at = edge_at(level, kind, t)
            for_even[at : at + 4, :] = jnp.where(is_even, last, first)
            for_odd[at : at + 4, :] = jnp.where(is_even, first, last)

    for level in (1, 2, 3):
        own = OWN[level]
        if level == 1:
            sizes = ((48, 16), (24, 4))
        else:
            rows = (48, 32)[level - 2]
            sizes = ((rows // 2, own),) * 2
            known, wide = WIDE[level - 1], WIDE[level]
            if level == 3:
                b_ref[24:32, :known] = jnp.zeros((8, known), jnp.float32)
            b_ref[0:rows, known : 2 * wide] = jnp.zeros((rows, 2 * wide - known), jnp.float32)
            halves = split_pairs(b_ref[0:rows, : 2 * wide])
            low, high = lift_lanes(*halves, EDGE[level], 1024 >> level, left_end, right_end)
            spread(l_ref, slice(0, rows), low)
            spread(h_ref, slice(0, rows), high)
        for t in range(WIDE[level] // 128):
            s = slice(128 * t, 128 * t + 128)
            low, high = lifted(l_ref, t, *sizes[0], own)
            keep(level, 1, t, s, high, sizes[0][1])
            if level == 3:
                keep(level, 3, t, s, low, sizes[0][1])
            else:
                b_ref[0 : sizes[0][0], s] = low
            low, high = lifted(h_ref, t, *sizes[1], own)
            keep(level, 0, t, s, low, sizes[1][1])
            keep(level, 2, t, s, high, sizes[1][1])


def detail_kernel(limit_ref, own_low, own_high, odd_ref, even_ref, hl_ref, lh_ref, hh_ref, x_ref):
    above, under = sides(odd_ref, even_ref)
    for j in range(18):
        own = own_low if j < 9 else own_high
        t, row = edge_place(j)
        x_ref[j, 0:8] = above(t, slice(row, row + 8))
        x_ref[j, 8:72] = own[j % 9]
        x_ref[j, 72:80] = under(t, slice(row, row + 8))

    def lift(t, s):
        high = lifted(x_ref, t, 40, 4, 32)[1]
        lh_ref[:, s] = soften(high, limit_ref[1:2, :])
        low, high = lifted(x_ref, t + 9, 40, 4, 32)
        hl_ref[:, s] = soften(low, limit_ref[0:1, :])
        hh_ref[:, s] = soften(high, limit_ref[2:3, :])

    tiles(WIDE[0], lift)


def inverse_kernel(odd_ref, even_ref, *rest):
    ins, out_ref, (v_ref, w_ref, r_ref), kept = rest[:13], rest[13], rest[14:17], rest[17:]
    _, at_start, at_end = ends("rows")
    _, left_end, right_end = ends("cols")
    above, under = sides(odd_ref, even_ref)
    for level in range(LEVELS - 1, -1, -1):
        own = OWN[level]
        long = max(own + 8, 16)
        near = neighbours(0, 4, own, at_start, at_end)

        def whole(kind, t, s, level=level, own=own, long=long):
            source = ins[3 * level + kind]
            if level == 2 or level == 0 or (level == 1 and kind == 1):
                return source[0:long, s]
            target, at = kept[kind], slice(edge_at(level, kind, t), edge_at(level, kind, t) + 4)
            target[0 : own + 8, s] = source[:, s]
            target[0:4, s] = above(at)
            target[4 + own : 8 + own, s] = under(at)
            return target[0:long, s]

        def lift_down(t, s, level=level, long=long, near=near, whole=whole):
            low = whole(3, t, s) if level == LEVELS - 1 else r_ref[4 : 4 + long, s]
            even, odd = inverse_lift(low, whole(1, t, s), near)
            v_ref[t, pl.ds(0, long, stride=2)] = even
            v_ref[t, pl.ds(1, long, stride=2)] = odd
            even, odd = inverse_lift(whole(0, t, s), whole(2, t, s), near)
            w_ref[t, pl.ds(0, long, stride=2)] = even
            w_ref[t, pl.ds(1, long, stride=2)] = odd

        wide = WIDE[level]
        tiles(wide, lift_down)
        first, rows = (8, 64) if level == 0 else (0, 2 * long)
        cut = slice(first, first + rows)
        even, odd = joined(v_ref, cut, wide), joined(w_ref, cut, wide)
        both = merge_pairs(
            *lift_lanes(even, odd, EDGE[level], 1024 >> level, left_end, right_end, inverse=True)
        )
        if level:
            r_ref[0:rows, : 2 * wide] = both
        else:
            out_ref[...] = both[:, 128 : 128 + COLS]


def swaps(axis, offset):
    count = lax.axis_size(axis)
    pairs = []
    for i in range(offset, count - 1, 2):
        pairs += [(i, i + 1), (i + 1, i)]
    return pairs


def exchange(for_even, for_odd, axis):
    even = lax.ppermute(for_even, axis, swaps(axis, 0))
    odd = lax.ppermute(for_odd, axis, swaps(axis, 1))
    return odd, even


def f32(*shape):
    return jax.ShapeDtypeStruct(shape, jnp.float32)


def scratch(*shape):
    return pltpu.VMEM(shape, jnp.float32)


def call(kernel, outs, scratches, *args, scalars=0, space=pltpu.VMEM, cost=None):
    vmem = pl.BlockSpec(memory_space=pltpu.VMEM)
    smem = pl.BlockSpec(memory_space=pltpu.SMEM)
    return pl.pallas_call(
        kernel,
        out_shape=outs,
        in_specs=[smem] * scalars + [pl.BlockSpec(memory_space=space)] * (len(args) - scalars),
        out_specs=jax.tree.map(lambda _: vmem, outs),
        scratch_shapes=scratches,
        compiler_params=pltpu.CompilerParams(vmem_limit_bytes=16 * 2**20),
        cost_estimate=cost,
    )(*args)


def local(micrograph, thresholds):
    for_even, for_odd = call(
        edges_kernel,
        (f32(ROWS, 128), f32(ROWS, 128)),
        [pltpu.SemaphoreType.DMA((2,))],
        micrograph,
        space=pltpu.HBM,
    )
    odd, even = exchange(for_even, for_odd, "cols")
    *inner, limits = call(
        inner_kernel,
        (f32(ROWS, 896), f32(ROWS, 896), f32(ROWS, 256), f32(16, 128)),
        [],
        thresholds,
        micrograph,
        scalars=1,
        cost=pl.CostEstimate(flops=2 * 10**9, bytes_accessed=4 * 10**6, transcendentals=0),
    )
    for_even, for_odd, *own = call(
        columns_kernel,
        (f32(5, 104, 128), f32(5, 104, 128))
        + (f32(9, ROWS, 128), f32(9, ROWS, 128), f32(5, ROWS, 128), f32(5, ROWS, 128)),
        [],
        *inner,
        odd,
        even,
    )
    own_low, own_high, own_low_low, own_low_high = own
    odd, even = exchange(for_even, for_odd, "rows")
    shapes = [f32(OWN[level] + 8, WIDE[level]) for level in range(LEVELS) for _ in range(3)]
    shapes.append(shapes[-1])
    for_even, for_odd, *bands = call(
        forward_kernel,
        (f32(72, 128), f32(72, 128), *shapes[3:]),
        [
            scratch(5, 96, 128),
            scratch(5, 96, 128),
            scratch(5, 192, 128),
            scratch(5, 96, 128),
            scratch(48, 768),
        ],
        limits,
        own_low_low,
        own_low_high,
        odd,
        even,
    )
    finest = call(
        detail_kernel,
        tuple(shapes[:3]),
        [scratch(18, 80, 128)],
        limits,
        own_low,
        own_high,
        odd,
        even,
        cost=pl.CostEstimate(flops=2 * 10**9, bytes_accessed=4 * 10**6, transcendentals=0),
    )
    odd, even = exchange(for_even, for_odd, "rows")
    return call(
        inverse_kernel,
        f32(ROWS, COLS),
        [scratch(9, 80, 128), scratch(9, 80, 128), scratch(48, 1280)]
        + [scratch(24, 640), scratch(16, 256), scratch(24, 640), scratch(16, 256)],
        odd,
        even,
        *finest,
        *bands,
    )


def solution(mesh):
    placed = (P("rows", "cols"), P())
    return jax.shard_map(
        local, mesh=mesh, in_specs=placed, out_specs=P("rows", "cols"), check_vma=False
    )
```

```python
import functools

import jax
import jax.numpy as jnp
from jax import lax
from jax.experimental import pallas as pl
from jax.experimental.pallas import tpu as pltpu
from jax.sharding import PartitionSpec as P

LEVELS = 4

step_one = -1.586134342
step_two = -0.05298011854
step_three = 0.8829110762
step_four = 0.4435068522
band_gain = 1.149604398
inv_gain = 1.0 / band_gain

ROWS, COLS = 64, 2048
WIDE = (1152, 640, 384, 256)
EDGE = (64, 32, 16, 8)
OWN = (32, 16, 8, 4)


STEPS_FROM = 1152
GROUP = 64
MATRIX_FROM = 640


def combined(*terms):
    total = {}
    for factor, taps, moved in terms:
        for (sequence, offset), tap in taps.items():
            key = (sequence, offset + moved)
            total[key] = total.get(key, 0.0) + factor * tap
    return total


def lifted_taps(inverse):
    even, odd = {("even", 0): 1.0}, {("odd", 0): 1.0}
    if inverse:
        even, odd = combined((1.0 / band_gain, even, 0)), combined((band_gain, odd, 0))
        for to_even, to_odd in ((step_four, step_three), (step_two, step_one)):
            even = combined((1.0, even, 0), (-to_even, odd, 0), (-to_even, odd, -1))
            odd = combined((1.0, odd, 0), (-to_odd, even, 0), (-to_odd, even, 1))
        return even, odd
    for to_odd, to_even in ((step_one, step_two), (step_three, step_four)):
        odd = combined((1.0, odd, 0), (to_odd, even, 0), (to_odd, even, 1))
        even = combined((1.0, even, 0), (to_even, odd, 0), (to_even, odd, -1))
    return combined((band_gain, even, 0)), combined((1.0 / band_gain, odd, 0))


def lift_lanes(even, odd, first, count, at_start, at_end, inverse=False):
    rows, width = even.shape
    if width >= STEPS_FROM:
        near = neighbours(1, first, count, at_start, at_end)
        lift = inverse_lift if inverse else forward_lift
        groups = [slice(k, min(k + GROUP, rows)) for k in range(0, rows, GROUP)]
        parts = [lift(even[g], odd[g], near) for g in groups]
        return [jnp.concatenate(x, 0) if len(x) > 1 else x[0] for x in zip(*parts)]
    last = first + count - 1
    e, o = {0: even}, {0: odd}
    for x in (e, o):
        width = x[0].shape[1]
        for offset in (-2, -1, 1, 2):
            x[offset] = pltpu.roll(x[0], -offset % width, 1)
    fixed = lambda x, source, lane, flag: patch(x, source, 1, lane, flag)
    ends_of = {
        ("even", -1): [(e[1], first, at_start)],
        ("even", -2): [(e[2], first, at_start), (e[0], first + 1, at_start)],
        ("even", 1): [(e[0], last, at_end)],
        ("even", 2): [(e[-1], last, at_end), (e[1], last - 1, at_end)],
        ("odd", -1): [(o[0], first, at_start)],
        ("odd", -2): [(o[1], first, at_start), (o[-1], first + 1, at_start)],
        ("odd", 1): [(o[-1], last, at_end)],
        ("odd", 2): [(o[-2], last, at_end), (o[0], last - 1, at_end)],
    }
    shifted = {("even", 0): even, ("odd", 0): odd}
    for (sequence, offset), patches in ends_of.items():
        x = (e if sequence == "even" else o)[offset]
        for patch_of in patches:
            x = fixed(x, *patch_of)
        shifted[sequence, offset] = x
    out = []
    for taps in lifted_taps(inverse):
        by_tap = {}
        for key, tap in sorted(taps.items()):
            by_tap.setdefault(round(tap, 9), []).append((tap, shifted[key]))
        total = None
        for group in by_tap.values():
            term = sum((x for _, x in group[1:]), group[0][1]) * group[0][0]
            total = term if total is None else total + term
        out.append(total)
    return out


def soften(coeffs, limit):
    return coeffs - jnp.minimum(jnp.maximum(coeffs, -limit), limit)


def patch(shifted, source, axis, index, flag):
    unit = 8 if axis == 0 else 128
    lo = index // unit * unit
    hi = min(lo + unit, shifted.shape[axis])
    cut = functools.partial(lax.slice_in_dim, axis=axis)
    tile = cut(shifted, lo, hi)
    here = (lax.broadcasted_iota(jnp.int32, tile.shape, axis) == index - lo) & flag
    tile = jnp.where(here, cut(source, lo, hi), tile)
    parts = [cut(shifted, 0, lo)] if lo else []
    parts.append(tile)
    if hi < shifted.shape[axis]:
        parts.append(cut(shifted, hi, shifted.shape[axis]))
    return jnp.concatenate(parts, axis) if len(parts) > 1 else tile


def neighbours(axis, first, count, at_start, at_end):
    def before(odd):
        return patch(pltpu.roll(odd, 1, axis), odd, axis, first, at_start)

    def after(even):
        rolled = pltpu.roll(even, even.shape[axis] - 1, axis)
        return patch(rolled, even, axis, first + count - 1, at_end)

    return before, after


def forward_lift(even, odd, near):
    before, after = near
    odd = odd + step_one * (even + after(even))
    even = even + step_two * (before(odd) + odd)
    odd = odd + step_three * (even + after(even))
    even = even + step_four * (before(odd) + odd)
    return even * band_gain, odd * inv_gain


def inverse_lift(low, high, near):
    before, after = near
    even = low * inv_gain
    odd = high * band_gain
    even = even - step_four * (before(odd) + odd)
    odd = odd - step_three * (even + after(even))
    even = even - step_two * (before(odd) + odd)
    odd = odd - step_one * (even + after(even))
    return even, odd


def pairing(transpose):
    a = lax.broadcasted_iota(jnp.int32, (256, 256), 1 if not transpose else 0)
    b = lax.broadcasted_iota(jnp.int32, (256, 256), 0 if not transpose else 1)
    target = jnp.where(a < 128, 2 * a, 2 * a - 255)
    return jnp.where(b == target, 1.0, 0.0).astype(jnp.bfloat16)


def permuted(x, matrix):
    rows = x.shape[0]
    high = x.astype(jnp.bfloat16)
    rest = x - high.astype(jnp.float32)
    middle = rest.astype(jnp.bfloat16)
    last = (rest - middle.astype(jnp.float32)).astype(jnp.bfloat16)
    out = jnp.dot(
        jnp.concatenate([high, middle, last], 0), matrix, preferred_element_type=jnp.float32
    )
    return (out[:rows] + out[rows : 2 * rows]) + out[2 * rows :]


def picked(x, index):
    return jnp.take_along_axis(x, index, axis=1, mode="promise_in_bounds")


def split_pairs(x):
    if x.shape[1] < 2 * MATRIX_FROM:
        return split_by_picks(x)
    matrix = pairing(False)
    both = [permuted(x[:, k : k + 256], matrix) for k in range(0, x.shape[1], 256)]
    return jnp.concatenate([y[:, :128] for y in both], 1), jnp.concatenate([y[:, 128:] for y in both], 1)


def merge_pairs(even, odd):
    if even.shape[1] < MATRIX_FROM:
        return merge_by_picks(even, odd)
    matrix = pairing(True)
    return jnp.concatenate(
        [
            permuted(jnp.concatenate([even[:, k : k + 128], odd[:, k : k + 128]], 1), matrix)
            for k in range(0, even.shape[1], 128)
        ],
        1,
    )


def split_by_picks(x):
    rows = x.shape[0]
    lane = lax.broadcasted_iota(jnp.int32, (rows, 128), 1)
    lower = lane < 64
    near = jnp.where(lower, 2 * lane, 2 * lane - 127)
    far = jnp.where(lower, 2 * lane + 1, 2 * lane - 128)
    evens, odds = [], []
    for k in range(0, x.shape[1], 256):
        first, second = picked(x[:, k : k + 128], near), picked(x[:, k + 128 : k + 256], far)
        evens.append(jnp.where(lower, first, second))
        odds.append(pltpu.roll(jnp.where(lower, second, first), 64, 1))
    return jnp.concatenate(evens, 1), jnp.concatenate(odds, 1)


def merge_by_picks(even, odd):
    rows = even.shape[0]
    lane = lax.broadcasted_iota(jnp.int32, (rows, 128), 1)
    lower = lane < 64
    is_odd = lane % 2 == 1
    half = lane // 2
    near = jnp.where(is_odd, half + 64, half)
    far = jnp.where(is_odd, half, half + 64)
    out = []
    for k in range(0, even.shape[1], 128):
        e, o = even[:, k : k + 128], pltpu.roll(odd[:, k : k + 128], 64, 1)
        out += [picked(jnp.where(lower, e, o), near), picked(jnp.where(lower, o, e), far)]
    return jnp.concatenate(out, 1)


def tiles(width, body):
    def step(t, carry):
        body(t, pl.ds(pl.multiple_of(t * 128, 128), 128))
        return carry

    if width > 640:
        lax.fori_loop(0, width // 128, step, 0)
    else:
        for t in range(width // 128):
            body(t, slice(128 * t, 128 * t + 128))


def joined(ref, rows, width):
    return jnp.concatenate([ref[k, rows] for k in range(width // 128)], 1)


def spread(ref, rows, value):
    for k in range(value.shape[1] // 128):
        ref[k, rows] = value[:, 128 * k : 128 * k + 128]


def ends(axis):
    position = lax.axis_index(axis)
    return position % 2 == 0, position == 0, position == lax.axis_size(axis) - 1


def edges_kernel(x_ref, for_even, for_odd, sems):
    is_even = ends("cols")[0]
    right = jnp.where(is_even, COLS - 128, 0)
    copies = []
    for k, (at, out) in enumerate(((right, for_even), (COLS - 128 - right, for_odd))):
        lanes = pl.ds(pl.multiple_of(at, 128), 128)
        copies.append(pltpu.make_async_copy(x_ref.at[:, lanes], out, sems.at[k]))
        copies[-1].start()
    for copy in copies:
        copy.wait()


def inner_kernel(t_ref, x_ref, e_ref, o_ref, edge_ref, limit_ref):
    for level in range(LEVELS):
        for kind in range(3):
            limit_ref[3 * level + kind : 3 * level + kind + 1, :] = jnp.full((1, 128), t_ref[level, kind])
    e_ref[...], o_ref[...] = split_pairs(x_ref[:, 128 : COLS - 128])
    edge_ref[:, :128] = x_ref[:, :128]
    edge_ref[:, 128:] = x_ref[:, COLS - 128 :]


def columns_kernel(
    e_ref, o_ref, edge_ref, odd_ref, even_ref, for_even, for_odd, low_ref, high_ref, low_low_ref, low_high_ref,
    one_ref, two_ref,
):
    is_even, at_start, at_end = ends("cols")
    left = jnp.where(is_even, odd_ref[...], even_ref[...])
    right = jnp.where(is_even, even_ref[...], odd_ref[...])
    first = split_pairs(jnp.concatenate([left, edge_ref[:, :128]], 1))
    last = split_pairs(jnp.concatenate([edge_ref[:, 128:], right], 1))
    low, high = lift_lanes(
        jnp.concatenate([first[0], e_ref[...], last[0]], 1),
        jnp.concatenate([first[1], o_ref[...], last[1]], 1),
        EDGE[0],
        1024,
        at_start,
        at_end,
    )
    spread(low_ref, slice(None), low)
    spread(high_ref, slice(None), high)
    wide = WIDE[1]
    low = jnp.concatenate([low, jnp.zeros((ROWS, 2 * wide - WIDE[0]), jnp.float32)], 1)
    low, high = lift_lanes(*split_pairs(low), EDGE[1], 512, at_start, at_end)
    spread(low_low_ref, slice(None), low)
    spread(low_high_ref, slice(None), high)
    below = ends("rows")[0].astype(jnp.int32)
    for t in range(wide // 128):
        one_ref[t] = plain_low(low_low_ref, t, 32)
        two_ref[t] = plain_low(one_ref, t, 16)
    for pack, last in ((for_even, below), (for_odd, 1 - below)):
        for t in range(wide // 128):
            pack[PIECE * t : PIECE * t + 8] = low_low_ref[t, pl.ds(56 * last, 8)]
            pack[PIECE * t + 8 : PIECE * t + 16] = one_ref[t, pl.ds(2 + 20 * last, 8)]
            pack[PIECE * t + 16 : PIECE * t + 25] = two_ref[t, pl.ds(3 + last, 9)]
            pack[PIECE * t + 25 : PIECE * t + 37] = low_high_ref[t, pl.ds(52 * last, 12)]
        for j in range(9):
            pack[EDGES + 8 * j : EDGES + 8 * j + 8] = high_ref[j, pl.ds(56 * last, 8)]


PIECE, EDGES, PACK = 37, 192, 264


def plain_low(ref, t, tall):
    near = (lambda x: pltpu.roll(x, 1, 0)), (lambda x: pltpu.roll(x, tall - 1, 0))
    return forward_lift(ref[t, pl.ds(0, tall, stride=2)], ref[t, pl.ds(1, tall, stride=2)], near)[0]


def edge_at(level, kind, t):
    return 4 * (2 * kind + t) if level == 3 else 32 + 4 * (5 * (kind // 2) + t)


def sides(odd_ref, even_ref):
    is_even = ends("rows")[0]

    def above(*at):
        return jnp.where(is_even, odd_ref[at], even_ref[at])

    def under(*at):
        return jnp.where(is_even, even_ref[at], odd_ref[at])

    return above, under


def lifted(ref, t, tall, begin, own):
    _, at_start, at_end = ends("rows")
    near = neighbours(0, begin, own, at_start, at_end)
    return forward_lift(ref[t, pl.ds(0, tall, stride=2)], ref[t, pl.ds(1, tall, stride=2)], near)


def forward_kernel(limit_ref, own_low, own_high, odd_ref, even_ref, for_even, for_odd, *rest):
    outs, (l_ref, h_ref, ll_ref, lh_ref, b_ref) = rest[:10], rest[10:]
    is_even = ends("rows")[0]
    _, left_end, right_end = ends("cols")
    above, under = sides(odd_ref, even_ref)
    for t in range(WIDE[1] // 128):
        at = PIECE * t
        s = slice(128 * t, 128 * t + 128)
        for first, side in ((0, above), (72, under)):
            ll_ref[t, first : first + 8] = side(slice(at, at + 8))
        ll_ref[t, 8:72] = own_low[t]
        l_ref[t, 8:48] = lifted(ll_ref, t, 40, 4, 32)[0]
        for first, side in ((2, above), (46, under)):
            l_ref[t, first : first + 8] = side(slice(at + 8, at + 16))
        for first, side in ((4, above), (35, under)):
            b_ref[first : first + 9, s] = side(slice(at + 16, at + 25))
        for first, side in ((4, above), (80, under)):
            lh_ref[t, first : first + 12] = side(slice(at + 25, at + 37))
        lh_ref[t, 16:80] = own_high[t]
        h_ref[t, 0:48] = lifted(lh_ref, t, 48, 8, 32)[0]

    def limited(coeffs, level, kind):
        if kind == 3:
            return coeffs
        at = 3 * level + kind
        return soften(coeffs, limit_ref[at : at + 1, :])

    def keep(level, kind, t, s, coeffs, begin):
        own = OWN[level]
        coeffs = limited(coeffs[begin - 4 : begin + own + 4], level, kind)
        outs[3 * (level - 1) + kind][:, s] = coeffs
        if level == 3 or (level == 1 and kind != 1):
            first, last = coeffs[4:8], coeffs[own : own + 4]
            at = edge_at(level, kind, t)
            for_even[at : at + 4, :] = jnp.where(is_even, last, first)
            for_odd[at : at + 4, :] = jnp.where(is_even, first, last)

    for level in (1, 2, 3):
        own = OWN[level]
        if level == 1:
            sizes = ((32, 6), (24, 4))
        else:
            rows = (48, 32)[level - 2]
            sizes = ((rows // 2, own),) * 2
            known, wide = WIDE[level - 1], WIDE[level]
            if level == 3:
                b_ref[24:32, :known] = jnp.zeros((8, known), jnp.float32)
            b_ref[0:rows, known : 2 * wide] = jnp.zeros((rows, 2 * wide - known), jnp.float32)
            halves = split_pairs(b_ref[0:rows, : 2 * wide])
            low, high = lift_lanes(*halves, EDGE[level], 1024 >> level, left_end, right_end)
            spread(l_ref, slice(0, rows), low)
            spread(h_ref, slice(0, rows), high)
        for t in range(WIDE[level] // 128):
            s = slice(128 * t, 128 * t + 128)
            low, high = lifted(l_ref, t, *sizes[0], own)
            keep(level, 1, t, s, high, sizes[0][1])
            if level == 3:
                keep(level, 3, t, s, low, sizes[0][1])
            elif level == 2:
                b_ref[0 : sizes[0][0], s] = low
            else:
                b_ref[13:35, s] = low[3:25]
            low, high = lifted(h_ref, t, *sizes[1], own)
            keep(level, 0, t, s, low, sizes[1][1])
            keep(level, 2, t, s, high, sizes[1][1])


def detail_kernel(limit_ref, own_low, own_high, odd_ref, even_ref, hl_ref, lh_ref, hh_ref, x_ref):
    above, under = sides(odd_ref, even_ref)
    _, at_start, at_end = ends("cols")
    low, high = (
        jnp.concatenate(
            [
                jnp.concatenate([side(slice(PIECE * t + at, PIECE * t + at + 8)) for t in range(5)], 1)
                for side, at in sources
            ],
            0,
        )
        for sources in (((above, 0), (under, 0)), ((above, 29), (under, 25)))
    )
    lows = merge_pairs(*lift_lanes(low, high, EDGE[1], 512, at_start, at_end, inverse=True))
    for j in range(9):
        x_ref[j, 0:8] = lows[0:8, 128 * j : 128 * j + 128]
        x_ref[j, 8:72] = own_low[j]
        x_ref[j, 72:80] = lows[8:16, 128 * j : 128 * j + 128]
        at = slice(EDGES + 8 * j, EDGES + 8 * j + 8)
        x_ref[j + 9, 0:8] = above(at)
        x_ref[j + 9, 8:72] = own_high[j]
        x_ref[j + 9, 72:80] = under(at)

    def lift(t, s):
        high = lifted(x_ref, t, 40, 4, 32)[1]
        lh_ref[:, s] = soften(high, limit_ref[1:2, :])
        low, high = lifted(x_ref, t + 9, 40, 4, 32)
        hl_ref[:, s] = soften(low, limit_ref[0:1, :])
        hh_ref[:, s] = soften(high, limit_ref[2:3, :])

    tiles(WIDE[0], lift)


def inverse_kernel(odd_ref, even_ref, *rest):
    ins, out_ref, (v_ref, w_ref, r_ref), kept = rest[:13], rest[13], rest[14:17], rest[17:]
    _, at_start, at_end = ends("rows")
    _, left_end, right_end = ends("cols")
    above, under = sides(odd_ref, even_ref)
    for level in range(LEVELS - 1, -1, -1):
        own = OWN[level]
        long = max(own + 8, 16)
        near = neighbours(0, 4, own, at_start, at_end)

        def whole(kind, t, s, level=level, own=own, long=long):
            source = ins[3 * level + kind]
            if level == 2 or level == 0 or (level == 1 and kind == 1):
                return source[0:long, s]
            target, at = kept[kind], slice(edge_at(level, kind, t), edge_at(level, kind, t) + 4)
            target[0 : own + 8, s] = source[:, s]
            target[0:4, s] = above(at)
            target[4 + own : 8 + own, s] = under(at)
            return target[0:long, s]

        def lift_down(t, s, level=level, long=long, near=near, whole=whole):
            low = whole(3, t, s) if level == LEVELS - 1 else r_ref[4 : 4 + long, s]
            even, odd = inverse_lift(low, whole(1, t, s), near)
            v_ref[t, pl.ds(0, long, stride=2)] = even
            v_ref[t, pl.ds(1, long, stride=2)] = odd
            even, odd = inverse_lift(whole(0, t, s), whole(2, t, s), near)
            w_ref[t, pl.ds(0, long, stride=2)] = even
            w_ref[t, pl.ds(1, long, stride=2)] = odd

        wide = WIDE[level]
        tiles(wide, lift_down)
        first, rows = (8, 64) if level == 0 else (0, 2 * long)
        cut = slice(first, first + rows)
        even, odd = joined(v_ref, cut, wide), joined(w_ref, cut, wide)
        both = merge_pairs(
            *lift_lanes(even, odd, EDGE[level], 1024 >> level, left_end, right_end, inverse=True)
        )
        if level:
            r_ref[0:rows, : 2 * wide] = both
        else:
            out_ref[...] = both[:, 128 : 128 + COLS]


def swaps(axis, offset):
    count = lax.axis_size(axis)
    pairs = []
    for i in range(offset, count - 1, 2):
        pairs += [(i, i + 1), (i + 1, i)]
    return pairs


def exchange(for_even, for_odd, axis):
    even = lax.ppermute(for_even, axis, swaps(axis, 0))
    odd = lax.ppermute(for_odd, axis, swaps(axis, 1))
    return odd, even


def f32(*shape):
    return jax.ShapeDtypeStruct(shape, jnp.float32)


def scratch(*shape):
    return pltpu.VMEM(shape, jnp.float32)


def call(kernel, outs, scratches, *args, scalars=0, space=pltpu.VMEM, cost=None):
    vmem = pl.BlockSpec(memory_space=pltpu.VMEM)
    smem = pl.BlockSpec(memory_space=pltpu.SMEM)
    return pl.pallas_call(
        kernel,
        out_shape=outs,
        in_specs=[smem] * scalars + [pl.BlockSpec(memory_space=space)] * (len(args) - scalars),
        out_specs=jax.tree.map(lambda _: vmem, outs),
        scratch_shapes=scratches,
        compiler_params=pltpu.CompilerParams(vmem_limit_bytes=16 * 2**20),
        cost_estimate=cost,
    )(*args)


def local(micrograph, thresholds):
    for_even, for_odd = call(
        edges_kernel,
        (f32(ROWS, 128), f32(ROWS, 128)),
        [pltpu.SemaphoreType.DMA((2,))],
        micrograph,
        space=pltpu.HBM,
    )
    odd, even = exchange(for_even, for_odd, "cols")
    *inner, limits = call(
        inner_kernel,
        (f32(ROWS, 896), f32(ROWS, 896), f32(ROWS, 256), f32(16, 128)),
        [],
        thresholds,
        micrograph,
        scalars=1,
        cost=pl.CostEstimate(flops=2 * 10**9, bytes_accessed=4 * 10**6, transcendentals=0),
    )
    for_even, for_odd, *own = call(
        columns_kernel,
        (f32(PACK, 128), f32(PACK, 128))
        + (f32(9, ROWS, 128), f32(9, ROWS, 128), f32(5, ROWS, 128), f32(5, ROWS, 128)),
        [scratch(5, 32, 128), scratch(5, 16, 128)],
        *inner,
        odd,
        even,
    )
    own_low, own_high, own_low_low, own_low_high = own
    odd, even = exchange(for_even, for_odd, "rows")
    shapes = [f32(OWN[level] + 8, WIDE[level]) for level in range(LEVELS) for _ in range(3)]
    shapes.append(shapes[-1])
    for_even, for_odd, *bands = call(
        forward_kernel,
        (f32(72, 128), f32(72, 128), *shapes[3:]),
        [
            scratch(5, 64, 128),
            scratch(5, 96, 128),
            scratch(5, 80, 128),
            scratch(5, 96, 128),
            scratch(48, 768),
        ],
        limits,
        own_low_low,
        own_low_high,
        odd,
        even,
    )
    finest = call(
        detail_kernel,
        tuple(shapes[:3]),
        [scratch(18, 80, 128)],
        limits,
        own_low,
        own_high,
        odd,
        even,
        cost=pl.CostEstimate(flops=2 * 10**9, bytes_accessed=4 * 10**6, transcendentals=0),
    )
    odd, even = exchange(for_even, for_odd, "rows")
    return call(
        inverse_kernel,
        f32(ROWS, COLS),
        [scratch(9, 80, 128), scratch(9, 80, 128), scratch(48, 1280)]
        + [scratch(24, 640), scratch(16, 256), scratch(24, 640), scratch(16, 256)],
        odd,
        even,
        *finest,
        *bands,
    )


def solution(mesh):
    placed = (P("rows", "cols"), P())
    return jax.shard_map(
        local, mesh=mesh, in_specs=placed, out_specs=P("rows", "cols"), check_vma=False
    )
```

```python
import functools

import jax
import jax.numpy as jnp
from jax import lax
from jax.experimental import pallas as pl
from jax.experimental.pallas import tpu as pltpu
from jax.sharding import PartitionSpec as P

LEVELS = 4

step_one = -1.586134342
step_two = -0.05298011854
step_three = 0.8829110762
step_four = 0.4435068522
band_gain = 1.149604398
inv_gain = 1.0 / band_gain

ROWS, COLS = 64, 2048
WIDE = (1152, 640, 384, 256)
EDGE = (64, 32, 16, 8)
OWN = (32, 16, 8, 4)


STEPS_FROM = 1152
GROUP = 64
MATRIX_FROM = 640


def combined(*terms):
    total = {}
    for factor, taps, moved in terms:
        for (sequence, offset), tap in taps.items():
            key = (sequence, offset + moved)
            total[key] = total.get(key, 0.0) + factor * tap
    return total


def lifted_taps(inverse):
    even, odd = {("even", 0): 1.0}, {("odd", 0): 1.0}
    if inverse:
        even, odd = combined((1.0 / band_gain, even, 0)), combined((band_gain, odd, 0))
        for to_even, to_odd in ((step_four, step_three), (step_two, step_one)):
            even = combined((1.0, even, 0), (-to_even, odd, 0), (-to_even, odd, -1))
            odd = combined((1.0, odd, 0), (-to_odd, even, 0), (-to_odd, even, 1))
        return even, odd
    for to_odd, to_even in ((step_one, step_two), (step_three, step_four)):
        odd = combined((1.0, odd, 0), (to_odd, even, 0), (to_odd, even, 1))
        even = combined((1.0, even, 0), (to_even, odd, 0), (to_even, odd, -1))
    return combined((band_gain, even, 0)), combined((1.0 / band_gain, odd, 0))


def lift_lanes(even, odd, first, count, at_start, at_end, inverse=False):
    rows, width = even.shape
    if width >= STEPS_FROM:
        near = neighbours(1, [(first, at_start)], [(first + count - 1, at_end)])
        lift = inverse_lift if inverse else forward_lift
        groups = [slice(k, min(k + GROUP, rows)) for k in range(0, rows, GROUP)]
        parts = [lift(even[g], odd[g], near) for g in groups]
        return [jnp.concatenate(x, 0) if len(x) > 1 else x[0] for x in zip(*parts)]
    last = first + count - 1
    e, o = {0: even}, {0: odd}
    for x in (e, o):
        width = x[0].shape[1]
        for offset in (-2, -1, 1, 2):
            x[offset] = pltpu.roll(x[0], -offset % width, 1)
    fixed = lambda x, source, lane, flag: patch(x, source, 1, lane, flag)
    ends_of = {
        ("even", -1): [(e[1], first, at_start)],
        ("even", -2): [(e[2], first, at_start), (e[0], first + 1, at_start)],
        ("even", 1): [(e[0], last, at_end)],
        ("even", 2): [(e[-1], last, at_end), (e[1], last - 1, at_end)],
        ("odd", -1): [(o[0], first, at_start)],
        ("odd", -2): [(o[1], first, at_start), (o[-1], first + 1, at_start)],
        ("odd", 1): [(o[-1], last, at_end)],
        ("odd", 2): [(o[-2], last, at_end), (o[0], last - 1, at_end)],
    }
    shifted = {("even", 0): even, ("odd", 0): odd}
    for (sequence, offset), patches in ends_of.items():
        x = (e if sequence == "even" else o)[offset]
        for patch_of in patches:
            x = fixed(x, *patch_of)
        shifted[sequence, offset] = x
    out = []
    for taps in lifted_taps(inverse):
        by_tap = {}
        for key, tap in sorted(taps.items()):
            by_tap.setdefault(round(tap, 9), []).append((tap, shifted[key]))
        total = None
        for group in by_tap.values():
            term = sum((x for _, x in group[1:]), group[0][1]) * group[0][0]
            total = term if total is None else total + term
        out.append(total)
    return out


def soften(coeffs, limit):
    return coeffs - jnp.minimum(jnp.maximum(coeffs, -limit), limit)


def patch(shifted, source, axis, index, flag):
    unit = 8 if axis == 0 else 128
    lo = index // unit * unit
    hi = min(lo + unit, shifted.shape[axis])
    cut = functools.partial(lax.slice_in_dim, axis=axis)
    tile = cut(shifted, lo, hi)
    here = (lax.broadcasted_iota(jnp.int32, tile.shape, axis) == index - lo) & flag
    tile = jnp.where(here, cut(source, lo, hi), tile)
    parts = [cut(shifted, 0, lo)] if lo else []
    parts.append(tile)
    if hi < shifted.shape[axis]:
        parts.append(cut(shifted, hi, shifted.shape[axis]))
    return jnp.concatenate(parts, axis) if len(parts) > 1 else tile


def neighbours(axis, starts, stops):
    def before(odd):
        rolled = pltpu.roll(odd, 1, axis)
        for index, flag in starts:
            rolled = patch(rolled, odd, axis, index, flag)
        return rolled

    def after(even):
        rolled = pltpu.roll(even, even.shape[axis] - 1, axis)
        for index, flag in stops:
            rolled = patch(rolled, even, axis, index, flag)
        return rolled

    return before, after


def forward_lift(even, odd, near):
    before, after = near
    odd = odd + step_one * (even + after(even))
    even = even + step_two * (before(odd) + odd)
    odd = odd + step_three * (even + after(even))
    even = even + step_four * (before(odd) + odd)
    return even * band_gain, odd * inv_gain


def inverse_lift(low, high, near):
    before, after = near
    even = low * inv_gain
    odd = high * band_gain
    even = even - step_four * (before(odd) + odd)
    odd = odd - step_three * (even + after(even))
    even = even - step_two * (before(odd) + odd)
    odd = odd - step_one * (even + after(even))
    return even, odd


def pairing(transpose):
    a = lax.broadcasted_iota(jnp.int32, (256, 256), 1 if not transpose else 0)
    b = lax.broadcasted_iota(jnp.int32, (256, 256), 0 if not transpose else 1)
    target = jnp.where(a < 128, 2 * a, 2 * a - 255)
    return jnp.where(b == target, 1.0, 0.0).astype(jnp.bfloat16)


def permuted(x, matrix):
    rows = x.shape[0]
    high = x.astype(jnp.bfloat16)
    rest = x - high.astype(jnp.float32)
    middle = rest.astype(jnp.bfloat16)
    last = (rest - middle.astype(jnp.float32)).astype(jnp.bfloat16)
    out = jnp.dot(
        jnp.concatenate([high, middle, last], 0), matrix, preferred_element_type=jnp.float32
    )
    return (out[:rows] + out[rows : 2 * rows]) + out[2 * rows :]


def picked(x, index):
    return jnp.take_along_axis(x, index, axis=1, mode="promise_in_bounds")


def split_pairs(x):
    if x.shape[1] < 2 * MATRIX_FROM:
        return split_by_picks(x)
    matrix = pairing(False)
    both = [permuted(x[:, k : k + 256], matrix) for k in range(0, x.shape[1], 256)]
    return jnp.concatenate([y[:, :128] for y in both], 1), jnp.concatenate([y[:, 128:] for y in both], 1)


def merge_pairs(even, odd):
    if even.shape[1] < MATRIX_FROM:
        return merge_by_picks(even, odd)
    matrix = pairing(True)
    return jnp.concatenate(
        [
            permuted(jnp.concatenate([even[:, k : k + 128], odd[:, k : k + 128]], 1), matrix)
            for k in range(0, even.shape[1], 128)
        ],
        1,
    )


def split_by_picks(x):
    rows = x.shape[0]
    lane = lax.broadcasted_iota(jnp.int32, (rows, 128), 1)
    lower = lane < 64
    near = jnp.where(lower, 2 * lane, 2 * lane - 127)
    far = jnp.where(lower, 2 * lane + 1, 2 * lane - 128)
    evens, odds = [], []
    for k in range(0, x.shape[1], 256):
        first, second = picked(x[:, k : k + 128], near), picked(x[:, k + 128 : k + 256], far)
        evens.append(jnp.where(lower, first, second))
        odds.append(pltpu.roll(jnp.where(lower, second, first), 64, 1))
    return jnp.concatenate(evens, 1), jnp.concatenate(odds, 1)


def merge_by_picks(even, odd):
    rows = even.shape[0]
    lane = lax.broadcasted_iota(jnp.int32, (rows, 128), 1)
    lower = lane < 64
    is_odd = lane % 2 == 1
    half = lane // 2
    near = jnp.where(is_odd, half + 64, half)
    far = jnp.where(is_odd, half, half + 64)
    out = []
    for k in range(0, even.shape[1], 128):
        e, o = even[:, k : k + 128], pltpu.roll(odd[:, k : k + 128], 64, 1)
        out += [picked(jnp.where(lower, e, o), near), picked(jnp.where(lower, o, e), far)]
    return jnp.concatenate(out, 1)


def tiles(width, body):
    def step(t, carry):
        body(t, pl.ds(pl.multiple_of(t * 128, 128), 128))
        return carry

    if width > 640:
        lax.fori_loop(0, width // 128, step, 0)
    else:
        for t in range(width // 128):
            body(t, slice(128 * t, 128 * t + 128))


def joined(ref, rows, width):
    return jnp.concatenate([ref[k, rows] for k in range(width // 128)], 1)


def spread(ref, rows, value):
    for k in range(value.shape[1] // 128):
        ref[k, rows] = value[:, 128 * k : 128 * k + 128]


def ends(axis):
    position = lax.axis_index(axis)
    return position % 2 == 0, position == 0, position == lax.axis_size(axis) - 1


def edges_kernel(x_ref, for_even, for_odd, sems):
    is_even = ends("cols")[0]
    right = jnp.where(is_even, COLS - 128, 0)
    copies = []
    for k, (at, out) in enumerate(((right, for_even), (COLS - 128 - right, for_odd))):
        lanes = pl.ds(pl.multiple_of(at, 128), 128)
        copies.append(pltpu.make_async_copy(x_ref.at[:, lanes], out, sems.at[k]))
        copies[-1].start()
    for copy in copies:
        copy.wait()


def inner_kernel(t_ref, x_ref, e_ref, o_ref, edge_ref, limit_ref):
    for level in range(LEVELS):
        for kind in range(3):
            limit_ref[3 * level + kind : 3 * level + kind + 1, :] = jnp.full((1, 128), t_ref[level, kind])
    e_ref[...], o_ref[...] = split_pairs(x_ref[:, 128 : COLS - 128])
    edge_ref[:, :128] = x_ref[:, :128]
    edge_ref[:, 128:] = x_ref[:, COLS - 128 :]


def columns_kernel(
    e_ref, o_ref, edge_ref, odd_ref, even_ref, for_even, for_odd, for_even_far, for_odd_far,
    low_ref, high_ref, low_low_ref, low_high_ref, one_ref, two_ref, one_high_ref,
):
    is_even, at_start, at_end = ends("cols")
    left = jnp.where(is_even, odd_ref[...], even_ref[...])
    right = jnp.where(is_even, even_ref[...], odd_ref[...])
    first = split_pairs(jnp.concatenate([left, edge_ref[:, :128]], 1))
    last = split_pairs(jnp.concatenate([edge_ref[:, 128:], right], 1))
    low, high = lift_lanes(
        jnp.concatenate([first[0], e_ref[...], last[0]], 1),
        jnp.concatenate([first[1], o_ref[...], last[1]], 1),
        EDGE[0],
        1024,
        at_start,
        at_end,
    )
    spread(low_ref, slice(None), low)
    spread(high_ref, slice(None), high)
    wide = WIDE[1]
    low = jnp.concatenate([low, jnp.zeros((ROWS, 2 * wide - WIDE[0]), jnp.float32)], 1)
    low, high = lift_lanes(*split_pairs(low), EDGE[1], 512, at_start, at_end)
    spread(low_low_ref, slice(None), low)
    spread(low_high_ref, slice(None), high)
    for t in range(wide // 128):
        one_ref[t] = plain_low(low_low_ref, t, 32)
        two_ref[t] = plain_low(one_ref, t, 16)
        one_high_ref[t] = plain_low(low_high_ref, t, 32)
    row = lax.axis_index("rows")
    below = (row % 2 == 0).astype(jnp.int32)
    for pack, last in ((for_even, below), (for_odd, 1 - below)):
        for t in range(wide // 128):
            at = PIECE * t
            pack[at : at + 8] = low_low_ref[t, 0:8]
            pack[at + 8 : at + 16] = low_low_ref[t, 56:64]
            pack[at + 16 : at + 24] = one_ref[t, 2:10]
            pack[at + 24 : at + 32] = one_ref[t, 22:30]
            pack[at + 32 : at + 42] = two_ref[t, 3:13]
            pack[at + 42 : at + 50] = low_high_ref[t, pl.ds(56 * last, 8)]
            pack[at + 50 : at + 58] = one_high_ref[t, pl.ds(2 + 20 * last, 8)]
        for j in range(9):
            pack[EDGES + 8 * j : EDGES + 8 * j + 8] = high_ref[j, pl.ds(56 * last, 8)]
    below = (row % 4 < 2).astype(jnp.int32)
    for pack, last in ((for_even_far, below), (for_odd_far, 1 - below)):
        for t in range(wide // 128):
            at = FAR_PIECE * t
            pack[at : at + 8] = low_low_ref[t, pl.ds(56 * last, 8)]
            pack[at + 8 : at + 16] = one_ref[t, pl.ds(2 + 20 * last, 8)]
            pack[at + 16 : at + 25] = two_ref[t, pl.ds(3 + last, 9)]


PIECE, EDGES, PACK = 58, 296, 368
FAR_PIECE, FAR_PACK = 25, 128


def plain_low(ref, t, tall):
    near = (lambda x: pltpu.roll(x, 1, 0)), (lambda x: pltpu.roll(x, tall - 1, 0))
    return forward_lift(ref[t, pl.ds(0, tall, stride=2)], ref[t, pl.ds(1, tall, stride=2)], near)[0]


def sides(flag, odd_ref, even_ref):
    def above(*at):
        return jnp.where(flag, odd_ref[at], even_ref[at])

    def under(*at):
        return jnp.where(flag, even_ref[at], odd_ref[at])

    return above, under


def halves_of(ref, t, tall):
    return ref[t, pl.ds(0, tall, stride=2)], ref[t, pl.ds(1, tall, stride=2)]


def lifted(ref, t, tall, begin, own):
    row, count = lax.axis_index("rows"), lax.axis_size("rows")
    starts, stops = [(begin, row == 0)], [(begin + own - 1, row == count - 1)]
    if begin >= own:
        starts.append((begin - own, row == 1))
        stops.append((begin + 2 * own - 1, row == count - 2))
    return forward_lift(*halves_of(ref, t, tall), neighbours(0, starts, stops))


def forward_part(limits, own_low, own_high, near_sides, far_sides, outs, refs):
    l_ref, h_ref, ll_ref, lh_ref, f_ref, g_ref, b_ref = refs
    (above, under), (above_far, under_far) = near_sides, far_sides
    row, count = lax.axis_index("rows"), lax.axis_size("rows")
    _, left_end, right_end = ends("cols")
    for t in range(WIDE[1] // 128):
        at, far = PIECE * t, FAR_PIECE * t
        s = slice(128 * t, 128 * t + 128)

        def part(offset, size=8, at=at):
            return slice(at + offset, at + offset + size)

        def far_part(offset, size=8, far=far):
            return slice(far + offset, far + offset + size)

        ll_ref[t, 0:8], ll_ref[t, 8:72], ll_ref[t, 72:80] = above(part(8)), own_low[t], under(part(0))
        lh_ref[t, 0:8], lh_ref[t, 8:72], lh_ref[t, 72:80] = above(part(42)), own_high[t], under(part(42))
        l_ref[t, 8:48] = lifted(ll_ref, t, 40, 4, 32)[0]
        l_ref[t, 2:10], l_ref[t, 46:54] = above(part(24)), under(part(16))
        h_ref[t, 8:48] = lifted(lh_ref, t, 40, 4, 32)[0]
        h_ref[t, 2:10], h_ref[t, 46:54] = above(part(50)), under(part(50))
        f_ref[t, 0:8], f_ref[t, 8:16] = above_far(far_part(0)), above(part(0))
        f_ref[t, 16:24], f_ref[t, 24:32] = under(part(8)), under_far(far_part(0))
        near = neighbours(0, [(4, row == 1)], [(11, row == count - 2)])
        one = forward_lift(*halves_of(f_ref, t, 16), near)[0]
        g_ref[t, 10:14], g_ref[t, 42:46] = one[2:6], one[10:14]
        g_ref[t, 2:10], g_ref[t, 14:22] = above_far(far_part(8)), above(part(16))
        g_ref[t, 34:42], g_ref[t, 46:54] = under(part(24)), under_far(far_part(8))
        near = neighbours(0, [(6, row == 1)], [(21, row == count - 2)])
        two = forward_lift(*halves_of(g_ref, t, 32), near)[0]
        b_ref[0:9, s], b_ref[9:15, s], b_ref[15:25, s] = above_far(far_part(16, 9)), two[3:9], above(part(32, 10))
        b_ref[47:57, s], b_ref[57:63, s], b_ref[63:72, s] = under(part(32, 10)), two[19:25], under_far(far_part(16, 9))

    def keep(level, kind, s, coeffs, begin):
        coeffs = coeffs[begin - 4 : begin + OWN[level] + 4]
        if kind < 3:
            at = 3 * level + kind
            coeffs = soften(coeffs, limits[at : at + 1, :])
        outs[3 * level + kind][0 : OWN[level] + 8, s] = coeffs

    for level in (1, 2, 3):
        own = OWN[level]
        tall, begin = ((32, 6), (40, 14), (16, 6))[level - 1]
        if level > 1:
            rows, known, wide = (72, 32)[level - 2], WIDE[level - 1], WIDE[level]
            b_ref[0:rows, known : 2 * wide] = jnp.zeros((rows, 2 * wide - known), jnp.float32)
            halves = split_pairs(b_ref[0:rows, : 2 * wide])
            low, high = lift_lanes(*halves, EDGE[level], 1024 >> level, left_end, right_end)
            spread(l_ref, slice(0, rows), low)
            spread(h_ref, slice(0, rows), high)
        for t in range(WIDE[level] // 128):
            s = slice(128 * t, 128 * t + 128)
            low, high = lifted(l_ref, t, tall, begin, own)
            keep(level, 1, s, high, begin)
            if level == 1:
                b_ref[25:47, s] = low[3:25]
            elif level == 2:
                b_ref[0:32, s] = low[2:34]
            else:
                keep(level, 3, s, low, begin)
            low, high = lifted(h_ref, t, tall, begin, own)
            keep(level, 0, s, low, begin)
            keep(level, 2, s, high, begin)


def detail_part(limits, own_low, own_high, near_sides, outs, x_ref):
    above, under = near_sides
    _, at_start, at_end = ends("cols")
    low, high = (
        jnp.concatenate(
            [
                jnp.concatenate([side(slice(PIECE * t + at, PIECE * t + at + 8)) for t in range(5)], 1)
                for side, at in sources
            ],
            0,
        )
        for sources in (((above, 8), (under, 0)), ((above, 42), (under, 42)))
    )
    lows = merge_pairs(*lift_lanes(low, high, EDGE[1], 512, at_start, at_end, inverse=True))
    for j in range(9):
        x_ref[j, 0:8] = lows[0:8, 128 * j : 128 * j + 128]
        x_ref[j, 8:72] = own_low[j]
        x_ref[j, 72:80] = lows[8:16, 128 * j : 128 * j + 128]
        at = slice(EDGES + 8 * j, EDGES + 8 * j + 8)
        x_ref[j + 9, 0:8] = above(at)
        x_ref[j + 9, 8:72] = own_high[j]
        x_ref[j + 9, 72:80] = under(at)

    def lift(t, s):
        high = lifted(x_ref, t, 40, 4, 32)[1]
        outs[1][:, s] = soften(high, limits[1:2, :])
        low, high = lifted(x_ref, t + 9, 40, 4, 32)
        outs[0][:, s] = soften(low, limits[0:1, :])
        outs[2][:, s] = soften(high, limits[2:3, :])

    tiles(WIDE[0], lift)


def inverse_part(ins, out_ref, v_ref, w_ref, r_ref):
    _, at_start, at_end = ends("rows")
    _, left_end, right_end = ends("cols")
    for level in range(LEVELS - 1, -1, -1):
        own = OWN[level]
        long = max(own + 8, 16)
        near = neighbours(0, [(4, at_start)], [(3 + own, at_end)])
        hl, lh, hh = ins[3 * level : 3 * level + 3]

        def lift_down(t, s, level=level, long=long, near=near, hl=hl, lh=lh, hh=hh):
            low = ins[12][0:long, s] if level == LEVELS - 1 else r_ref[4 : 4 + long, s]
            even, odd = inverse_lift(low, lh[0:long, s], near)
            v_ref[t, pl.ds(0, long, stride=2)] = even
            v_ref[t, pl.ds(1, long, stride=2)] = odd
            even, odd = inverse_lift(hl[0:long, s], hh[0:long, s], near)
            w_ref[t, pl.ds(0, long, stride=2)] = even
            w_ref[t, pl.ds(1, long, stride=2)] = odd

        wide = WIDE[level]
        tiles(wide, lift_down)
        first, rows = (8, 64) if level == 0 else (0, 2 * long)
        cut = slice(first, first + rows)
        even, odd = joined(v_ref, cut, wide), joined(w_ref, cut, wide)
        both = merge_pairs(
            *lift_lanes(even, odd, EDGE[level], 1024 >> level, left_end, right_end, inverse=True)
        )
        if level:
            r_ref[0:rows, : 2 * wide] = both
        else:
            out_ref[...] = both[:, 128 : 128 + COLS]


def rows_kernel(
    limits, own_low, own_high, own_low_low, own_low_high, odd_ref, even_ref, odd_far, even_far, out_ref, *refs
):
    bands, refs = refs[:13], refs[13:]
    row = lax.axis_index("rows")
    near_sides = sides(row % 2 == 0, odd_ref, even_ref)
    far_sides = sides(row % 4 < 2, odd_far, even_far)
    forward_part(limits, own_low_low, own_low_high, near_sides, far_sides, bands, refs[:7])
    detail_part(limits, own_low, own_high, near_sides, bands, refs[7])
    inverse_part(bands, out_ref, *refs[8:])


def swaps(axis, offset, apart):
    count = lax.axis_size(axis)
    pairs = []
    for block in range(offset, count, 2 * apart):
        for i in range(block, min(block + apart, count - apart)):
            pairs += [(i, i + apart), (i + apart, i)]
    return pairs


def exchange(for_even, for_odd, axis, apart=1):
    even = lax.ppermute(for_even, axis, swaps(axis, 0, apart))
    odd = lax.ppermute(for_odd, axis, swaps(axis, apart, apart))
    return odd, even


def f32(*shape):
    return jax.ShapeDtypeStruct(shape, jnp.float32)


def scratch(*shape):
    return pltpu.VMEM(shape, jnp.float32)


def call(kernel, outs, scratches, *args, scalars=0, space=pltpu.VMEM, cost=None):
    vmem = pl.BlockSpec(memory_space=pltpu.VMEM)
    smem = pl.BlockSpec(memory_space=pltpu.SMEM)
    return pl.pallas_call(
        kernel,
        out_shape=outs,
        in_specs=[smem] * scalars + [pl.BlockSpec(memory_space=space)] * (len(args) - scalars),
        out_specs=jax.tree.map(lambda _: vmem, outs),
        scratch_shapes=scratches,
        compiler_params=pltpu.CompilerParams(vmem_limit_bytes=16 * 2**20),
        cost_estimate=cost,
    )(*args)


def local(micrograph, thresholds):
    for_even, for_odd = call(
        edges_kernel,
        (f32(ROWS, 128), f32(ROWS, 128)),
        [pltpu.SemaphoreType.DMA((2,))],
        micrograph,
        space=pltpu.HBM,
    )
    odd, even = exchange(for_even, for_odd, "cols")
    *inner, limits = call(
        inner_kernel,
        (f32(ROWS, 896), f32(ROWS, 896), f32(ROWS, 256), f32(16, 128)),
        [],
        thresholds,
        micrograph,
        scalars=1,
        cost=pl.CostEstimate(flops=2 * 10**9, bytes_accessed=4 * 10**6, transcendentals=0),
    )
    for_even, for_odd, for_even_far, for_odd_far, *own = call(
        columns_kernel,
        (f32(PACK, 128), f32(PACK, 128), f32(FAR_PACK, 128), f32(FAR_PACK, 128))
        + (f32(9, ROWS, 128), f32(9, ROWS, 128), f32(5, ROWS, 128), f32(5, ROWS, 128)),
        [scratch(5, 32, 128), scratch(5, 16, 128), scratch(5, 32, 128)],
        *inner,
        odd,
        even,
    )
    received = exchange(for_even, for_odd, "rows")
    received += exchange(for_even_far, for_odd_far, "rows", 2)
    bands = [scratch(max(OWN[level] + 8, 16), WIDE[level]) for level in range(LEVELS) for _ in range(3)]
    return call(
        rows_kernel,
        f32(ROWS, COLS),
        [*bands, bands[-1]]
        + [scratch(5, 80, 128), scratch(5, 80, 128), scratch(5, 80, 128), scratch(5, 80, 128)]
        + [scratch(5, 32, 128), scratch(5, 64, 128), scratch(72, 768), scratch(18, 80, 128)]
        + [scratch(9, 80, 128), scratch(9, 80, 128), scratch(48, 1280)],
        limits,
        *own,
        *received,
    )


def solution(mesh):
    placed = (P("rows", "cols"), P())
    return jax.shard_map(
        local, mesh=mesh, in_specs=placed, out_specs=P("rows", "cols"), check_vma=False
    )
```

```python
import functools

import jax
import jax.numpy as jnp
from jax import lax
from jax.experimental import pallas as pl
from jax.experimental.pallas import tpu as pltpu
from jax.sharding import PartitionSpec as P

LEVELS = 4

step_one = -1.586134342
step_two = -0.05298011854
step_three = 0.8829110762
step_four = 0.4435068522
band_gain = 1.149604398
inv_gain = 1.0 / band_gain

ROWS, COLS = 64, 2048
WIDE = (1152, 640, 384, 256)
EDGE = (64, 32, 16, 8)
OWN = (32, 16, 8, 4)


STEPS_FROM = 1152
GROUP = 64
MATRIX_FROM = 640


def combined(*terms):
    total = {}
    for factor, taps, moved in terms:
        for (sequence, offset), tap in taps.items():
            key = (sequence, offset + moved)
            total[key] = total.get(key, 0.0) + factor * tap
    return total


def lifted_taps(inverse):
    even, odd = {("even", 0): 1.0}, {("odd", 0): 1.0}
    if inverse:
        even, odd = combined((1.0 / band_gain, even, 0)), combined((band_gain, odd, 0))
        for to_even, to_odd in ((step_four, step_three), (step_two, step_one)):
            even = combined((1.0, even, 0), (-to_even, odd, 0), (-to_even, odd, -1))
            odd = combined((1.0, odd, 0), (-to_odd, even, 0), (-to_odd, even, 1))
        return even, odd
    for to_odd, to_even in ((step_one, step_two), (step_three, step_four)):
        odd = combined((1.0, odd, 0), (to_odd, even, 0), (to_odd, even, 1))
        even = combined((1.0, even, 0), (to_even, odd, 0), (to_even, odd, -1))
    return combined((band_gain, even, 0)), combined((1.0 / band_gain, odd, 0))


def lift_lanes(even, odd, first, count, at_start, at_end, inverse=False):
    rows, width = even.shape
    if width >= STEPS_FROM:
        near = neighbours(1, [(first, at_start)], [(first + count - 1, at_end)])
        lift = inverse_lift if inverse else forward_lift
        groups = [slice(k, min(k + GROUP, rows)) for k in range(0, rows, GROUP)]
        parts = [lift(even[g], odd[g], near) for g in groups]
        return [jnp.concatenate(x, 0) if len(x) > 1 else x[0] for x in zip(*parts)]
    last = first + count - 1
    e, o = {0: even}, {0: odd}
    for x in (e, o):
        width = x[0].shape[1]
        for offset in (-2, -1, 1, 2):
            x[offset] = pltpu.roll(x[0], -offset % width, 1)
    fixed = lambda x, source, lane, flag: patch(x, source, 1, lane, flag)
    ends_of = {
        ("even", -1): [(e[1], first, at_start)],
        ("even", -2): [(e[2], first, at_start), (e[0], first + 1, at_start)],
        ("even", 1): [(e[0], last, at_end)],
        ("even", 2): [(e[-1], last, at_end), (e[1], last - 1, at_end)],
        ("odd", -1): [(o[0], first, at_start)],
        ("odd", -2): [(o[1], first, at_start), (o[-1], first + 1, at_start)],
        ("odd", 1): [(o[-1], last, at_end)],
        ("odd", 2): [(o[-2], last, at_end), (o[0], last - 1, at_end)],
    }
    shifted = {("even", 0): even, ("odd", 0): odd}
    for (sequence, offset), patches in ends_of.items():
        x = (e if sequence == "even" else o)[offset]
        for patch_of in patches:
            x = fixed(x, *patch_of)
        shifted[sequence, offset] = x
    out = []
    for taps in lifted_taps(inverse):
        by_tap = {}
        for key, tap in sorted(taps.items()):
            by_tap.setdefault(round(tap, 9), []).append((tap, shifted[key]))
        total = None
        for group in by_tap.values():
            term = sum((x for _, x in group[1:]), group[0][1]) * group[0][0]
            total = term if total is None else total + term
        out.append(total)
    return out


def soften(coeffs, limit):
    return coeffs - jnp.minimum(jnp.maximum(coeffs, -limit), limit)


def patch(shifted, source, axis, index, flag):
    unit = 8 if axis == 0 else 128
    lo = index // unit * unit
    hi = min(lo + unit, shifted.shape[axis])
    cut = functools.partial(lax.slice_in_dim, axis=axis)
    tile = cut(shifted, lo, hi)
    here = (lax.broadcasted_iota(jnp.int32, tile.shape, axis) == index - lo) & flag
    tile = jnp.where(here, cut(source, lo, hi), tile)
    parts = [cut(shifted, 0, lo)] if lo else []
    parts.append(tile)
    if hi < shifted.shape[axis]:
        parts.append(cut(shifted, hi, shifted.shape[axis]))
    return jnp.concatenate(parts, axis) if len(parts) > 1 else tile


def neighbours(axis, starts, stops):
    def before(odd):
        rolled = pltpu.roll(odd, 1, axis)
        for index, flag in starts:
            rolled = patch(rolled, odd, axis, index, flag)
        return rolled

    def after(even):
        rolled = pltpu.roll(even, even.shape[axis] - 1, axis)
        for index, flag in stops:
            rolled = patch(rolled, even, axis, index, flag)
        return rolled

    return before, after


def forward_lift(even, odd, near):
    before, after = near
    odd = odd + step_one * (even + after(even))
    even = even + step_two * (before(odd) + odd)
    odd = odd + step_three * (even + after(even))
    even = even + step_four * (before(odd) + odd)
    return even * band_gain, odd * inv_gain


def inverse_lift(low, high, near):
    before, after = near
    even = low * inv_gain
    odd = high * band_gain
    even = even - step_four * (before(odd) + odd)
    odd = odd - step_three * (even + after(even))
    even = even - step_two * (before(odd) + odd)
    odd = odd - step_one * (even + after(even))
    return even, odd


def pairing(transpose):
    a = lax.broadcasted_iota(jnp.int32, (256, 256), 1 if not transpose else 0)
    b = lax.broadcasted_iota(jnp.int32, (256, 256), 0 if not transpose else 1)
    target = jnp.where(a < 128, 2 * a, 2 * a - 255)
    return jnp.where(b == target, 1.0, 0.0).astype(jnp.bfloat16)


def permuted(x, matrix):
    rows = x.shape[0]
    high = x.astype(jnp.bfloat16).astype(jnp.float32)
    rest = x - high
    middle = rest.astype(jnp.bfloat16).astype(jnp.float32)
    pieces = [high, middle, rest - middle]
    if rows % 16:
        pieces.append(jnp.zeros((-3 * rows % 16, x.shape[1]), jnp.float32))
        pieces = [jnp.concatenate(pieces, 0).astype(jnp.bfloat16)]
    else:
        pieces = [jnp.concatenate([piece.astype(jnp.bfloat16) for piece in pieces], 0)]
    out = jnp.dot(pieces[0], matrix, preferred_element_type=jnp.float32)
    return (out[:rows] + out[rows : 2 * rows]) + out[2 * rows : 3 * rows]


def picked(x, index):
    return jnp.take_along_axis(x, index, axis=1, mode="promise_in_bounds")


def split_pairs(x):
    if x.shape[1] < 2 * MATRIX_FROM:
        return split_by_picks(x)
    matrix = pairing(False)
    both = [permuted(x[:, k : k + 256], matrix) for k in range(0, x.shape[1], 256)]
    return jnp.concatenate([y[:, :128] for y in both], 1), jnp.concatenate([y[:, 128:] for y in both], 1)


def merge_pairs(even, odd):
    if even.shape[1] < MATRIX_FROM:
        return merge_by_picks(even, odd)
    matrix = pairing(True)
    return jnp.concatenate(
        [
            permuted(jnp.concatenate([even[:, k : k + 128], odd[:, k : k + 128]], 1), matrix)
            for k in range(0, even.shape[1], 128)
        ],
        1,
    )


def split_by_picks(x):
    rows = x.shape[0]
    lane = lax.broadcasted_iota(jnp.int32, (rows, 128), 1)
    lower = lane < 64
    near = jnp.where(lower, 2 * lane, 2 * lane - 127)
    far = jnp.where(lower, 2 * lane + 1, 2 * lane - 128)
    evens, odds = [], []
    for k in range(0, x.shape[1], 256):
        first, second = picked(x[:, k : k + 128], near), picked(x[:, k + 128 : k + 256], far)
        evens.append(jnp.where(lower, first, second))
        odds.append(pltpu.roll(jnp.where(lower, second, first), 64, 1))
    return jnp.concatenate(evens, 1), jnp.concatenate(odds, 1)


def merge_by_picks(even, odd):
    rows = even.shape[0]
    lane = lax.broadcasted_iota(jnp.int32, (rows, 128), 1)
    lower = lane < 64
    is_odd = lane % 2 == 1
    half = lane // 2
    near = jnp.where(is_odd, half + 64, half)
    far = jnp.where(is_odd, half, half + 64)
    out = []
    for k in range(0, even.shape[1], 128):
        e, o = even[:, k : k + 128], pltpu.roll(odd[:, k : k + 128], 64, 1)
        out += [picked(jnp.where(lower, e, o), near), picked(jnp.where(lower, o, e), far)]
    return jnp.concatenate(out, 1)


def tiles(width, body):
    def step(t, carry):
        body(t, pl.ds(pl.multiple_of(t * 128, 128), 128))
        return carry

    if width > 640:
        lax.fori_loop(0, width // 128, step, 0)
    else:
        for t in range(width // 128):
            body(t, slice(128 * t, 128 * t + 128))


def joined(ref, rows, width):
    return jnp.concatenate([ref[k, rows] for k in range(width // 128)], 1)


def spread(ref, rows, value):
    for k in range(value.shape[1] // 128):
        ref[k, rows] = value[:, 128 * k : 128 * k + 128]


def ends(axis):
    position = lax.axis_index(axis)
    return position % 2 == 0, position == 0, position == lax.axis_size(axis) - 1


def edges_kernel(x_ref, for_even, for_odd, sems):
    is_even = ends("cols")[0]
    right = jnp.where(is_even, COLS - 128, 0)
    copies = []
    for k, (at, out) in enumerate(((right, for_even), (COLS - 128 - right, for_odd))):
        lanes = pl.ds(pl.multiple_of(at, 128), 128)
        copies.append(pltpu.make_async_copy(x_ref.at[:, lanes], out, sems.at[k]))
        copies[-1].start()
    for copy in copies:
        copy.wait()


def inner_kernel(t_ref, x_ref, e_ref, o_ref, edge_ref, limit_ref):
    for level in range(LEVELS):
        for kind in range(3):
            limit_ref[3 * level + kind : 3 * level + kind + 1, :] = jnp.full((1, 128), t_ref[level, kind])
    e_ref[...], o_ref[...] = split_pairs(x_ref[:, 128 : COLS - 128])
    edge_ref[:, :128] = x_ref[:, :128]
    edge_ref[:, 128:] = x_ref[:, COLS - 128 :]


def columns_kernel(
    e_ref, o_ref, edge_ref, odd_ref, even_ref, for_even, for_odd, for_even_far, for_odd_far,
    low_ref, high_ref, low_low_ref, low_high_ref, one_ref, two_ref, one_high_ref,
):
    is_even, at_start, at_end = ends("cols")
    left = jnp.where(is_even, odd_ref[...], even_ref[...])
    right = jnp.where(is_even, even_ref[...], odd_ref[...])
    first = split_pairs(jnp.concatenate([left, edge_ref[:, :128]], 1))
    last = split_pairs(jnp.concatenate([edge_ref[:, 128:], right], 1))
    low, high = lift_lanes(
        jnp.concatenate([first[0], e_ref[...], last[0]], 1),
        jnp.concatenate([first[1], o_ref[...], last[1]], 1),
        EDGE[0],
        1024,
        at_start,
        at_end,
    )
    spread(low_ref, slice(None), low)
    spread(high_ref, slice(None), high)
    wide = WIDE[1]
    low = jnp.concatenate([low, jnp.zeros((ROWS, 2 * wide - WIDE[0]), jnp.float32)], 1)
    low, high = lift_lanes(*split_pairs(low), EDGE[1], 512, at_start, at_end)
    spread(low_low_ref, slice(None), low)
    spread(low_high_ref, slice(None), high)
    for t in range(wide // 128):
        one_ref[t] = plain_low(low_low_ref, t, 32)
        two_ref[t] = plain_low(one_ref, t, 16)
        one_high_ref[t] = plain_low(low_high_ref, t, 32)
    row = lax.axis_index("rows")
    below = (row % 2 == 0).astype(jnp.int32)
    for pack, last in ((for_even, below), (for_odd, 1 - below)):
        for t in range(wide // 128):
            at = PIECE * t
            pack[at : at + 8] = low_low_ref[t, 0:8]
            pack[at + 8 : at + 16] = low_low_ref[t, 56:64]
            pack[at + 16 : at + 24] = one_ref[t, 2:10]
            pack[at + 24 : at + 32] = one_ref[t, 22:30]
            pack[at + 32 : at + 42] = two_ref[t, 3:13]
            pack[at + 42 : at + 50] = low_high_ref[t, pl.ds(56 * last, 8)]
            pack[at + 50 : at + 58] = one_high_ref[t, pl.ds(2 + 20 * last, 8)]
        for j in range(9):
            pack[EDGES + 8 * j : EDGES + 8 * j + 8] = high_ref[j, pl.ds(56 * last, 8)]
    below = (row % 4 < 2).astype(jnp.int32)
    for pack, last in ((for_even_far, below), (for_odd_far, 1 - below)):
        for t in range(wide // 128):
            at = FAR_PIECE * t
            pack[at : at + 8] = low_low_ref[t, pl.ds(56 * last, 8)]
            pack[at + 8 : at + 16] = one_ref[t, pl.ds(2 + 20 * last, 8)]
            pack[at + 16 : at + 25] = two_ref[t, pl.ds(3 + last, 9)]


PIECE, EDGES, PACK = 58, 296, 368
FAR_PIECE, FAR_PACK = 25, 128


def plain_low(ref, t, tall):
    near = (lambda x: pltpu.roll(x, 1, 0)), (lambda x: pltpu.roll(x, tall - 1, 0))
    return forward_lift(ref[t, pl.ds(0, tall, stride=2)], ref[t, pl.ds(1, tall, stride=2)], near)[0]


def sides(flag, odd_ref, even_ref):
    def above(*at):
        return jnp.where(flag, odd_ref[at], even_ref[at])

    def under(*at):
        return jnp.where(flag, even_ref[at], odd_ref[at])

    return above, under


def halves_of(ref, t, tall):
    return ref[t, pl.ds(0, tall, stride=2)], ref[t, pl.ds(1, tall, stride=2)]


def lifted(ref, t, tall, begin, own):
    row, count = lax.axis_index("rows"), lax.axis_size("rows")
    starts, stops = [(begin, row == 0)], [(begin + own - 1, row == count - 1)]
    if begin >= own:
        starts.append((begin - own, row == 1))
        stops.append((begin + 2 * own - 1, row == count - 2))
    return forward_lift(*halves_of(ref, t, tall), neighbours(0, starts, stops))


def across(level, low, high):
    _, at_start, at_end = ends("cols")
    halves = lift_lanes(low, high, EDGE[level], 1024 >> level, at_start, at_end, inverse=True)
    return merge_pairs(*halves)


def split_lanes(level, band):
    _, at_start, at_end = ends("cols")
    wide = WIDE[level]
    pad = jnp.zeros((band.shape[0], 2 * wide - band.shape[1]), jnp.float32)
    halves = split_pairs(jnp.concatenate([band, pad], 1))
    return lift_lanes(*halves, EDGE[level], 1024 >> level, at_start, at_end)


def limited(limits, level, kind, coeffs):
    at = 3 * level + kind
    return soften(coeffs, limits[at : at + 1, :])


def near_kernel(
    limits, own_low, own_high, own_low_low, own_low_high, odd_ref, even_ref,
    hl0_ref, vh0_ref, hl1_ref, vh1_ref, hl2_ref, vh2_ref, next_ref,
    l_ref, h_ref, b_ref, x_ref, lh_ref, hh_ref,
):
    above, under = sides(lax.axis_index("rows") % 2 == 0, odd_ref, even_ref)
    for t in range(WIDE[1] // 128):
        at = PIECE * t
        s = slice(128 * t, 128 * t + 128)

        def part(offset, size=8, at=at):
            return slice(at + offset, at + offset + size)

        x_ref[0, 0:8], x_ref[0, 8:72], x_ref[0, 72:80] = above(part(8)), own_low_low[t], under(part(0))
        x_ref[1, 0:8], x_ref[1, 8:72], x_ref[1, 72:80] = above(part(42)), own_low_high[t], under(part(42))
        l_ref[t, 8:48] = lifted(x_ref, 0, 40, 4, 32)[0]
        l_ref[t, 2:10], l_ref[t, 46:54] = above(part(24)), under(part(16))
        h_ref[t, 8:48] = lifted(x_ref, 1, 40, 4, 32)[0]
        h_ref[t, 2:10], h_ref[t, 46:54] = above(part(50)), under(part(50))
        low, high = lifted(l_ref, t, 32, 6, 16)
        lh_ref[0:24, s] = limited(limits, 1, 1, high[2:26])
        b_ref[3:13, s], b_ref[13:35, s], b_ref[35:45, s] = above(part(32, 10)), low[3:25], under(part(32, 10))
        low, high = lifted(h_ref, t, 32, 6, 16)
        hl1_ref[:, s] = limited(limits, 1, 0, low[2:26])
        hh_ref[0:24, s] = limited(limits, 1, 2, high[2:26])
    vh1_ref[...] = across(1, lh_ref[0:24, :640], hh_ref[0:24, :640])[:, :1152]
    low, high = split_lanes(2, b_ref[...])
    spread(next_ref, slice(None), low)
    spread(h_ref, slice(0, 48), high)
    for t in range(WIDE[2] // 128):
        s = slice(128 * t, 128 * t + 128)
        high = lifted(next_ref, t, 24, 8, 8)[1]
        lh_ref[0:16, s] = limited(limits, 2, 1, high[4:20])
        low, high = lifted(h_ref, t, 24, 8, 8)
        hl2_ref[:, s] = limited(limits, 2, 0, low[4:20])
        hh_ref[0:16, s] = limited(limits, 2, 2, high[4:20])
    vh2_ref[...] = across(2, lh_ref[0:16, :384], hh_ref[0:16, :384])[:, :640]
    low, high = (
        jnp.concatenate(
            [
                jnp.concatenate([side(slice(PIECE * t + at, PIECE * t + at + 8)) for t in range(5)], 1)
                for side, at in sources
            ],
            0,
        )
        for sources in (((above, 8), (under, 0)), ((above, 42), (under, 42)))
    )
    lows = across(1, low, high)
    for j in range(9):
        x_ref[j, 0:8] = lows[0:8, 128 * j : 128 * j + 128]
        x_ref[j, 8:72] = own_low[j]
        x_ref[j, 72:80] = lows[8:16, 128 * j : 128 * j + 128]
        at = slice(EDGES + 8 * j, EDGES + 8 * j + 8)
        x_ref[j + 9, 0:8] = above(at)
        x_ref[j + 9, 8:72] = own_high[j]
        x_ref[j + 9, 72:80] = under(at)

    def lift(t, s):
        high = lifted(x_ref, t, 40, 4, 32)[1]
        lh_ref[:, s] = limited(limits, 0, 1, high)
        low, high = lifted(x_ref, t + 9, 40, 4, 32)
        hl0_ref[:, s] = limited(limits, 0, 0, low)
        hh_ref[:, s] = limited(limits, 0, 2, high)

    tiles(WIDE[0], lift)
    vh0_ref[...] = across(0, lh_ref[...], hh_ref[...])[:, 128 : 128 + COLS]


def far_kernel(
    limits, hl0_ref, vh0_ref, hl1_ref, vh1_ref, hl2_ref, vh2_ref, next_ref,
    odd_ref, even_ref, odd_far, even_far, out_ref, f_ref, g_ref, l_ref, h_ref, b_ref, v_ref, r_ref, o_ref,
):
    row, count = lax.axis_index("rows"), lax.axis_size("rows")
    above, under = sides(row % 2 == 0, odd_ref, even_ref)
    above_far, under_far = sides(row % 4 < 2, odd_far, even_far)
    for t in range(WIDE[1] // 128):
        s = slice(128 * t, 128 * t + 128)

        def part(offset, at=PIECE * t):
            return slice(at + offset, at + offset + 8)

        def far_part(offset, size=8, at=FAR_PIECE * t):
            return slice(at + offset, at + offset + size)

        f_ref[t, 0:8], f_ref[t, 8:16] = above_far(far_part(0)), above(part(0))
        f_ref[t, 16:24], f_ref[t, 24:32] = under(part(8)), under_far(far_part(0))
        near = neighbours(0, [(4, row == 1)], [(11, row == count - 2)])
        one = forward_lift(*halves_of(f_ref, t, 16), near)[0]
        g_ref[t, 10:14], g_ref[t, 42:46] = one[2:6], one[10:14]
        g_ref[t, 2:10], g_ref[t, 14:22] = above_far(far_part(8)), above(part(16))
        g_ref[t, 34:42], g_ref[t, 46:54] = under(part(24)), under_far(far_part(8))
        near = neighbours(0, [(6, row == 1)], [(21, row == count - 2)])
        two = forward_lift(*halves_of(g_ref, t, 32), near)[0]
        b_ref[0:9, s], b_ref[9:15, s] = above_far(far_part(16, 9)), two[3:9]
        b_ref[16:22, s], b_ref[22:31, s] = two[19:25], under_far(far_part(16, 9))
    low = split_lanes(2, b_ref[0:32, :640])[0]
    for t in range(WIDE[2] // 128):
        s = slice(128 * t, 128 * t + 128)
        l_ref[t, 0:15], l_ref[t, 15:57], l_ref[t, 57:72] = low[0:15, s], next_ref[t, 3:45], low[16:31, s]
        b_ref[0:32, s] = lifted(l_ref, t, 40, 14, 8)[0][2:34]
    low, high = split_lanes(3, b_ref[0:32, :384])
    spread(l_ref, slice(0, 32), low)
    spread(h_ref, slice(0, 32), high)
    for t in range(WIDE[3] // 128):
        s = slice(128 * t, 128 * t + 128)
        low, high = lifted(l_ref, t, 16, 6, 4)
        v_ref[0:12, s] = low[2:14]
        v_ref[16:28, s] = limited(limits, 3, 1, high[2:14])
        low, high = lifted(h_ref, t, 16, 6, 4)
        r_ref[0:12, s] = limited(limits, 3, 0, low[2:14])
        r_ref[16:28, s] = limited(limits, 3, 2, high[2:14])
    both = across(3, v_ref[0:32, :256], r_ref[0:32, :256])[:, :384]
    low, high = both[0:16], both[16:32]
    _, at_start, at_end = ends("rows")
    for level in (3, 2, 1):
        own = OWN[level]
        long = max(own + 8, 16)
        near = neighbours(0, [(4, at_start)], [(3 + own, at_end)])
        for t in range(low.shape[1] // 128):
            s = slice(128 * t, 128 * t + 128)
            even, odd = inverse_lift(low[0:long, s], high[0:long, s], near)
            o_ref[t, pl.ds(0, long, stride=2)] = even
            o_ref[t, pl.ds(1, long, stride=2)] = odd
        size = OWN[level - 1] + 8
        low = joined(o_ref, slice(4, 4 + size), low.shape[1])
        hl, high = ((hl0_ref, vh0_ref), (hl1_ref, vh1_ref), (hl2_ref, vh2_ref))[level - 1]
        low = across(level - 1, low, hl[...])
        low = low[:, 128 : 128 + COLS] if level == 1 else low[:, : high.shape[1]]
    v_ref[...] = low
    near = neighbours(0, [(4, at_start)], [(35, at_end)])

    def finish(i, carry):
        for t in (2 * i, 2 * i + 1):
            s = pl.ds(pl.multiple_of(128 * t, 128), 128)
            even, odd = inverse_lift(v_ref[:, s], vh0_ref[:, s], near)
            o_ref[t, pl.ds(0, 40, stride=2)] = even
            o_ref[t, pl.ds(1, 40, stride=2)] = odd
            out_ref[:, s] = o_ref[t, 8:72]
        return carry

    lax.fori_loop(0, COLS // 256, finish, 0)


def swaps(axis, offset, apart):
    count = lax.axis_size(axis)
    pairs = []
    for block in range(offset, count, 2 * apart):
        for i in range(block, min(block + apart, count - apart)):
            pairs += [(i, i + apart), (i + apart, i)]
    return pairs


def exchange(for_even, for_odd, axis, apart=1):
    even = lax.ppermute(for_even, axis, swaps(axis, 0, apart))
    odd = lax.ppermute(for_odd, axis, swaps(axis, apart, apart))
    return odd, even


def f32(*shape):
    return jax.ShapeDtypeStruct(shape, jnp.float32)


def scratch(*shape):
    return pltpu.VMEM(shape, jnp.float32)


def call(kernel, outs, scratches, *args, scalars=0, space=pltpu.VMEM, cost=None):
    vmem = pl.BlockSpec(memory_space=pltpu.VMEM)
    smem = pl.BlockSpec(memory_space=pltpu.SMEM)
    return pl.pallas_call(
        kernel,
        out_shape=outs,
        in_specs=[smem] * scalars + [pl.BlockSpec(memory_space=space)] * (len(args) - scalars),
        out_specs=jax.tree.map(lambda _: vmem, outs),
        scratch_shapes=scratches,
        compiler_params=pltpu.CompilerParams(vmem_limit_bytes=16 * 2**20),
        cost_estimate=cost,
    )(*args)


def local(micrograph, thresholds):
    for_even, for_odd = call(
        edges_kernel,
        (f32(ROWS, 128), f32(ROWS, 128)),
        [pltpu.SemaphoreType.DMA((2,))],
        micrograph,
        space=pltpu.HBM,
    )
    odd, even = exchange(for_even, for_odd, "cols")
    *inner, limits = call(
        inner_kernel,
        (f32(ROWS, 896), f32(ROWS, 896), f32(ROWS, 256), f32(16, 128)),
        [],
        thresholds,
        micrograph,
        scalars=1,
        cost=pl.CostEstimate(flops=2 * 10**9, bytes_accessed=4 * 10**6, transcendentals=0),
    )
    for_even, for_odd, for_even_far, for_odd_far, *own = call(
        columns_kernel,
        (f32(PACK, 128), f32(PACK, 128), f32(FAR_PACK, 128), f32(FAR_PACK, 128))
        + (f32(9, ROWS, 128), f32(9, ROWS, 128), f32(5, ROWS, 128), f32(5, ROWS, 128)),
        [scratch(5, 32, 128), scratch(5, 16, 128), scratch(5, 32, 128)],
        *inner,
        odd,
        even,
    )
    near = exchange(for_even, for_odd, "rows")
    far = exchange(for_even_far, for_odd_far, "rows", 2)
    known = call(
        near_kernel,
        (f32(40, 1152), f32(40, COLS), f32(24, 640), f32(24, 1152), f32(16, 384), f32(16, 640), f32(3, 48, 128)),
        [scratch(5, 64, 128), scratch(5, 64, 128), scratch(48, 640), scratch(18, 80, 128)]
        + [scratch(40, 1152), scratch(40, 1152)],
        limits,
        *own,
        *near,
        cost=pl.CostEstimate(flops=2 * 10**9, bytes_accessed=4 * 10**6, transcendentals=0),
    )
    return call(
        far_kernel,
        f32(ROWS, COLS),
        [scratch(5, 32, 128), scratch(5, 64, 128), scratch(3, 80, 128), scratch(3, 80, 128)]
        + [scratch(32, 640), scratch(40, COLS), scratch(32, 256), scratch(16, 80, 128)],
        limits,
        *known,
        *near,
        *far,
    )


def solution(mesh):
    placed = (P("rows", "cols"), P())
    return jax.shard_map(
        local, mesh=mesh, in_specs=placed, out_specs=P("rows", "cols"), check_vma=False
    )
```

```python
import functools

import jax
import jax.numpy as jnp
from jax import lax
from jax.experimental import pallas as pl
from jax.experimental.pallas import tpu as pltpu
from jax.sharding import PartitionSpec as P

LEVELS = 4

step_one = -1.586134342
step_two = -0.05298011854
step_three = 0.8829110762
step_four = 0.4435068522
band_gain = 1.149604398
inv_gain = 1.0 / band_gain

ROWS, COLS = 64, 2048
WIDE = (1152, 640, 384, 256)
EDGE = (64, 32, 16, 8)
OWN = (32, 16, 8, 4)


STEPS_FROM = 1152
GROUP = 64
MATRIX_FROM = 640


def combined(*terms):
    total = {}
    for factor, taps, moved in terms:
        for (sequence, offset), tap in taps.items():
            key = (sequence, offset + moved)
            total[key] = total.get(key, 0.0) + factor * tap
    return total


def lifted_taps(inverse):
    even, odd = {("even", 0): 1.0}, {("odd", 0): 1.0}
    if inverse:
        even, odd = combined((1.0 / band_gain, even, 0)), combined((band_gain, odd, 0))
        for to_even, to_odd in ((step_four, step_three), (step_two, step_one)):
            even = combined((1.0, even, 0), (-to_even, odd, 0), (-to_even, odd, -1))
            odd = combined((1.0, odd, 0), (-to_odd, even, 0), (-to_odd, even, 1))
        return even, odd
    for to_odd, to_even in ((step_one, step_two), (step_three, step_four)):
        odd = combined((1.0, odd, 0), (to_odd, even, 0), (to_odd, even, 1))
        even = combined((1.0, even, 0), (to_even, odd, 0), (to_even, odd, -1))
    return combined((band_gain, even, 0)), combined((1.0 / band_gain, odd, 0))


def lift_lanes(even, odd, first, count, at_start, at_end, inverse=False):
    rows, width = even.shape
    if width >= STEPS_FROM:
        near = neighbours(1, [(first, at_start)], [(first + count - 1, at_end)])
        lift = inverse_lift if inverse else forward_lift
        groups = [slice(k, min(k + GROUP, rows)) for k in range(0, rows, GROUP)]
        parts = [lift(even[g], odd[g], near) for g in groups]
        return [jnp.concatenate(x, 0) if len(x) > 1 else x[0] for x in zip(*parts)]
    last = first + count - 1
    e, o = {0: even}, {0: odd}
    for x in (e, o):
        width = x[0].shape[1]
        for offset in (-2, -1, 1, 2):
            x[offset] = pltpu.roll(x[0], -offset % width, 1)
    fixed = lambda x, source, lane, flag: patch(x, source, 1, lane, flag)
    ends_of = {
        ("even", -1): [(e[1], first, at_start)],
        ("even", -2): [(e[2], first, at_start), (e[0], first + 1, at_start)],
        ("even", 1): [(e[0], last, at_end)],
        ("even", 2): [(e[-1], last, at_end), (e[1], last - 1, at_end)],
        ("odd", -1): [(o[0], first, at_start)],
        ("odd", -2): [(o[1], first, at_start), (o[-1], first + 1, at_start)],
        ("odd", 1): [(o[-1], last, at_end)],
        ("odd", 2): [(o[-2], last, at_end), (o[0], last - 1, at_end)],
    }
    shifted = {("even", 0): even, ("odd", 0): odd}
    for (sequence, offset), patches in ends_of.items():
        x = (e if sequence == "even" else o)[offset]
        for patch_of in patches:
            x = fixed(x, *patch_of)
        shifted[sequence, offset] = x
    out = []
    for taps in lifted_taps(inverse):
        by_tap = {}
        for key, tap in sorted(taps.items()):
            by_tap.setdefault(round(tap, 9), []).append((tap, shifted[key]))
        total = None
        for group in by_tap.values():
            term = sum((x for _, x in group[1:]), group[0][1]) * group[0][0]
            total = term if total is None else total + term
        out.append(total)
    return out


def soften(coeffs, limit):
    return coeffs - jnp.minimum(jnp.maximum(coeffs, -limit), limit)


def patch(shifted, source, axis, index, flag):
    unit = 8 if axis == 0 else 128
    lo = index // unit * unit
    hi = min(lo + unit, shifted.shape[axis])
    cut = functools.partial(lax.slice_in_dim, axis=axis)
    tile = cut(shifted, lo, hi)
    here = (lax.broadcasted_iota(jnp.int32, tile.shape, axis) == index - lo) & flag
    tile = jnp.where(here, cut(source, lo, hi), tile)
    parts = [cut(shifted, 0, lo)] if lo else []
    parts.append(tile)
    if hi < shifted.shape[axis]:
        parts.append(cut(shifted, hi, shifted.shape[axis]))
    return jnp.concatenate(parts, axis) if len(parts) > 1 else tile


def neighbours(axis, starts, stops):
    def before(odd):
        rolled = pltpu.roll(odd, 1, axis)
        for index, flag in starts:
            rolled = patch(rolled, odd, axis, index, flag)
        return rolled

    def after(even):
        rolled = pltpu.roll(even, even.shape[axis] - 1, axis)
        for index, flag in stops:
            rolled = patch(rolled, even, axis, index, flag)
        return rolled

    return before, after


def forward_lift(even, odd, near):
    before, after = near
    odd = odd + step_one * (even + after(even))
    even = even + step_two * (before(odd) + odd)
    odd = odd + step_three * (even + after(even))
    even = even + step_four * (before(odd) + odd)
    return even * band_gain, odd * inv_gain


def inverse_lift(low, high, near):
    before, after = near
    even = low * inv_gain
    odd = high * band_gain
    even = even - step_four * (before(odd) + odd)
    odd = odd - step_three * (even + after(even))
    even = even - step_two * (before(odd) + odd)
    odd = odd - step_one * (even + after(even))
    return even, odd


def pairing(transpose):
    a = lax.broadcasted_iota(jnp.int32, (256, 256), 1 if not transpose else 0)
    b = lax.broadcasted_iota(jnp.int32, (256, 256), 0 if not transpose else 1)
    target = jnp.where(a < 128, 2 * a, 2 * a - 255)
    return jnp.where(b == target, 1.0, 0.0).astype(jnp.bfloat16)


def permuted(x, matrix):
    rows = x.shape[0]
    high = x.astype(jnp.bfloat16).astype(jnp.float32)
    rest = x - high
    middle = rest.astype(jnp.bfloat16).astype(jnp.float32)
    pieces = [high, middle, rest - middle]
    if rows % 16:
        pieces.append(jnp.zeros((-3 * rows % 16, x.shape[1]), jnp.float32))
        pieces = [jnp.concatenate(pieces, 0).astype(jnp.bfloat16)]
    else:
        pieces = [jnp.concatenate([piece.astype(jnp.bfloat16) for piece in pieces], 0)]
    out = jnp.dot(pieces[0], matrix, preferred_element_type=jnp.float32)
    return (out[:rows] + out[rows : 2 * rows]) + out[2 * rows : 3 * rows]


def picked(x, index):
    return jnp.take_along_axis(x, index, axis=1, mode="promise_in_bounds")


def split_pairs(x):
    if x.shape[1] < 2 * MATRIX_FROM:
        return split_by_picks(x)
    matrix = pairing(False)
    both = [permuted(x[:, k : k + 256], matrix) for k in range(0, x.shape[1], 256)]
    return jnp.concatenate([y[:, :128] for y in both], 1), jnp.concatenate([y[:, 128:] for y in both], 1)


def merge_pairs(even, odd):
    if even.shape[1] < MATRIX_FROM:
        return merge_by_picks(even, odd)
    matrix = pairing(True)
    return jnp.concatenate(
        [
            permuted(jnp.concatenate([even[:, k : k + 128], odd[:, k : k + 128]], 1), matrix)
            for k in range(0, even.shape[1], 128)
        ],
        1,
    )


def split_by_picks(x):
    rows = x.shape[0]
    lane = lax.broadcasted_iota(jnp.int32, (rows, 128), 1)
    lower = lane < 64
    near = jnp.where(lower, 2 * lane, 2 * lane - 127)
    far = jnp.where(lower, 2 * lane + 1, 2 * lane - 128)
    evens, odds = [], []
    for k in range(0, x.shape[1], 256):
        first, second = picked(x[:, k : k + 128], near), picked(x[:, k + 128 : k + 256], far)
        evens.append(jnp.where(lower, first, second))
        odds.append(pltpu.roll(jnp.where(lower, second, first), 64, 1))
    return jnp.concatenate(evens, 1), jnp.concatenate(odds, 1)


def merge_by_picks(even, odd):
    rows = even.shape[0]
    lane = lax.broadcasted_iota(jnp.int32, (rows, 128), 1)
    lower = lane < 64
    is_odd = lane % 2 == 1
    half = lane // 2
    near = jnp.where(is_odd, half + 64, half)
    far = jnp.where(is_odd, half, half + 64)
    out = []
    for k in range(0, even.shape[1], 128):
        e, o = even[:, k : k + 128], pltpu.roll(odd[:, k : k + 128], 64, 1)
        out += [picked(jnp.where(lower, e, o), near), picked(jnp.where(lower, o, e), far)]
    return jnp.concatenate(out, 1)


def tiles(width, body):
    def step(t, carry):
        body(t, pl.ds(pl.multiple_of(t * 128, 128), 128))
        return carry

    if width > 640:
        lax.fori_loop(0, width // 128, step, 0)
    else:
        for t in range(width // 128):
            body(t, slice(128 * t, 128 * t + 128))


def joined(ref, rows, width):
    return jnp.concatenate([ref[k, rows] for k in range(width // 128)], 1)


def spread(ref, rows, value):
    for k in range(value.shape[1] // 128):
        ref[k, rows] = value[:, 128 * k : 128 * k + 128]


def ends(axis):
    position = lax.axis_index(axis)
    return position % 2 == 0, position == 0, position == lax.axis_size(axis) - 1


def edges_kernel(x_ref, for_even, for_odd, sems):
    is_even = ends("cols")[0]
    right = jnp.where(is_even, COLS - 128, 0)
    copies = []
    for k, (at, out) in enumerate(((right, for_even), (COLS - 128 - right, for_odd))):
        lanes = pl.ds(pl.multiple_of(at, 128), 128)
        copies.append(pltpu.make_async_copy(x_ref.at[:, lanes], out, sems.at[k]))
        copies[-1].start()
    for copy in copies:
        copy.wait()


def inner_kernel(t_ref, x_ref, e_ref, o_ref, edge_ref, limit_ref):
    for level in range(LEVELS):
        for kind in range(3):
            limit_ref[3 * level + kind : 3 * level + kind + 1, :] = jnp.full((1, 128), t_ref[level, kind])
    e_ref[...], o_ref[...] = split_pairs(x_ref[:, 128 : COLS - 128])
    edge_ref[:, :128] = x_ref[:, :128]
    edge_ref[:, 128:] = x_ref[:, COLS - 128 :]


def columns_kernel(
    e_ref, o_ref, edge_ref, odd_ref, even_ref, for_even, for_odd, for_even_far, for_odd_far,
    low_ref, high_ref, low_low_ref, low_high_ref, one_ref, two_ref, one_high_ref,
):
    is_even, at_start, at_end = ends("cols")
    left = jnp.where(is_even, odd_ref[...], even_ref[...])
    right = jnp.where(is_even, even_ref[...], odd_ref[...])
    first = split_pairs(jnp.concatenate([left, edge_ref[:, :128]], 1))
    last = split_pairs(jnp.concatenate([edge_ref[:, 128:], right], 1))
    low, high = lift_lanes(
        jnp.concatenate([first[0], e_ref[...], last[0]], 1),
        jnp.concatenate([first[1], o_ref[...], last[1]], 1),
        EDGE[0],
        1024,
        at_start,
        at_end,
    )
    spread(low_ref, slice(None), low)
    spread(high_ref, slice(None), high)
    wide = WIDE[1]
    low = jnp.concatenate([low, jnp.zeros((ROWS, 2 * wide - WIDE[0]), jnp.float32)], 1)
    low, high = lift_lanes(*split_pairs(low), EDGE[1], 512, at_start, at_end)
    spread(low_low_ref, slice(None), low)
    spread(low_high_ref, slice(None), high)
    for t in range(wide // 128):
        one_ref[t] = plain_low(low_low_ref, t, 32)
        two_ref[t] = plain_low(one_ref, t, 16)
        one_high_ref[t] = plain_low(low_high_ref, t, 32)
    row = lax.axis_index("rows")
    below = (row % 2 == 0).astype(jnp.int32)
    for pack, last in ((for_even, below), (for_odd, 1 - below)):
        for t in range(wide // 128):
            at = PIECE * t
            pack[at : at + 8] = low_low_ref[t, 0:8]
            pack[at + 8 : at + 16] = low_low_ref[t, 56:64]
            pack[at + 16 : at + 24] = one_ref[t, 2:10]
            pack[at + 24 : at + 32] = one_ref[t, 22:30]
            pack[at + 32 : at + 42] = two_ref[t, 3:13]
            pack[at + 42 : at + 50] = low_high_ref[t, pl.ds(56 * last, 8)]
            pack[at + 50 : at + 58] = one_high_ref[t, pl.ds(2 + 20 * last, 8)]
        for j in range(9):
            pack[EDGES + 8 * j : EDGES + 8 * j + 8] = high_ref[j, pl.ds(56 * last, 8)]
    below = (row % 4 < 2).astype(jnp.int32)
    for pack, last in ((for_even_far, below), (for_odd_far, 1 - below)):
        for t in range(wide // 128):
            at = FAR_PIECE * t
            pack[at : at + 8] = low_low_ref[t, pl.ds(56 * last, 8)]
            pack[at + 8 : at + 16] = one_ref[t, pl.ds(2 + 20 * last, 8)]
            pack[at + 16 : at + 25] = two_ref[t, pl.ds(3 + last, 9)]


PIECE, EDGES, PACK = 58, 296, 368
FAR_PIECE, FAR_PACK = 25, 128


def plain_low(ref, t, tall):
    near = (lambda x: pltpu.roll(x, 1, 0)), (lambda x: pltpu.roll(x, tall - 1, 0))
    return forward_lift(ref[t, pl.ds(0, tall, stride=2)], ref[t, pl.ds(1, tall, stride=2)], near)[0]


def sides(flag, odd_ref, even_ref):
    def above(*at):
        return jnp.where(flag, odd_ref[at], even_ref[at])

    def under(*at):
        return jnp.where(flag, even_ref[at], odd_ref[at])

    return above, under


def halves_of(ref, t, tall):
    return ref[t, pl.ds(0, tall, stride=2)], ref[t, pl.ds(1, tall, stride=2)]


def lifted(ref, t, tall, begin, own):
    row, count = lax.axis_index("rows"), lax.axis_size("rows")
    starts, stops = [(begin, row == 0)], [(begin + own - 1, row == count - 1)]
    if begin >= own:
        starts.append((begin - own, row == 1))
        stops.append((begin + 2 * own - 1, row == count - 2))
    return forward_lift(*halves_of(ref, t, tall), neighbours(0, starts, stops))


def across(level, low, high):
    _, at_start, at_end = ends("cols")
    halves = lift_lanes(low, high, EDGE[level], 1024 >> level, at_start, at_end, inverse=True)
    return merge_pairs(*halves)


def split_lanes(level, band):
    _, at_start, at_end = ends("cols")
    wide = WIDE[level]
    pad = jnp.zeros((band.shape[0], 2 * wide - band.shape[1]), jnp.float32)
    halves = split_pairs(jnp.concatenate([band, pad], 1))
    return lift_lanes(*halves, EDGE[level], 1024 >> level, at_start, at_end)


def limited(limits, level, kind, coeffs):
    at = 3 * level + kind
    return soften(coeffs, limits[at : at + 1, :])


def near_kernel(
    limits, own_low, own_high, own_low_low, own_low_high, odd_ref, even_ref,
    hl0_ref, vh0_ref, hl1_ref, vh1_ref, hl2_ref, vh2_ref, next_ref,
    l_ref, h_ref, b_ref, x_ref, lh_ref, hh_ref,
):
    above, under = sides(lax.axis_index("rows") % 2 == 0, odd_ref, even_ref)
    for t in range(WIDE[1] // 128):
        at = PIECE * t
        s = slice(128 * t, 128 * t + 128)

        def part(offset, size=8, at=at):
            return slice(at + offset, at + offset + size)

        x_ref[0, 0:8], x_ref[0, 8:72], x_ref[0, 72:80] = above(part(8)), own_low_low[t], under(part(0))
        x_ref[1, 0:8], x_ref[1, 8:72], x_ref[1, 72:80] = above(part(42)), own_low_high[t], under(part(42))
        l_ref[t, 8:48] = lifted(x_ref, 0, 40, 4, 32)[0]
        l_ref[t, 2:10], l_ref[t, 46:54] = above(part(24)), under(part(16))
        h_ref[t, 8:48] = lifted(x_ref, 1, 40, 4, 32)[0]
        h_ref[t, 2:10], h_ref[t, 46:54] = above(part(50)), under(part(50))
        low, high = lifted(l_ref, t, 32, 6, 16)
        lh_ref[0:24, s] = limited(limits, 1, 1, high[2:26])
        b_ref[3:13, s], b_ref[13:35, s], b_ref[35:45, s] = above(part(32, 10)), low[3:25], under(part(32, 10))
        low, high = lifted(h_ref, t, 32, 6, 16)
        hl1_ref[:, s] = limited(limits, 1, 0, low[2:26])
        hh_ref[0:24, s] = limited(limits, 1, 2, high[2:26])
    vh1_ref[...] = across(1, lh_ref[0:24, :640], hh_ref[0:24, :640])[:, :1152]
    low, high = split_lanes(2, b_ref[...])
    spread(next_ref, slice(None), low)
    spread(h_ref, slice(0, 48), high)
    for t in range(WIDE[2] // 128):
        s = slice(128 * t, 128 * t + 128)
        high = lifted(next_ref, t, 24, 8, 8)[1]
        lh_ref[0:16, s] = limited(limits, 2, 1, high[4:20])
        low, high = lifted(h_ref, t, 24, 8, 8)
        hl2_ref[:, s] = limited(limits, 2, 0, low[4:20])
        hh_ref[0:16, s] = limited(limits, 2, 2, high[4:20])
    vh2_ref[...] = across(2, lh_ref[0:16, :384], hh_ref[0:16, :384])[:, :640]
    low, high = (
        jnp.concatenate(
            [
                jnp.concatenate([side(slice(PIECE * t + at, PIECE * t + at + 8)) for t in range(5)], 1)
                for side, at in sources
            ],
            0,
        )
        for sources in (((above, 8), (under, 0)), ((above, 42), (under, 42)))
    )
    lows = across(1, low, high)
    for j in range(9):
        x_ref[j, 0:8] = lows[0:8, 128 * j : 128 * j + 128]
        x_ref[j, 8:72] = own_low[j]
        x_ref[j, 72:80] = lows[8:16, 128 * j : 128 * j + 128]
        at = slice(EDGES + 8 * j, EDGES + 8 * j + 8)
        x_ref[j + 9, 0:8] = above(at)
        x_ref[j + 9, 8:72] = own_high[j]
        x_ref[j + 9, 72:80] = under(at)

    def lift(t, s):
        high = lifted(x_ref, t, 40, 4, 32)[1]
        lh_ref[:, s] = limited(limits, 0, 1, high)
        low, high = lifted(x_ref, t + 9, 40, 4, 32)
        hl0_ref[:, s] = limited(limits, 0, 0, low)
        hh_ref[:, s] = limited(limits, 0, 2, high)

    tiles(WIDE[0], lift)
    vh0_ref[...] = across(0, lh_ref[...], hh_ref[...])[:, 128 : 128 + COLS]


def far_kernel(
    limits, hl0_ref, vh0_ref, hl1_ref, vh1_ref, hl2_ref, vh2_ref, next_ref,
    odd_ref, even_ref, even_far, odd_far, out_ref, f_ref, g_ref, l_ref, h_ref, b_ref, v_ref, r_ref, o_ref, sems,
):
    row, count = lax.axis_index("rows"), lax.axis_size("rows")
    above, under = sides(row % 2 == 0, odd_ref, even_ref)
    above_far, under_far = sides(row % 4 < 2, odd_far, even_far)
    for t in range(WIDE[1] // 128):
        s = slice(128 * t, 128 * t + 128)

        def part(offset, at=PIECE * t):
            return slice(at + offset, at + offset + 8)

        def far_part(offset, size=8, at=FAR_PIECE * t):
            return slice(at + offset, at + offset + size)

        f_ref[t, 0:8], f_ref[t, 8:16] = above_far(far_part(0)), above(part(0))
        f_ref[t, 16:24], f_ref[t, 24:32] = under(part(8)), under_far(far_part(0))
        near = neighbours(0, [(4, row == 1)], [(11, row == count - 2)])
        one = forward_lift(*halves_of(f_ref, t, 16), near)[0]
        g_ref[t, 10:14], g_ref[t, 42:46] = one[2:6], one[10:14]
        g_ref[t, 2:10], g_ref[t, 14:22] = above_far(far_part(8)), above(part(16))
        g_ref[t, 34:42], g_ref[t, 46:54] = under(part(24)), under_far(far_part(8))
        near = neighbours(0, [(6, row == 1)], [(21, row == count - 2)])
        two = forward_lift(*halves_of(g_ref, t, 32), near)[0]
        b_ref[0:9, s], b_ref[9:15, s] = above_far(far_part(16, 9)), two[3:9]
        b_ref[16:22, s], b_ref[22:31, s] = two[19:25], under_far(far_part(16, 9))
    low = split_lanes(2, b_ref[0:32, :640])[0]
    for t in range(WIDE[2] // 128):
        s = slice(128 * t, 128 * t + 128)
        l_ref[t, 0:15], l_ref[t, 15:57], l_ref[t, 57:72] = low[0:15, s], next_ref[t, 3:45], low[16:31, s]
        b_ref[0:32, s] = lifted(l_ref, t, 40, 14, 8)[0][2:34]
    low, high = split_lanes(3, b_ref[0:32, :384])
    spread(l_ref, slice(0, 32), low)
    spread(h_ref, slice(0, 32), high)
    for t in range(WIDE[3] // 128):
        s = slice(128 * t, 128 * t + 128)
        low, high = lifted(l_ref, t, 16, 6, 4)
        v_ref[0:12, s] = low[2:14]
        v_ref[16:28, s] = limited(limits, 3, 1, high[2:14])
        low, high = lifted(h_ref, t, 16, 6, 4)
        r_ref[0:12, s] = limited(limits, 3, 0, low[2:14])
        r_ref[16:28, s] = limited(limits, 3, 2, high[2:14])
    both = across(3, v_ref[0:32, :256], r_ref[0:32, :256])[:, :384]
    low, high = both[0:16], both[16:32]
    _, at_start, at_end = ends("rows")
    for level in (3, 2, 1):
        own = OWN[level]
        long = max(own + 8, 16)
        near = neighbours(0, [(4, at_start)], [(3 + own, at_end)])
        for t in range(low.shape[1] // 128):
            s = slice(128 * t, 128 * t + 128)
            even, odd = inverse_lift(low[0:long, s], high[0:long, s], near)
            o_ref[t, pl.ds(0, long, stride=2)] = even
            o_ref[t, pl.ds(1, long, stride=2)] = odd
        size = OWN[level - 1] + 8
        low = joined(o_ref, slice(4, 4 + size), low.shape[1])
        hl, high = ((hl0_ref, vh0_ref), (hl1_ref, vh1_ref), (hl2_ref, vh2_ref))[level - 1]
        low = across(level - 1, low, hl[...])
        low = low[:, 128 : 128 + COLS] if level == 1 else low[:, : high.shape[1]]
    v_ref[...] = low
    near = neighbours(0, [(4, at_start)], [(35, at_end)])

    def finish(i, carry):
        for t in (2 * i, 2 * i + 1):
            s = pl.ds(pl.multiple_of(128 * t, 128), 128)
            even, odd = inverse_lift(v_ref[:, s], vh0_ref[:, s], near)
            o_ref[t, pl.ds(0, 40, stride=2)] = even
            o_ref[t, pl.ds(1, 40, stride=2)] = odd
            pltpu.make_async_copy(o_ref.at[t, 8:72], out_ref.at[:, s], sems.at[t]).start()
        return carry

    lax.fori_loop(0, COLS // 256, finish, 0)
    for t in range(COLS // 128):
        lanes = slice(128 * t, 128 * t + 128)
        pltpu.make_async_copy(o_ref.at[t, 8:72], out_ref.at[:, lanes], sems.at[t]).wait()


def swaps(axis, offset, apart):
    count = lax.axis_size(axis)
    pairs = []
    for block in range(offset, count, 2 * apart):
        for i in range(block, min(block + apart, count - apart)):
            pairs += [(i, i + apart), (i + apart, i)]
    return pairs


def exchange(for_even, for_odd, axis, apart=1):
    even = lax.ppermute(for_even, axis, swaps(axis, 0, apart))
    odd = lax.ppermute(for_odd, axis, swaps(axis, apart, apart))
    return odd, even


def f32(*shape):
    return jax.ShapeDtypeStruct(shape, jnp.float32)


def scratch(*shape):
    return pltpu.VMEM(shape, jnp.float32)


def call(kernel, outs, scratches, *args, scalars=0, space=pltpu.VMEM, out_space=pltpu.VMEM, cost=None):
    vmem = pl.BlockSpec(memory_space=pltpu.VMEM)
    smem = pl.BlockSpec(memory_space=pltpu.SMEM)
    return pl.pallas_call(
        kernel,
        out_shape=outs,
        in_specs=[smem] * scalars + [pl.BlockSpec(memory_space=space)] * (len(args) - scalars),
        out_specs=jax.tree.map(lambda _: pl.BlockSpec(memory_space=out_space), outs),
        scratch_shapes=scratches,
        compiler_params=pltpu.CompilerParams(vmem_limit_bytes=16 * 2**20),
        cost_estimate=cost,
    )(*args)


def local(micrograph, thresholds):
    for_even, for_odd = call(
        edges_kernel,
        (f32(ROWS, 128), f32(ROWS, 128)),
        [pltpu.SemaphoreType.DMA((2,))],
        micrograph,
        space=pltpu.HBM,
    )
    odd, even = exchange(for_even, for_odd, "cols")
    *inner, limits = call(
        inner_kernel,
        (f32(ROWS, 896), f32(ROWS, 896), f32(ROWS, 256), f32(16, 128)),
        [],
        thresholds,
        micrograph,
        scalars=1,
        cost=pl.CostEstimate(flops=2 * 10**9, bytes_accessed=4 * 10**6, transcendentals=0),
    )
    for_even, for_odd, for_even_far, for_odd_far, *own = call(
        columns_kernel,
        (f32(PACK, 128), f32(PACK, 128), f32(FAR_PACK, 128), f32(FAR_PACK, 128))
        + (f32(9, ROWS, 128), f32(9, ROWS, 128), f32(5, ROWS, 128), f32(5, ROWS, 128)),
        [scratch(5, 32, 128), scratch(5, 16, 128), scratch(5, 32, 128)],
        *inner,
        odd,
        even,
    )
    near = exchange(for_even, for_odd, "rows")
    far = exchange(for_even_far, for_odd_far, "rows", 2)
    known = call(
        near_kernel,
        (f32(40, 1152), f32(40, COLS), f32(24, 640), f32(24, 1152), f32(16, 384), f32(16, 640), f32(3, 48, 128)),
        [scratch(5, 64, 128), scratch(5, 64, 128), scratch(48, 640), scratch(18, 80, 128)]
        + [scratch(40, 1152), scratch(40, 1152)],
        limits,
        *own,
        *near,
        cost=pl.CostEstimate(flops=2 * 10**9, bytes_accessed=4 * 10**6, transcendentals=0),
    )
    return call(
        far_kernel,
        f32(ROWS, COLS),
        [scratch(5, 32, 128), scratch(5, 64, 128), scratch(3, 80, 128), scratch(3, 80, 128)]
        + [scratch(32, 640), scratch(40, COLS), scratch(32, 256), scratch(16, 80, 128)]
        + [pltpu.SemaphoreType.DMA((16,))],
        limits,
        *known,
        *near,
        far[1],
        far[0],
        out_space=pl.ANY,
    )


def solution(mesh):
    placed = (P("rows", "cols"), P())
    return jax.shard_map(
        local, mesh=mesh, in_specs=placed, out_specs=P("rows", "cols"), check_vma=False
    )
```

```python
import functools

import jax
import jax.numpy as jnp
from jax import lax
from jax.experimental import pallas as pl
from jax.experimental.pallas import tpu as pltpu
from jax.sharding import PartitionSpec as P

LEVELS = 4

step_one = -1.586134342
step_two = -0.05298011854
step_three = 0.8829110762
step_four = 0.4435068522
band_gain = 1.149604398
inv_gain = 1.0 / band_gain

ROWS, COLS = 64, 2048
WIDE = (1152, 640, 384, 256)
EDGE = (64, 32, 16, 8)
OWN = (32, 16, 8, 4)


STEPS_FROM = 1152
GROUP = 64
MATRIX_FROM = 640


def combined(*terms):
    total = {}
    for factor, taps, moved in terms:
        for (sequence, offset), tap in taps.items():
            key = (sequence, offset + moved)
            total[key] = total.get(key, 0.0) + factor * tap
    return total


def lifted_taps(inverse):
    even, odd = {("even", 0): 1.0}, {("odd", 0): 1.0}
    if inverse:
        even, odd = combined((1.0 / band_gain, even, 0)), combined((band_gain, odd, 0))
        for to_even, to_odd in ((step_four, step_three), (step_two, step_one)):
            even = combined((1.0, even, 0), (-to_even, odd, 0), (-to_even, odd, -1))
            odd = combined((1.0, odd, 0), (-to_odd, even, 0), (-to_odd, even, 1))
        return even, odd
    for to_odd, to_even in ((step_one, step_two), (step_three, step_four)):
        odd = combined((1.0, odd, 0), (to_odd, even, 0), (to_odd, even, 1))
        even = combined((1.0, even, 0), (to_even, odd, 0), (to_even, odd, -1))
    return combined((band_gain, even, 0)), combined((1.0 / band_gain, odd, 0))


def lift_lanes(even, odd, first, count, at_start, at_end, inverse=False):
    rows, width = even.shape
    if width >= STEPS_FROM:
        near = neighbours(1, [(first, at_start)], [(first + count - 1, at_end)])
        lift = inverse_lift if inverse else forward_lift
        groups = [slice(k, min(k + GROUP, rows)) for k in range(0, rows, GROUP)]
        parts = [lift(even[g], odd[g], near) for g in groups]
        return [jnp.concatenate(x, 0) if len(x) > 1 else x[0] for x in zip(*parts)]
    last = first + count - 1
    e, o = {0: even}, {0: odd}
    for x in (e, o):
        width = x[0].shape[1]
        for offset in (-2, -1, 1, 2):
            x[offset] = pltpu.roll(x[0], -offset % width, 1)
    fixed = lambda x, source, lane, flag: patch(x, source, 1, lane, flag)
    ends_of = {
        ("even", -1): [(e[1], first, at_start)],
        ("even", -2): [(e[2], first, at_start), (e[0], first + 1, at_start)],
        ("even", 1): [(e[0], last, at_end)],
        ("even", 2): [(e[-1], last, at_end), (e[1], last - 1, at_end)],
        ("odd", -1): [(o[0], first, at_start)],
        ("odd", -2): [(o[1], first, at_start), (o[-1], first + 1, at_start)],
        ("odd", 1): [(o[-1], last, at_end)],
        ("odd", 2): [(o[-2], last, at_end), (o[0], last - 1, at_end)],
    }
    shifted = {("even", 0): even, ("odd", 0): odd}
    for (sequence, offset), patches in ends_of.items():
        x = (e if sequence == "even" else o)[offset]
        for patch_of in patches:
            x = fixed(x, *patch_of)
        shifted[sequence, offset] = x
    out = []
    for taps in lifted_taps(inverse):
        by_tap = {}
        for key, tap in sorted(taps.items()):
            by_tap.setdefault(round(tap, 9), []).append((tap, shifted[key]))
        total = None
        for group in by_tap.values():
            term = sum((x for _, x in group[1:]), group[0][1]) * group[0][0]
            total = term if total is None else total + term
        out.append(total)
    return out


def soften(coeffs, limit):
    return coeffs - jnp.minimum(jnp.maximum(coeffs, -limit), limit)


def patch(shifted, source, axis, index, flag):
    unit = 8 if axis == 0 else 128
    lo = index // unit * unit
    hi = min(lo + unit, shifted.shape[axis])
    cut = functools.partial(lax.slice_in_dim, axis=axis)
    tile = cut(shifted, lo, hi)
    here = (lax.broadcasted_iota(jnp.int32, tile.shape, axis) == index - lo) & flag
    tile = jnp.where(here, cut(source, lo, hi), tile)
    parts = [cut(shifted, 0, lo)] if lo else []
    parts.append(tile)
    if hi < shifted.shape[axis]:
        parts.append(cut(shifted, hi, shifted.shape[axis]))
    return jnp.concatenate(parts, axis) if len(parts) > 1 else tile


def neighbours(axis, starts, stops):
    def before(odd):
        rolled = pltpu.roll(odd, 1, axis)
        for index, flag in starts:
            rolled = patch(rolled, odd, axis, index, flag)
        return rolled

    def after(even):
        rolled = pltpu.roll(even, even.shape[axis] - 1, axis)
        for index, flag in stops:
            rolled = patch(rolled, even, axis, index, flag)
        return rolled

    return before, after


def forward_lift(even, odd, near):
    before, after = near
    odd = odd + step_one * (even + after(even))
    even = even + step_two * (before(odd) + odd)
    odd = odd + step_three * (even + after(even))
    even = even + step_four * (before(odd) + odd)
    return even * band_gain, odd * inv_gain


def inverse_lift(low, high, near):
    before, after = near
    even = low * inv_gain
    odd = high * band_gain
    even = even - step_four * (before(odd) + odd)
    odd = odd - step_three * (even + after(even))
    even = even - step_two * (before(odd) + odd)
    odd = odd - step_one * (even + after(even))
    return even, odd


def pairing(transpose):
    a = lax.broadcasted_iota(jnp.int32, (256, 256), 1 if not transpose else 0)
    b = lax.broadcasted_iota(jnp.int32, (256, 256), 0 if not transpose else 1)
    target = jnp.where(a < 128, 2 * a, 2 * a - 255)
    return jnp.where(b == target, 1.0, 0.0).astype(jnp.bfloat16)


def permuted(x, matrix):
    rows = x.shape[0]
    high = x.astype(jnp.bfloat16).astype(jnp.float32)
    rest = x - high
    middle = rest.astype(jnp.bfloat16).astype(jnp.float32)
    pieces = [high, middle, rest - middle]
    if rows % 16:
        pieces.append(jnp.zeros((-3 * rows % 16, x.shape[1]), jnp.float32))
        pieces = [jnp.concatenate(pieces, 0).astype(jnp.bfloat16)]
    else:
        pieces = [jnp.concatenate([piece.astype(jnp.bfloat16) for piece in pieces], 0)]
    out = jnp.dot(pieces[0], matrix, preferred_element_type=jnp.float32)
    return (out[:rows] + out[rows : 2 * rows]) + out[2 * rows : 3 * rows]


def picked(x, index):
    return jnp.take_along_axis(x, index, axis=1, mode="promise_in_bounds")


def split_pairs(x):
    if x.shape[1] < 2 * MATRIX_FROM:
        return split_by_picks(x)
    matrix = pairing(False)
    both = [permuted(x[:, k : k + 256], matrix) for k in range(0, x.shape[1], 256)]
    return jnp.concatenate([y[:, :128] for y in both], 1), jnp.concatenate([y[:, 128:] for y in both], 1)


def merge_pairs(even, odd):
    if even.shape[1] < MATRIX_FROM:
        return merge_by_picks(even, odd)
    matrix = pairing(True)
    return jnp.concatenate(
        [
            permuted(jnp.concatenate([even[:, k : k + 128], odd[:, k : k + 128]], 1), matrix)
            for k in range(0, even.shape[1], 128)
        ],
        1,
    )


def split_by_picks(x):
    rows = x.shape[0]
    lane = lax.broadcasted_iota(jnp.int32, (rows, 128), 1)
    lower = lane < 64
    near = jnp.where(lower, 2 * lane, 2 * lane - 127)
    far = jnp.where(lower, 2 * lane + 1, 2 * lane - 128)
    evens, odds = [], []
    for k in range(0, x.shape[1], 256):
        first, second = picked(x[:, k : k + 128], near), picked(x[:, k + 128 : k + 256], far)
        evens.append(jnp.where(lower, first, second))
        odds.append(pltpu.roll(jnp.where(lower, second, first), 64, 1))
    return jnp.concatenate(evens, 1), jnp.concatenate(odds, 1)


def merge_by_picks(even, odd):
    rows = even.shape[0]
    lane = lax.broadcasted_iota(jnp.int32, (rows, 128), 1)
    lower = lane < 64
    is_odd = lane % 2 == 1
    half = lane // 2
    near = jnp.where(is_odd, half + 64, half)
    far = jnp.where(is_odd, half, half + 64)
    out = []
    for k in range(0, even.shape[1], 128):
        e, o = even[:, k : k + 128], pltpu.roll(odd[:, k : k + 128], 64, 1)
        out += [picked(jnp.where(lower, e, o), near), picked(jnp.where(lower, o, e), far)]
    return jnp.concatenate(out, 1)


def tiles(width, body):
    def step(t, carry):
        body(t, pl.ds(pl.multiple_of(t * 128, 128), 128))
        return carry

    if width > 640:
        lax.fori_loop(0, width // 128, step, 0)
    else:
        for t in range(width // 128):
            body(t, slice(128 * t, 128 * t + 128))


def joined(ref, rows, width):
    return jnp.concatenate([ref[k, rows] for k in range(width // 128)], 1)


def spread(ref, rows, value):
    for k in range(value.shape[1] // 128):
        ref[k, rows] = value[:, 128 * k : 128 * k + 128]


def ends(axis):
    position = lax.axis_index(axis)
    return position % 2 == 0, position == 0, position == lax.axis_size(axis) - 1


def edges_kernel(x_ref, for_even, for_odd, sems):
    is_even = ends("cols")[0]
    right = jnp.where(is_even, COLS - 128, 0)
    copies = []
    for k, (at, out) in enumerate(((right, for_even), (COLS - 128 - right, for_odd))):
        lanes = pl.ds(pl.multiple_of(at, 128), 128)
        copies.append(pltpu.make_async_copy(x_ref.at[:, lanes], out, sems.at[k]))
        copies[-1].start()
    for copy in copies:
        copy.wait()


def inner_kernel(t_ref, x_ref, e_ref, o_ref, edge_ref, limit_ref):
    for level in range(LEVELS):
        for kind in range(3):
            limit_ref[3 * level + kind : 3 * level + kind + 1, :] = jnp.full((1, 128), t_ref[level, kind])
    e_ref[...], o_ref[...] = split_pairs(x_ref[:, 128 : COLS - 128])
    edge_ref[:, :128] = x_ref[:, :128]
    edge_ref[:, 128:] = x_ref[:, COLS - 128 :]


def columns_kernel(
    e_ref, o_ref, edge_ref, odd_ref, even_ref, for_even, for_odd, for_even_far, for_odd_far,
    low_ref, high_ref, low_low_ref, low_high_ref, one_ref, two_ref, one_high_ref,
    x_ref, y_ref,
):
    is_even, at_start, at_end = ends("cols")
    left = jnp.where(is_even, odd_ref[...], even_ref[...])
    right = jnp.where(is_even, even_ref[...], odd_ref[...])
    first = split_pairs(jnp.concatenate([left, edge_ref[:, :128]], 1))
    last = split_pairs(jnp.concatenate([edge_ref[:, 128:], right], 1))
    low, high = lift_lanes(
        jnp.concatenate([first[0], e_ref[...], last[0]], 1),
        jnp.concatenate([first[1], o_ref[...], last[1]], 1),
        EDGE[0],
        1024,
        at_start,
        at_end,
    )
    spread(low_ref, slice(None), low)
    spread(high_ref, slice(None), high)
    wide = WIDE[1]
    low = jnp.concatenate([low, jnp.zeros((ROWS, 2 * wide - WIDE[0]), jnp.float32)], 1)
    low, high = lift_lanes(*split_pairs(low), EDGE[1], 512, at_start, at_end)
    spread(low_low_ref, slice(None), low)
    spread(low_high_ref, slice(None), high)
    for t in range(wide // 128):
        one_ref[t] = plain_low(low_low_ref, t, 32)
        two_ref[t] = plain_low(one_ref, t, 16)
        one_high_ref[t] = plain_low(low_high_ref, t, 32)
    row = lax.axis_index("rows")
    below = (row % 2 == 0).astype(jnp.int32)
    for pack, last in ((for_even, below), (for_odd, 1 - below)):
        for t in range(wide // 128):
            at = PIECE * t
            pack[at : at + 8] = low_low_ref[t, 0:8]
            pack[at + 8 : at + 16] = low_low_ref[t, 56:64]
            pack[at + 16 : at + 24] = one_ref[t, 2:10]
            pack[at + 24 : at + 32] = one_ref[t, 22:30]
            pack[at + 32 : at + 42] = two_ref[t, 3:13]
            pack[at + 42 : at + 50] = low_high_ref[t, pl.ds(56 * last, 8)]
            pack[at + 50 : at + 58] = one_high_ref[t, pl.ds(2 + 20 * last, 8)]
        for j in range(9):
            pack[EDGES + 8 * j : EDGES + 8 * j + 8] = high_ref[j, pl.ds(56 * last, 8)]
    for t in range(wide // 128):
        s = slice(128 * t, 128 * t + 128)
        x_ref[0:8, s], x_ref[8:16, s] = low_low_ref[t, 0:8], low_low_ref[t, 56:64]
        x_ref[16:24, s], x_ref[24:32, s] = one_ref[t, 2:10], one_ref[t, 22:30]
        x_ref[32:42, s] = two_ref[t, 3:13]
    spread(y_ref, slice(None), split_lanes(2, x_ref[...])[0])
    below = (row % 4 < 2).astype(jnp.int32)
    for pack, last in ((for_even_far, below), (for_odd_far, 1 - below)):
        for t in range(WIDE[2] // 128):
            at = FAR_PIECE * t
            pack[at : at + 8] = y_ref[t, pl.ds(8 * last, 8)]
            pack[at + 8 : at + 16] = y_ref[t, pl.ds(16 + 8 * last, 8)]
            pack[at + 16 : at + 25] = y_ref[t, pl.ds(32 + last, 9)]


PIECE, EDGES, PACK = 58, 296, 368
FAR_PIECE, FAR_PACK = 25, 80


def plain_low(ref, t, tall):
    near = (lambda x: pltpu.roll(x, 1, 0)), (lambda x: pltpu.roll(x, tall - 1, 0))
    return forward_lift(ref[t, pl.ds(0, tall, stride=2)], ref[t, pl.ds(1, tall, stride=2)], near)[0]


def sides(flag, odd_ref, even_ref):
    def above(*at):
        return jnp.where(flag, odd_ref[at], even_ref[at])

    def under(*at):
        return jnp.where(flag, even_ref[at], odd_ref[at])

    return above, under


def halves_of(ref, t, tall):
    return ref[t, pl.ds(0, tall, stride=2)], ref[t, pl.ds(1, tall, stride=2)]


def lifted(ref, t, tall, begin, own):
    row, count = lax.axis_index("rows"), lax.axis_size("rows")
    starts, stops = [(begin, row == 0)], [(begin + own - 1, row == count - 1)]
    if begin >= own:
        starts.append((begin - own, row == 1))
        stops.append((begin + 2 * own - 1, row == count - 2))
    return forward_lift(*halves_of(ref, t, tall), neighbours(0, starts, stops))


def across(level, low, high):
    _, at_start, at_end = ends("cols")
    halves = lift_lanes(low, high, EDGE[level], 1024 >> level, at_start, at_end, inverse=True)
    return merge_pairs(*halves)


def split_lanes(level, band):
    _, at_start, at_end = ends("cols")
    wide = WIDE[level]
    pad = jnp.zeros((band.shape[0], 2 * wide - band.shape[1]), jnp.float32)
    halves = split_pairs(jnp.concatenate([band, pad], 1))
    return lift_lanes(*halves, EDGE[level], 1024 >> level, at_start, at_end)


def limited(limits, level, kind, coeffs):
    at = 3 * level + kind
    return soften(coeffs, limits[at : at + 1, :])


def near_kernel(
    limits, own_low, own_high, own_low_low, own_low_high, odd_ref, even_ref,
    hl0_ref, vh0_ref, hl1_ref, vh1_ref, hl2_ref, vh2_ref, next_ref, edge_ref,
    l_ref, h_ref, b_ref, x_ref, lh_ref, hh_ref,
):
    above, under = sides(lax.axis_index("rows") % 2 == 0, odd_ref, even_ref)
    for t in range(WIDE[1] // 128):
        at = PIECE * t
        s = slice(128 * t, 128 * t + 128)

        def part(offset, size=8, at=at):
            return slice(at + offset, at + offset + size)

        x_ref[0, 0:8], x_ref[0, 8:72], x_ref[0, 72:80] = above(part(8)), own_low_low[t], under(part(0))
        x_ref[1, 0:8], x_ref[1, 8:72], x_ref[1, 72:80] = above(part(42)), own_low_high[t], under(part(42))
        l_ref[t, 8:48] = lifted(x_ref, 0, 40, 4, 32)[0]
        l_ref[t, 2:10], l_ref[t, 46:54] = above(part(24)), under(part(16))
        h_ref[t, 8:48] = lifted(x_ref, 1, 40, 4, 32)[0]
        h_ref[t, 2:10], h_ref[t, 46:54] = above(part(50)), under(part(50))
        low, high = lifted(l_ref, t, 32, 6, 16)
        lh_ref[0:24, s] = limited(limits, 1, 1, high[2:26])
        b_ref[3:13, s], b_ref[13:35, s], b_ref[35:45, s] = above(part(32, 10)), low[3:25], under(part(32, 10))
        b_ref[48:56, s], b_ref[56:64, s] = above(part(0)), under(part(8))
        b_ref[64:72, s], b_ref[72:80, s] = above(part(16)), under(part(24))
        low, high = lifted(h_ref, t, 32, 6, 16)
        hl1_ref[:, s] = limited(limits, 1, 0, low[2:26])
        hh_ref[0:24, s] = limited(limits, 1, 2, high[2:26])
    vh1_ref[...] = across(1, lh_ref[0:24, :640], hh_ref[0:24, :640])[:, :1152]
    low, high = split_lanes(2, b_ref[...])
    spread(next_ref, slice(None), low[0:48])
    spread(edge_ref, slice(None), low[48:80])
    spread(h_ref, slice(0, 48), high[0:48])
    for t in range(WIDE[2] // 128):
        s = slice(128 * t, 128 * t + 128)
        high = lifted(next_ref, t, 24, 8, 8)[1]
        lh_ref[0:16, s] = limited(limits, 2, 1, high[4:20])
        low, high = lifted(h_ref, t, 24, 8, 8)
        hl2_ref[:, s] = limited(limits, 2, 0, low[4:20])
        hh_ref[0:16, s] = limited(limits, 2, 2, high[4:20])
    vh2_ref[...] = across(2, lh_ref[0:16, :384], hh_ref[0:16, :384])[:, :640]
    low, high = (
        jnp.concatenate(
            [
                jnp.concatenate([side(slice(PIECE * t + at, PIECE * t + at + 8)) for t in range(5)], 1)
                for side, at in sources
            ],
            0,
        )
        for sources in (((above, 8), (under, 0)), ((above, 42), (under, 42)))
    )
    lows = across(1, low, high)
    for j in range(9):
        x_ref[j, 0:8] = lows[0:8, 128 * j : 128 * j + 128]
        x_ref[j, 8:72] = own_low[j]
        x_ref[j, 72:80] = lows[8:16, 128 * j : 128 * j + 128]
        at = slice(EDGES + 8 * j, EDGES + 8 * j + 8)
        x_ref[j + 9, 0:8] = above(at)
        x_ref[j + 9, 8:72] = own_high[j]
        x_ref[j + 9, 72:80] = under(at)

    def lift(t, s):
        high = lifted(x_ref, t, 40, 4, 32)[1]
        lh_ref[:, s] = limited(limits, 0, 1, high)
        low, high = lifted(x_ref, t + 9, 40, 4, 32)
        hl0_ref[:, s] = limited(limits, 0, 0, low)
        hh_ref[:, s] = limited(limits, 0, 2, high)

    tiles(WIDE[0], lift)
    vh0_ref[...] = across(0, lh_ref[...], hh_ref[...])[:, 128 : 128 + COLS]


def far_kernel(
    limits, hl0_ref, vh0_ref, hl1_ref, vh1_ref, hl2_ref, vh2_ref, next_ref, edge_ref,
    odd_far, even_far, out_ref, f_ref, g_ref, l_ref, h_ref, b_ref, v_ref, r_ref, o_ref, sems,
):
    row, count = lax.axis_index("rows"), lax.axis_size("rows")
    above_far, under_far = sides(row % 4 < 2, odd_far, even_far)
    for t in range(WIDE[2] // 128):
        s = slice(128 * t, 128 * t + 128)

        def far_part(offset, size=8, at=FAR_PIECE * t):
            return slice(at + offset, at + offset + size)

        f_ref[t, 0:8], f_ref[t, 8:24], f_ref[t, 24:32] = (
            above_far(far_part(0)), edge_ref[t, 0:16], under_far(far_part(0))
        )
        near = neighbours(0, [(4, row == 1)], [(11, row == count - 2)])
        one = forward_lift(*halves_of(f_ref, t, 16), near)[0]
        g_ref[t, 10:14], g_ref[t, 42:46] = one[2:6], one[10:14]
        g_ref[t, 2:10], g_ref[t, 14:22] = above_far(far_part(8)), edge_ref[t, 16:24]
        g_ref[t, 34:42], g_ref[t, 46:54] = edge_ref[t, 24:32], under_far(far_part(8))
        near = neighbours(0, [(6, row == 1)], [(21, row == count - 2)])
        two = forward_lift(*halves_of(g_ref, t, 32), near)[0]
        l_ref[t, 0:9], l_ref[t, 9:15] = above_far(far_part(16, 9)), two[3:9]
        l_ref[t, 15:57] = next_ref[t, 3:45]
        l_ref[t, 57:63], l_ref[t, 63:72] = two[19:25], under_far(far_part(16, 9))
        b_ref[0:32, s] = lifted(l_ref, t, 40, 14, 8)[0][2:34]
    low, high = split_lanes(3, b_ref[0:32, :384])
    spread(l_ref, slice(0, 32), low)
    spread(h_ref, slice(0, 32), high)
    for t in range(WIDE[3] // 128):
        s = slice(128 * t, 128 * t + 128)
        low, high = lifted(l_ref, t, 16, 6, 4)
        v_ref[0:12, s] = low[2:14]
        v_ref[16:28, s] = limited(limits, 3, 1, high[2:14])
        low, high = lifted(h_ref, t, 16, 6, 4)
        r_ref[0:12, s] = limited(limits, 3, 0, low[2:14])
        r_ref[16:28, s] = limited(limits, 3, 2, high[2:14])
    both = across(3, v_ref[0:32, :256], r_ref[0:32, :256])[:, :384]
    low, high = both[0:16], both[16:32]
    _, at_start, at_end = ends("rows")
    for level in (3, 2, 1):
        own = OWN[level]
        long = max(own + 8, 16)
        near = neighbours(0, [(4, at_start)], [(3 + own, at_end)])
        for t in range(low.shape[1] // 128):
            s = slice(128 * t, 128 * t + 128)
            even, odd = inverse_lift(low[0:long, s], high[0:long, s], near)
            o_ref[t, pl.ds(0, long, stride=2)] = even
            o_ref[t, pl.ds(1, long, stride=2)] = odd
        size = OWN[level - 1] + 8
        low = joined(o_ref, slice(4, 4 + size), low.shape[1])
        hl, high = ((hl0_ref, vh0_ref), (hl1_ref, vh1_ref), (hl2_ref, vh2_ref))[level - 1]
        low = across(level - 1, low, hl[...])
        low = low[:, 128 : 128 + COLS] if level == 1 else low[:, : high.shape[1]]
    v_ref[...] = low
    near = neighbours(0, [(4, at_start)], [(35, at_end)])

    def finish(i, carry):
        for t in (2 * i, 2 * i + 1):
            s = pl.ds(pl.multiple_of(128 * t, 128), 128)
            even, odd = inverse_lift(v_ref[:, s], vh0_ref[:, s], near)
            o_ref[t, pl.ds(0, 40, stride=2)] = even
            o_ref[t, pl.ds(1, 40, stride=2)] = odd
            pltpu.make_async_copy(o_ref.at[t, 8:72], out_ref.at[:, s], sems.at[t]).start()
        return carry

    lax.fori_loop(0, COLS // 256, finish, 0)
    for t in range(COLS // 128):
        lanes = slice(128 * t, 128 * t + 128)
        pltpu.make_async_copy(o_ref.at[t, 8:72], out_ref.at[:, lanes], sems.at[t]).wait()


def swaps(axis, offset, apart):
    count = lax.axis_size(axis)
    pairs = []
    for block in range(offset, count, 2 * apart):
        for i in range(block, min(block + apart, count - apart)):
            pairs += [(i, i + apart), (i + apart, i)]
    return pairs


def exchange(for_even, for_odd, axis, apart=1):
    even = lax.ppermute(for_even, axis, swaps(axis, 0, apart))
    odd = lax.ppermute(for_odd, axis, swaps(axis, apart, apart))
    return odd, even


def f32(*shape):
    return jax.ShapeDtypeStruct(shape, jnp.float32)


def scratch(*shape):
    return pltpu.VMEM(shape, jnp.float32)


def call(kernel, outs, scratches, *args, scalars=0, space=pltpu.VMEM, out_space=pltpu.VMEM, cost=None):
    vmem = pl.BlockSpec(memory_space=pltpu.VMEM)
    smem = pl.BlockSpec(memory_space=pltpu.SMEM)
    return pl.pallas_call(
        kernel,
        out_shape=outs,
        in_specs=[smem] * scalars + [pl.BlockSpec(memory_space=space)] * (len(args) - scalars),
        out_specs=jax.tree.map(lambda _: pl.BlockSpec(memory_space=out_space), outs),
        scratch_shapes=scratches,
        compiler_params=pltpu.CompilerParams(vmem_limit_bytes=16 * 2**20),
        cost_estimate=cost,
    )(*args)


def local(micrograph, thresholds):
    for_even, for_odd = call(
        edges_kernel,
        (f32(ROWS, 128), f32(ROWS, 128)),
        [pltpu.SemaphoreType.DMA((2,))],
        micrograph,
        space=pltpu.HBM,
    )
    odd, even = exchange(for_even, for_odd, "cols")
    *inner, limits = call(
        inner_kernel,
        (f32(ROWS, 896), f32(ROWS, 896), f32(ROWS, 256), f32(16, 128)),
        [],
        thresholds,
        micrograph,
        scalars=1,
        cost=pl.CostEstimate(flops=2 * 10**9, bytes_accessed=4 * 10**6, transcendentals=0),
    )
    for_even, for_odd, for_even_far, for_odd_far, *own = call(
        columns_kernel,
        (f32(PACK, 128), f32(PACK, 128), f32(FAR_PACK, 128), f32(FAR_PACK, 128))
        + (f32(9, ROWS, 128), f32(9, ROWS, 128), f32(5, ROWS, 128), f32(5, ROWS, 128)),
        [scratch(5, 32, 128), scratch(5, 16, 128), scratch(5, 32, 128), scratch(48, 640), scratch(3, 48, 128)],
        *inner,
        odd,
        even,
    )
    near = exchange(for_even, for_odd, "rows")
    far = exchange(for_even_far, for_odd_far, "rows", 2)
    known = call(
        near_kernel,
        (f32(40, 1152), f32(40, COLS), f32(24, 640), f32(24, 1152), f32(16, 384), f32(16, 640))
        + (f32(3, 48, 128), f32(3, 32, 128)),
        [scratch(5, 64, 128), scratch(5, 64, 128), scratch(80, 640), scratch(18, 80, 128)]
        + [scratch(40, 1152), scratch(40, 1152)],
        limits,
        *own,
        *near,
        cost=pl.CostEstimate(flops=2 * 10**9, bytes_accessed=4 * 10**6, transcendentals=0),
    )
    return call(
        far_kernel,
        f32(ROWS, COLS),
        [scratch(3, 32, 128), scratch(3, 64, 128), scratch(3, 80, 128), scratch(3, 80, 128)]
        + [scratch(32, 384), scratch(40, COLS), scratch(32, 256), scratch(16, 80, 128)]
        + [pltpu.SemaphoreType.DMA((16,))],
        limits,
        *known,
        *far,
        out_space=pl.ANY,
    )


def solution(mesh):
    placed = (P("rows", "cols"), P())
    return jax.shard_map(
        local, mesh=mesh, in_specs=placed, out_specs=P("rows", "cols"), check_vma=False
    )
```

```python
import functools

import jax
import jax.numpy as jnp
from jax import lax
from jax.experimental import pallas as pl
from jax.experimental.pallas import tpu as pltpu
from jax.sharding import PartitionSpec as P

LEVELS = 4

step_one = -1.586134342
step_two = -0.05298011854
step_three = 0.8829110762
step_four = 0.4435068522
band_gain = 1.149604398
inv_gain = 1.0 / band_gain

ROWS, COLS = 64, 2048
WIDE = (1152, 640, 384, 256)
EDGE = (64, 32, 16, 8)
OWN = (32, 16, 8, 4)


STEPS_FROM = 1152
GROUP = 64
MATRIX_FROM = 640


def combined(*terms):
    total = {}
    for factor, taps, moved in terms:
        for (sequence, offset), tap in taps.items():
            key = (sequence, offset + moved)
            total[key] = total.get(key, 0.0) + factor * tap
    return total


def lifted_taps(inverse):
    even, odd = {("even", 0): 1.0}, {("odd", 0): 1.0}
    if inverse:
        even, odd = combined((1.0 / band_gain, even, 0)), combined((band_gain, odd, 0))
        for to_even, to_odd in ((step_four, step_three), (step_two, step_one)):
            even = combined((1.0, even, 0), (-to_even, odd, 0), (-to_even, odd, -1))
            odd = combined((1.0, odd, 0), (-to_odd, even, 0), (-to_odd, even, 1))
        return even, odd
    for to_odd, to_even in ((step_one, step_two), (step_three, step_four)):
        odd = combined((1.0, odd, 0), (to_odd, even, 0), (to_odd, even, 1))
        even = combined((1.0, even, 0), (to_even, odd, 0), (to_even, odd, -1))
    return combined((band_gain, even, 0)), combined((1.0 / band_gain, odd, 0))


def lift_lanes(even, odd, first, count, at_start, at_end, inverse=False):
    rows, width = (odd if even is None else even).shape
    if width >= STEPS_FROM and even is not None and odd is not None:
        near = neighbours(1, [(first, at_start)], [(first + count - 1, at_end)])
        lift = inverse_lift if inverse else forward_lift
        groups = [slice(k, min(k + GROUP, rows)) for k in range(0, rows, GROUP)]
        parts = [lift(even[g], odd[g], near) for g in groups]
        return [jnp.concatenate(x, 0) if len(x) > 1 else x[0] for x in zip(*parts)]
    last = first + count - 1
    shifted = {}
    for name, half in (("even", even), ("odd", odd)):
        if half is None:
            continue
        x = {offset: pltpu.roll(half, -offset % width, 1) for offset in (-2, -1, 1, 2)}
        x[0] = half
        if name == "even":
            mirrored = {
                -1: [(1, first, at_start)],
                -2: [(2, first, at_start), (0, first + 1, at_start)],
                1: [(0, last, at_end)],
                2: [(-1, last, at_end), (1, last - 1, at_end)],
            }
        else:
            mirrored = {
                -1: [(0, first, at_start)],
                -2: [(1, first, at_start), (-1, first + 1, at_start)],
                1: [(-1, last, at_end)],
                2: [(-2, last, at_end), (0, last - 1, at_end)],
            }
        shifted[name, 0] = half
        for offset, patches in mirrored.items():
            moved = x[offset]
            for source, lane, flag in patches:
                moved = patch(moved, x[source], 1, lane, flag)
            shifted[name, offset] = moved
    out = []
    for taps in lifted_taps(inverse):
        by_tap = {}
        for key, tap in sorted(taps.items()):
            if key not in shifted:
                continue
            by_tap.setdefault(round(tap, 9), []).append((tap, shifted[key]))
        total = None
        for group in by_tap.values():
            term = sum((x for _, x in group[1:]), group[0][1]) * group[0][0]
            total = term if total is None else total + term
        out.append(total)
    return out


def soften(coeffs, limit):
    return coeffs - jnp.minimum(jnp.maximum(coeffs, -limit), limit)


def patch(shifted, source, axis, index, flag):
    unit = 8 if axis == 0 else 128
    lo = index // unit * unit
    hi = min(lo + unit, shifted.shape[axis])
    cut = functools.partial(lax.slice_in_dim, axis=axis)
    tile = cut(shifted, lo, hi)
    here = (lax.broadcasted_iota(jnp.int32, tile.shape, axis) == index - lo) & flag
    tile = jnp.where(here, cut(source, lo, hi), tile)
    parts = [cut(shifted, 0, lo)] if lo else []
    parts.append(tile)
    if hi < shifted.shape[axis]:
        parts.append(cut(shifted, hi, shifted.shape[axis]))
    return jnp.concatenate(parts, axis) if len(parts) > 1 else tile


def neighbours(axis, starts, stops):
    def before(odd):
        rolled = pltpu.roll(odd, 1, axis)
        for index, flag in starts:
            rolled = patch(rolled, odd, axis, index, flag)
        return rolled

    def after(even):
        rolled = pltpu.roll(even, even.shape[axis] - 1, axis)
        for index, flag in stops:
            rolled = patch(rolled, even, axis, index, flag)
        return rolled

    return before, after


def forward_lift(even, odd, near):
    before, after = near
    odd = odd + step_one * (even + after(even))
    even = even + step_two * (before(odd) + odd)
    odd = odd + step_three * (even + after(even))
    even = even + step_four * (before(odd) + odd)
    return even * band_gain, odd * inv_gain


def inverse_lift(low, high, near):
    before, after = near
    even = low * inv_gain
    odd = high * band_gain
    even = even - step_four * (before(odd) + odd)
    odd = odd - step_three * (even + after(even))
    even = even - step_two * (before(odd) + odd)
    odd = odd - step_one * (even + after(even))
    return even, odd


def pairing(transpose):
    a = lax.broadcasted_iota(jnp.int32, (256, 256), 1 if not transpose else 0)
    b = lax.broadcasted_iota(jnp.int32, (256, 256), 0 if not transpose else 1)
    target = jnp.where(a < 128, 2 * a, 2 * a - 255)
    return jnp.where(b == target, 1.0, 0.0).astype(jnp.bfloat16)


def permuted(x, matrix):
    rows = x.shape[0]
    high = x.astype(jnp.bfloat16).astype(jnp.float32)
    rest = x - high
    middle = rest.astype(jnp.bfloat16).astype(jnp.float32)
    pieces = [high, middle, rest - middle]
    if rows % 16:
        pieces.append(jnp.zeros((-3 * rows % 16, x.shape[1]), jnp.float32))
        pieces = [jnp.concatenate(pieces, 0).astype(jnp.bfloat16)]
    else:
        pieces = [jnp.concatenate([piece.astype(jnp.bfloat16) for piece in pieces], 0)]
    out = jnp.dot(pieces[0], matrix, preferred_element_type=jnp.float32)
    return (out[:rows] + out[rows : 2 * rows]) + out[2 * rows : 3 * rows]


def picked(x, index):
    return jnp.take_along_axis(x, index, axis=1, mode="promise_in_bounds")


def split_pairs(x):
    if x.shape[1] < 2 * MATRIX_FROM:
        return split_by_picks(x)
    matrix = pairing(False)
    both = [permuted(x[:, k : k + 256], matrix) for k in range(0, x.shape[1], 256)]
    return jnp.concatenate([y[:, :128] for y in both], 1), jnp.concatenate([y[:, 128:] for y in both], 1)


def merge_pairs(even, odd):
    if even.shape[1] < MATRIX_FROM:
        return merge_by_picks(even, odd)
    matrix = pairing(True)
    return jnp.concatenate(
        [
            permuted(jnp.concatenate([even[:, k : k + 128], odd[:, k : k + 128]], 1), matrix)
            for k in range(0, even.shape[1], 128)
        ],
        1,
    )


def split_by_picks(x):
    rows = x.shape[0]
    lane = lax.broadcasted_iota(jnp.int32, (rows, 128), 1)
    lower = lane < 64
    near = jnp.where(lower, 2 * lane, 2 * lane - 127)
    far = jnp.where(lower, 2 * lane + 1, 2 * lane - 128)
    evens, odds = [], []
    for k in range(0, x.shape[1], 256):
        first, second = picked(x[:, k : k + 128], near), picked(x[:, k + 128 : k + 256], far)
        evens.append(jnp.where(lower, first, second))
        odds.append(pltpu.roll(jnp.where(lower, second, first), 64, 1))
    return jnp.concatenate(evens, 1), jnp.concatenate(odds, 1)


def merge_by_picks(even, odd):
    rows = even.shape[0]
    lane = lax.broadcasted_iota(jnp.int32, (rows, 128), 1)
    lower = lane < 64
    is_odd = lane % 2 == 1
    half = lane // 2
    near = jnp.where(is_odd, half + 64, half)
    far = jnp.where(is_odd, half, half + 64)
    out = []
    for k in range(0, even.shape[1], 128):
        e, o = even[:, k : k + 128], pltpu.roll(odd[:, k : k + 128], 64, 1)
        out += [picked(jnp.where(lower, e, o), near), picked(jnp.where(lower, o, e), far)]
    return jnp.concatenate(out, 1)


def tiles(width, body):
    def step(t, carry):
        body(t, pl.ds(pl.multiple_of(t * 128, 128), 128))
        return carry

    if width > 640:
        lax.fori_loop(0, width // 128, step, 0)
    else:
        for t in range(width // 128):
            body(t, slice(128 * t, 128 * t + 128))


def joined(ref, rows, width):
    return jnp.concatenate([ref[k, rows] for k in range(width // 128)], 1)


def spread(ref, rows, value):
    for k in range(value.shape[1] // 128):
        ref[k, rows] = value[:, 128 * k : 128 * k + 128]


def ends(axis):
    position = lax.axis_index(axis)
    return position % 2 == 0, position == 0, position == lax.axis_size(axis) - 1


def edges_kernel(x_ref, for_even, for_odd, sems):
    is_even = ends("cols")[0]
    right = jnp.where(is_even, COLS - 128, 0)
    copies = []
    for k, (at, out) in enumerate(((right, for_even), (COLS - 128 - right, for_odd))):
        lanes = pl.ds(pl.multiple_of(at, 128), 128)
        copies.append(pltpu.make_async_copy(x_ref.at[:, lanes], out, sems.at[k]))
        copies[-1].start()
    for copy in copies:
        copy.wait()


def inner_kernel(t_ref, x_ref, e_ref, o_ref, edge_ref, limit_ref):
    for level in range(LEVELS):
        for kind in range(3):
            limit_ref[3 * level + kind : 3 * level + kind + 1, :] = jnp.full((1, 128), t_ref[level, kind])
    e_ref[...], o_ref[...] = split_pairs(x_ref[:, 128 : COLS - 128])
    edge_ref[:, :128] = x_ref[:, :128]
    edge_ref[:, 128:] = x_ref[:, COLS - 128 :]


def columns_kernel(
    e_ref, o_ref, edge_ref, odd_ref, even_ref, for_even, for_odd, for_even_far, for_odd_far,
    low_ref, high_ref, low_low_ref, low_high_ref, one_ref, two_ref, one_high_ref,
    x_ref, y_ref,
):
    is_even, at_start, at_end = ends("cols")
    left = jnp.where(is_even, odd_ref[...], even_ref[...])
    right = jnp.where(is_even, even_ref[...], odd_ref[...])
    first = split_pairs(jnp.concatenate([left, edge_ref[:, :128]], 1))
    last = split_pairs(jnp.concatenate([edge_ref[:, 128:], right], 1))
    low, high = lift_lanes(
        jnp.concatenate([first[0], e_ref[...], last[0]], 1),
        jnp.concatenate([first[1], o_ref[...], last[1]], 1),
        EDGE[0],
        1024,
        at_start,
        at_end,
    )
    spread(low_ref, slice(None), low)
    spread(high_ref, slice(None), high)
    wide = WIDE[1]
    low = jnp.concatenate([low, jnp.zeros((ROWS, 2 * wide - WIDE[0]), jnp.float32)], 1)
    low, high = lift_lanes(*split_pairs(low), EDGE[1], 512, at_start, at_end)
    spread(low_low_ref, slice(None), low)
    spread(low_high_ref, slice(None), high)
    for t in range(wide // 128):
        one_ref[t] = plain_low(low_low_ref, t, 32)
        two_ref[t] = plain_low(one_ref, t, 16)
        one_high_ref[t] = plain_low(low_high_ref, t, 32)
    row = lax.axis_index("rows")
    below = (row % 2 == 0).astype(jnp.int32)
    for pack, last in ((for_even, below), (for_odd, 1 - below)):
        for t in range(wide // 128):
            at = PIECE * t
            pack[at : at + 8] = low_low_ref[t, 0:8]
            pack[at + 8 : at + 16] = low_low_ref[t, 56:64]
            pack[at + 16 : at + 24] = one_ref[t, 2:10]
            pack[at + 24 : at + 32] = one_ref[t, 22:30]
            pack[at + 32 : at + 42] = two_ref[t, 3:13]
            pack[at + 42 : at + 50] = low_high_ref[t, pl.ds(56 * last, 8)]
            pack[at + 50 : at + 58] = one_high_ref[t, pl.ds(2 + 20 * last, 8)]
        for j in range(9):
            pack[EDGES + 8 * j : EDGES + 8 * j + 8] = high_ref[j, pl.ds(56 * last, 8)]
    for t in range(wide // 128):
        s = slice(128 * t, 128 * t + 128)
        x_ref[0:8, s], x_ref[8:16, s] = low_low_ref[t, 0:8], low_low_ref[t, 56:64]
        x_ref[16:24, s], x_ref[24:32, s] = one_ref[t, 2:10], one_ref[t, 22:30]
        x_ref[32:42, s] = two_ref[t, 3:13]
    spread(y_ref, slice(None), split_lanes(2, x_ref[...])[0])
    below = (row % 4 < 2).astype(jnp.int32)
    for pack, last in ((for_even_far, below), (for_odd_far, 1 - below)):
        for t in range(WIDE[2] // 128):
            at = FAR_PIECE * t
            pack[at : at + 8] = y_ref[t, pl.ds(8 * last, 8)]
            pack[at + 8 : at + 16] = y_ref[t, pl.ds(16 + 8 * last, 8)]
            pack[at + 16 : at + 25] = y_ref[t, pl.ds(32 + last, 9)]


PIECE, EDGES, PACK = 58, 296, 368
FAR_PIECE, FAR_PACK = 25, 80


def plain_low(ref, t, tall):
    near = (lambda x: pltpu.roll(x, 1, 0)), (lambda x: pltpu.roll(x, tall - 1, 0))
    return forward_lift(ref[t, pl.ds(0, tall, stride=2)], ref[t, pl.ds(1, tall, stride=2)], near)[0]


def sides(flag, odd_ref, even_ref):
    def above(*at):
        return jnp.where(flag, odd_ref[at], even_ref[at])

    def under(*at):
        return jnp.where(flag, even_ref[at], odd_ref[at])

    return above, under


def halves_of(ref, t, tall):
    return ref[t, pl.ds(0, tall, stride=2)], ref[t, pl.ds(1, tall, stride=2)]


def lifted(ref, t, tall, begin, own):
    row, count = lax.axis_index("rows"), lax.axis_size("rows")
    starts, stops = [(begin, row == 0)], [(begin + own - 1, row == count - 1)]
    if begin >= own:
        starts.append((begin - own, row == 1))
        stops.append((begin + 2 * own - 1, row == count - 2))
    return forward_lift(*halves_of(ref, t, tall), neighbours(0, starts, stops))


def across(level, low, high):
    _, at_start, at_end = ends("cols")
    halves = lift_lanes(low, high, EDGE[level], 1024 >> level, at_start, at_end, inverse=True)
    return merge_pairs(*halves)


def split_lanes(level, band):
    _, at_start, at_end = ends("cols")
    wide = WIDE[level]
    pad = jnp.zeros((band.shape[0], 2 * wide - band.shape[1]), jnp.float32)
    halves = split_pairs(jnp.concatenate([band, pad], 1))
    return lift_lanes(*halves, EDGE[level], 1024 >> level, at_start, at_end)


def limited(limits, level, kind, coeffs):
    at = 3 * level + kind
    return soften(coeffs, limits[at : at + 1, :])


def near_kernel(
    limits, own_low, own_high, own_low_low, own_low_high, odd_ref, even_ref,
    ah0_ref, vh0_ref, ah1_ref, vh1_ref, ah2_ref, vh2_ref, next_ref, edge_ref,
    l_ref, h_ref, b_ref, x_ref, lh_ref, hh_ref, hl_ref,
):
    above, under = sides(lax.axis_index("rows") % 2 == 0, odd_ref, even_ref)
    for t in range(WIDE[1] // 128):
        at = PIECE * t
        s = slice(128 * t, 128 * t + 128)

        def part(offset, size=8, at=at):
            return slice(at + offset, at + offset + size)

        x_ref[0, 0:8], x_ref[0, 8:72], x_ref[0, 72:80] = above(part(8)), own_low_low[t], under(part(0))
        x_ref[1, 0:8], x_ref[1, 8:72], x_ref[1, 72:80] = above(part(42)), own_low_high[t], under(part(42))
        l_ref[t, 8:48] = lifted(x_ref, 0, 40, 4, 32)[0]
        l_ref[t, 2:10], l_ref[t, 46:54] = above(part(24)), under(part(16))
        h_ref[t, 8:48] = lifted(x_ref, 1, 40, 4, 32)[0]
        h_ref[t, 2:10], h_ref[t, 46:54] = above(part(50)), under(part(50))
        low, high = lifted(l_ref, t, 32, 6, 16)
        lh_ref[0:24, s] = limited(limits, 1, 1, high[2:26])
        b_ref[3:13, s], b_ref[13:35, s], b_ref[35:45, s] = above(part(32, 10)), low[3:25], under(part(32, 10))
        b_ref[48:56, s], b_ref[56:64, s] = above(part(0)), under(part(8))
        b_ref[64:72, s], b_ref[72:80, s] = above(part(16)), under(part(24))
        low, high = lifted(h_ref, t, 32, 6, 16)
        hl_ref[0:24, s] = limited(limits, 1, 0, low[2:26])
        hh_ref[0:24, s] = limited(limits, 1, 2, high[2:26])
    ah1_ref[...] = across(1, None, hl_ref[0:24, :640])[:, :1152]
    vh1_ref[...] = across(1, lh_ref[0:24, :640], hh_ref[0:24, :640])[:, :1152]
    low, high = split_lanes(2, b_ref[...])
    spread(next_ref, slice(None), low[0:48])
    spread(edge_ref, slice(None), low[48:80])
    spread(h_ref, slice(0, 48), high[0:48])
    for t in range(WIDE[2] // 128):
        s = slice(128 * t, 128 * t + 128)
        high = lifted(next_ref, t, 24, 8, 8)[1]
        lh_ref[0:16, s] = limited(limits, 2, 1, high[4:20])
        low, high = lifted(h_ref, t, 24, 8, 8)
        hl_ref[0:16, s] = limited(limits, 2, 0, low[4:20])
        hh_ref[0:16, s] = limited(limits, 2, 2, high[4:20])
    ah2_ref[...] = across(2, None, hl_ref[0:16, :384])[:, :640]
    vh2_ref[...] = across(2, lh_ref[0:16, :384], hh_ref[0:16, :384])[:, :640]
    low, high = (
        jnp.concatenate(
            [
                jnp.concatenate([side(slice(PIECE * t + at, PIECE * t + at + 8)) for t in range(5)], 1)
                for side, at in sources
            ],
            0,
        )
        for sources in (((above, 8), (under, 0)), ((above, 42), (under, 42)))
    )
    lows = across(1, low, high)
    for j in range(9):
        x_ref[j, 0:8] = lows[0:8, 128 * j : 128 * j + 128]
        x_ref[j, 8:72] = own_low[j]
        x_ref[j, 72:80] = lows[8:16, 128 * j : 128 * j + 128]
        at = slice(EDGES + 8 * j, EDGES + 8 * j + 8)
        x_ref[j + 9, 0:8] = above(at)
        x_ref[j + 9, 8:72] = own_high[j]
        x_ref[j + 9, 72:80] = under(at)

    def lift(t, s):
        high = lifted(x_ref, t, 40, 4, 32)[1]
        lh_ref[:, s] = limited(limits, 0, 1, high)
        low, high = lifted(x_ref, t + 9, 40, 4, 32)
        hl_ref[:, s] = limited(limits, 0, 0, low)
        hh_ref[:, s] = limited(limits, 0, 2, high)

    tiles(WIDE[0], lift)
    ah0_ref[...] = across(0, None, hl_ref[...])[:, 128 : 128 + COLS]
    vh0_ref[...] = across(0, lh_ref[...], hh_ref[...])[:, 128 : 128 + COLS]


def far_kernel(
    limits, ah0_ref, vh0_ref, ah1_ref, vh1_ref, ah2_ref, vh2_ref, next_ref, edge_ref,
    odd_far, even_far, out_ref, f_ref, g_ref, l_ref, h_ref, b_ref, v_ref, r_ref, o_ref, sems,
):
    row, count = lax.axis_index("rows"), lax.axis_size("rows")
    above_far, under_far = sides(row % 4 < 2, odd_far, even_far)
    for t in range(WIDE[2] // 128):
        s = slice(128 * t, 128 * t + 128)

        def far_part(offset, size=8, at=FAR_PIECE * t):
            return slice(at + offset, at + offset + size)

        f_ref[t, 0:8], f_ref[t, 8:24], f_ref[t, 24:32] = (
            above_far(far_part(0)), edge_ref[t, 0:16], under_far(far_part(0))
        )
        near = neighbours(0, [(4, row == 1)], [(11, row == count - 2)])
        one = forward_lift(*halves_of(f_ref, t, 16), near)[0]
        g_ref[t, 10:14], g_ref[t, 42:46] = one[2:6], one[10:14]
        g_ref[t, 2:10], g_ref[t, 14:22] = above_far(far_part(8)), edge_ref[t, 16:24]
        g_ref[t, 34:42], g_ref[t, 46:54] = edge_ref[t, 24:32], under_far(far_part(8))
        near = neighbours(0, [(6, row == 1)], [(21, row == count - 2)])
        two = forward_lift(*halves_of(g_ref, t, 32), near)[0]
        l_ref[t, 0:9], l_ref[t, 9:15] = above_far(far_part(16, 9)), two[3:9]
        l_ref[t, 15:57] = next_ref[t, 3:45]
        l_ref[t, 57:63], l_ref[t, 63:72] = two[19:25], under_far(far_part(16, 9))
        b_ref[0:32, s] = lifted(l_ref, t, 40, 14, 8)[0][2:34]
    low, high = split_lanes(3, b_ref[0:32, :384])
    spread(l_ref, slice(0, 32), low)
    spread(h_ref, slice(0, 32), high)
    for t in range(WIDE[3] // 128):
        s = slice(128 * t, 128 * t + 128)
        low, high = lifted(l_ref, t, 16, 6, 4)
        v_ref[0:12, s] = low[2:14]
        v_ref[16:28, s] = limited(limits, 3, 1, high[2:14])
        low, high = lifted(h_ref, t, 16, 6, 4)
        r_ref[0:12, s] = limited(limits, 3, 0, low[2:14])
        r_ref[16:28, s] = limited(limits, 3, 2, high[2:14])
    both = across(3, v_ref[0:32, :256], r_ref[0:32, :256])[:, :384]
    low, high = both[0:16], both[16:32]
    _, at_start, at_end = ends("rows")
    for level in (3, 2, 1):
        own = OWN[level]
        long = max(own + 8, 16)
        near = neighbours(0, [(4, at_start)], [(3 + own, at_end)])
        for t in range(low.shape[1] // 128):
            s = slice(128 * t, 128 * t + 128)
            even, odd = inverse_lift(low[0:long, s], high[0:long, s], near)
            o_ref[t, pl.ds(0, long, stride=2)] = even
            o_ref[t, pl.ds(1, long, stride=2)] = odd
        size = OWN[level - 1] + 8
        low = joined(o_ref, slice(4, 4 + size), low.shape[1])
        added, high = ((ah0_ref, vh0_ref), (ah1_ref, vh1_ref), (ah2_ref, vh2_ref))[level - 1]
        low = across(level - 1, low, None)
        low = low[:, 128 : 128 + COLS] if level == 1 else low[:, : high.shape[1]]
        low = low + added[...]
    v_ref[...] = low
    near = neighbours(0, [(4, at_start)], [(35, at_end)])

    def finish(i, carry):
        for t in (2 * i, 2 * i + 1):
            s = pl.ds(pl.multiple_of(128 * t, 128), 128)
            even, odd = inverse_lift(v_ref[:, s], vh0_ref[:, s], near)
            o_ref[t, pl.ds(0, 40, stride=2)] = even
            o_ref[t, pl.ds(1, 40, stride=2)] = odd
            pltpu.make_async_copy(o_ref.at[t, 8:72], out_ref.at[:, s], sems.at[t]).start()
        return carry

    lax.fori_loop(0, COLS // 256, finish, 0)
    for t in range(COLS // 128):
        lanes = slice(128 * t, 128 * t + 128)
        pltpu.make_async_copy(o_ref.at[t, 8:72], out_ref.at[:, lanes], sems.at[t]).wait()


def swaps(axis, offset, apart):
    count = lax.axis_size(axis)
    pairs = []
    for block in range(offset, count, 2 * apart):
        for i in range(block, min(block + apart, count - apart)):
            pairs += [(i, i + apart), (i + apart, i)]
    return pairs


def exchange(for_even, for_odd, axis, apart=1):
    even = lax.ppermute(for_even, axis, swaps(axis, 0, apart))
    odd = lax.ppermute(for_odd, axis, swaps(axis, apart, apart))
    return odd, even


def f32(*shape):
    return jax.ShapeDtypeStruct(shape, jnp.float32)


def scratch(*shape):
    return pltpu.VMEM(shape, jnp.float32)


def call(kernel, outs, scratches, *args, scalars=0, space=pltpu.VMEM, out_space=pltpu.VMEM, cost=None):
    vmem = pl.BlockSpec(memory_space=pltpu.VMEM)
    smem = pl.BlockSpec(memory_space=pltpu.SMEM)
    return pl.pallas_call(
        kernel,
        out_shape=outs,
        in_specs=[smem] * scalars + [pl.BlockSpec(memory_space=space)] * (len(args) - scalars),
        out_specs=jax.tree.map(lambda _: pl.BlockSpec(memory_space=out_space), outs),
        scratch_shapes=scratches,
        compiler_params=pltpu.CompilerParams(vmem_limit_bytes=16 * 2**20),
        cost_estimate=cost,
    )(*args)


def local(micrograph, thresholds):
    for_even, for_odd = call(
        edges_kernel,
        (f32(ROWS, 128), f32(ROWS, 128)),
        [pltpu.SemaphoreType.DMA((2,))],
        micrograph,
        space=pltpu.HBM,
    )
    odd, even = exchange(for_even, for_odd, "cols")
    *inner, limits = call(
        inner_kernel,
        (f32(ROWS, 896), f32(ROWS, 896), f32(ROWS, 256), f32(16, 128)),
        [],
        thresholds,
        micrograph,
        scalars=1,
        cost=pl.CostEstimate(flops=2 * 10**9, bytes_accessed=4 * 10**6, transcendentals=0),
    )
    for_even, for_odd, for_even_far, for_odd_far, *own = call(
        columns_kernel,
        (f32(PACK, 128), f32(PACK, 128), f32(FAR_PACK, 128), f32(FAR_PACK, 128))
        + (f32(9, ROWS, 128), f32(9, ROWS, 128), f32(5, ROWS, 128), f32(5, ROWS, 128)),
        [scratch(5, 32, 128), scratch(5, 16, 128), scratch(5, 32, 128), scratch(48, 640), scratch(3, 48, 128)],
        *inner,
        odd,
        even,
    )
    near = exchange(for_even, for_odd, "rows")
    far = exchange(for_even_far, for_odd_far, "rows", 2)
    known = call(
        near_kernel,
        (f32(40, COLS), f32(40, COLS), f32(24, 1152), f32(24, 1152), f32(16, 640), f32(16, 640))
        + (f32(3, 48, 128), f32(3, 32, 128)),
        [scratch(5, 64, 128), scratch(5, 64, 128), scratch(80, 640), scratch(18, 80, 128)]
        + [scratch(40, 1152), scratch(40, 1152), scratch(40, 1152)],
        limits,
        *own,
        *near,
        cost=pl.CostEstimate(flops=2 * 10**9, bytes_accessed=4 * 10**6, transcendentals=0),
    )
    return call(
        far_kernel,
        f32(ROWS, COLS),
        [scratch(3, 32, 128), scratch(3, 64, 128), scratch(3, 80, 128), scratch(3, 80, 128)]
        + [scratch(32, 384), scratch(40, COLS), scratch(32, 256), scratch(16, 80, 128)]
        + [pltpu.SemaphoreType.DMA((16,))],
        limits,
        *known,
        *far,
        out_space=pl.ANY,
    )


def solution(mesh):
    placed = (P("rows", "cols"), P())
    return jax.shard_map(
        local, mesh=mesh, in_specs=placed, out_specs=P("rows", "cols"), check_vma=False
    )
```

```python
import functools

import jax
import jax.numpy as jnp
from jax import lax
from jax.experimental import pallas as pl
from jax.experimental.pallas import tpu as pltpu
from jax.sharding import PartitionSpec as P

LEVELS = 4

step_one = -1.586134342
step_two = -0.05298011854
step_three = 0.8829110762
step_four = 0.4435068522
band_gain = 1.149604398
inv_gain = 1.0 / band_gain

ROWS, COLS = 64, 2048
WIDE = (1152, 640, 384, 256)
EDGE = (64, 32, 16, 8)
OWN = (32, 16, 8, 4)


STEPS_FROM = 640
GROUP = 64
MATRIX_FROM = 640


def combined(*terms):
    total = {}
    for factor, taps, moved in terms:
        for (sequence, offset), tap in taps.items():
            key = (sequence, offset + moved)
            total[key] = total.get(key, 0.0) + factor * tap
    return total


def lifted_taps(inverse):
    even, odd = {("even", 0): 1.0}, {("odd", 0): 1.0}
    if inverse:
        even, odd = combined((1.0 / band_gain, even, 0)), combined((band_gain, odd, 0))
        for to_even, to_odd in ((step_four, step_three), (step_two, step_one)):
            even = combined((1.0, even, 0), (-to_even, odd, 0), (-to_even, odd, -1))
            odd = combined((1.0, odd, 0), (-to_odd, even, 0), (-to_odd, even, 1))
        return even, odd
    for to_odd, to_even in ((step_one, step_two), (step_three, step_four)):
        odd = combined((1.0, odd, 0), (to_odd, even, 0), (to_odd, even, 1))
        even = combined((1.0, even, 0), (to_even, odd, 0), (to_even, odd, -1))
    return combined((band_gain, even, 0)), combined((1.0 / band_gain, odd, 0))


def lift_lanes(even, odd, first, count, at_start, at_end, inverse=False):
    rows, width = (odd if even is None else even).shape
    if width >= STEPS_FROM and even is not None and odd is not None:
        near = neighbours(1, [(first, at_start)], [(first + count - 1, at_end)])
        lift = inverse_lift if inverse else forward_lift
        groups = [slice(k, min(k + GROUP, rows)) for k in range(0, rows, GROUP)]
        parts = [lift(even[g], odd[g], near) for g in groups]
        return [jnp.concatenate(x, 0) if len(x) > 1 else x[0] for x in zip(*parts)]
    last = first + count - 1
    shifted = {}
    for name, half in (("even", even), ("odd", odd)):
        if half is None:
            continue
        x = {offset: pltpu.roll(half, -offset % width, 1) for offset in (-2, -1, 1, 2)}
        x[0] = half
        if name == "even":
            mirrored = {
                -1: [(1, first, at_start)],
                -2: [(2, first, at_start), (0, first + 1, at_start)],
                1: [(0, last, at_end)],
                2: [(-1, last, at_end), (1, last - 1, at_end)],
            }
        else:
            mirrored = {
                -1: [(0, first, at_start)],
                -2: [(1, first, at_start), (-1, first + 1, at_start)],
                1: [(-1, last, at_end)],
                2: [(-2, last, at_end), (0, last - 1, at_end)],
            }
        shifted[name, 0] = half
        for offset, patches in mirrored.items():
            moved = x[offset]
            for source, lane, flag in patches:
                moved = patch(moved, x[source], 1, lane, flag)
            shifted[name, offset] = moved
    out = []
    for taps in lifted_taps(inverse):
        by_tap = {}
        for key, tap in sorted(taps.items()):
            if key not in shifted:
                continue
            by_tap.setdefault(round(tap, 9), []).append((tap, shifted[key]))
        total = None
        for group in by_tap.values():
            term = sum((x for _, x in group[1:]), group[0][1]) * group[0][0]
            total = term if total is None else total + term
        out.append(total)
    return out


def soften(coeffs, limit):
    return coeffs - jnp.minimum(jnp.maximum(coeffs, -limit), limit)


def patch(shifted, source, axis, index, flag):
    unit = 8 if axis == 0 else 128
    lo = index // unit * unit
    hi = min(lo + unit, shifted.shape[axis])
    cut = functools.partial(lax.slice_in_dim, axis=axis)
    tile = cut(shifted, lo, hi)
    here = (lax.broadcasted_iota(jnp.int32, tile.shape, axis) == index - lo) & flag
    tile = jnp.where(here, cut(source, lo, hi), tile)
    parts = [cut(shifted, 0, lo)] if lo else []
    parts.append(tile)
    if hi < shifted.shape[axis]:
        parts.append(cut(shifted, hi, shifted.shape[axis]))
    return jnp.concatenate(parts, axis) if len(parts) > 1 else tile


def neighbours(axis, starts, stops):
    def before(odd):
        rolled = pltpu.roll(odd, 1, axis)
        for index, flag in starts:
            rolled = patch(rolled, odd, axis, index, flag)
        return rolled

    def after(even):
        rolled = pltpu.roll(even, even.shape[axis] - 1, axis)
        for index, flag in stops:
            rolled = patch(rolled, even, axis, index, flag)
        return rolled

    return before, after


def forward_lift(even, odd, near):
    before, after = near
    odd = odd + step_one * (even + after(even))
    even = even + step_two * (before(odd) + odd)
    odd = odd + step_three * (even + after(even))
    even = even + step_four * (before(odd) + odd)
    return even * band_gain, odd * inv_gain


def inverse_lift(low, high, near):
    before, after = near
    even = low * inv_gain
    odd = high * band_gain
    even = even - step_four * (before(odd) + odd)
    odd = odd - step_three * (even + after(even))
    even = even - step_two * (before(odd) + odd)
    odd = odd - step_one * (even + after(even))
    return even, odd


def pairing(transpose):
    a = lax.broadcasted_iota(jnp.int32, (256, 256), 1 if not transpose else 0)
    b = lax.broadcasted_iota(jnp.int32, (256, 256), 0 if not transpose else 1)
    target = jnp.where(a < 128, 2 * a, 2 * a - 255)
    return jnp.where(b == target, 1.0, 0.0).astype(jnp.bfloat16)


def permuted(x, matrix):
    rows = x.shape[0]
    high = x.astype(jnp.bfloat16).astype(jnp.float32)
    rest = x - high
    middle = rest.astype(jnp.bfloat16).astype(jnp.float32)
    pieces = [high, middle, rest - middle]
    if rows % 16:
        pieces.append(jnp.zeros((-3 * rows % 16, x.shape[1]), jnp.float32))
        pieces = [jnp.concatenate(pieces, 0).astype(jnp.bfloat16)]
    else:
        pieces = [jnp.concatenate([piece.astype(jnp.bfloat16) for piece in pieces], 0)]
    out = jnp.dot(pieces[0], matrix, preferred_element_type=jnp.float32)
    return (out[:rows] + out[rows : 2 * rows]) + out[2 * rows : 3 * rows]


def picked(x, index):
    return jnp.take_along_axis(x, index, axis=1, mode="promise_in_bounds")


def split_pairs(x):
    if x.shape[1] < 2 * MATRIX_FROM:
        return split_by_picks(x)
    matrix = pairing(False)
    both = [permuted(x[:, k : k + 256], matrix) for k in range(0, x.shape[1], 256)]
    return jnp.concatenate([y[:, :128] for y in both], 1), jnp.concatenate([y[:, 128:] for y in both], 1)


def merge_pairs(even, odd):
    if even.shape[1] < MATRIX_FROM:
        return merge_by_picks(even, odd)
    matrix = pairing(True)
    return jnp.concatenate(
        [
            permuted(jnp.concatenate([even[:, k : k + 128], odd[:, k : k + 128]], 1), matrix)
            for k in range(0, even.shape[1], 128)
        ],
        1,
    )


def split_by_picks(x):
    rows = x.shape[0]
    lane = lax.broadcasted_iota(jnp.int32, (rows, 128), 1)
    lower = lane < 64
    near = jnp.where(lower, 2 * lane, 2 * lane - 127)
    far = jnp.where(lower, 2 * lane + 1, 2 * lane - 128)
    evens, odds = [], []
    for k in range(0, x.shape[1], 256):
        first, second = picked(x[:, k : k + 128], near), picked(x[:, k + 128 : k + 256], far)
        evens.append(jnp.where(lower, first, second))
        odds.append(pltpu.roll(jnp.where(lower, second, first), 64, 1))
    return jnp.concatenate(evens, 1), jnp.concatenate(odds, 1)


def merge_by_picks(even, odd):
    rows = even.shape[0]
    lane = lax.broadcasted_iota(jnp.int32, (rows, 128), 1)
    lower = lane < 64
    is_odd = lane % 2 == 1
    half = lane // 2
    near = jnp.where(is_odd, half + 64, half)
    far = jnp.where(is_odd, half, half + 64)
    out = []
    for k in range(0, even.shape[1], 128):
        e, o = even[:, k : k + 128], pltpu.roll(odd[:, k : k + 128], 64, 1)
        out += [picked(jnp.where(lower, e, o), near), picked(jnp.where(lower, o, e), far)]
    return jnp.concatenate(out, 1)


def tiles(width, body):
    def step(t, carry):
        body(t, pl.ds(pl.multiple_of(t * 128, 128), 128))
        return carry

    if width > 640:
        lax.fori_loop(0, width // 128, step, 0)
    else:
        for t in range(width // 128):
            body(t, slice(128 * t, 128 * t + 128))


def joined(ref, rows, width):
    return jnp.concatenate([ref[k, rows] for k in range(width // 128)], 1)


def spread(ref, rows, value):
    for k in range(value.shape[1] // 128):
        ref[k, rows] = value[:, 128 * k : 128 * k + 128]


def ends(axis):
    position = lax.axis_index(axis)
    return position % 2 == 0, position == 0, position == lax.axis_size(axis) - 1


def edges_kernel(x_ref, for_even, for_odd, sems):
    is_even = ends("cols")[0]
    right = jnp.where(is_even, COLS - 128, 0)
    copies = []
    for k, (at, out) in enumerate(((right, for_even), (COLS - 128 - right, for_odd))):
        lanes = pl.ds(pl.multiple_of(at, 128), 128)
        copies.append(pltpu.make_async_copy(x_ref.at[:, lanes], out, sems.at[k]))
        copies[-1].start()
    for copy in copies:
        copy.wait()


def inner_kernel(t_ref, x_ref, e_ref, o_ref, edge_ref, limit_ref):
    for level in range(LEVELS):
        for kind in range(3):
            limit_ref[3 * level + kind : 3 * level + kind + 1, :] = jnp.full((1, 128), t_ref[level, kind])
    e_ref[...], o_ref[...] = split_pairs(x_ref[:, 128 : COLS - 128])
    edge_ref[:, :128] = x_ref[:, :128]
    edge_ref[:, 128:] = x_ref[:, COLS - 128 :]


def columns_kernel(
    e_ref, o_ref, edge_ref, odd_ref, even_ref, for_even, for_odd, for_even_far, for_odd_far,
    low_ref, high_ref, low_low_ref, low_high_ref, one_ref, two_ref, one_high_ref,
    x_ref, y_ref,
):
    is_even, at_start, at_end = ends("cols")
    left = jnp.where(is_even, odd_ref[...], even_ref[...])
    right = jnp.where(is_even, even_ref[...], odd_ref[...])
    first = split_pairs(jnp.concatenate([left, edge_ref[:, :128]], 1))
    last = split_pairs(jnp.concatenate([edge_ref[:, 128:], right], 1))
    low, high = lift_lanes(
        jnp.concatenate([first[0], e_ref[...], last[0]], 1),
        jnp.concatenate([first[1], o_ref[...], last[1]], 1),
        EDGE[0],
        1024,
        at_start,
        at_end,
    )
    spread(low_ref, slice(None), low)
    spread(high_ref, slice(None), high)
    wide = WIDE[1]
    low = jnp.concatenate([low, jnp.zeros((ROWS, 2 * wide - WIDE[0]), jnp.float32)], 1)
    low, high = lift_lanes(*split_pairs(low), EDGE[1], 512, at_start, at_end)
    spread(low_low_ref, slice(None), low)
    spread(low_high_ref, slice(None), high)
    for t in range(wide // 128):
        one_ref[t] = plain_low(low_low_ref, t, 32)
        two_ref[t] = plain_low(one_ref, t, 16)
        one_high_ref[t] = plain_low(low_high_ref, t, 32)
    row = lax.axis_index("rows")
    below = (row % 2 == 0).astype(jnp.int32)
    for pack, last in ((for_even, below), (for_odd, 1 - below)):
        for t in range(wide // 128):
            at = PIECE * t
            pack[at : at + 8] = low_low_ref[t, 0:8]
            pack[at + 8 : at + 16] = low_low_ref[t, 56:64]
            pack[at + 16 : at + 24] = one_ref[t, 2:10]
            pack[at + 24 : at + 32] = one_ref[t, 22:30]
            pack[at + 32 : at + 42] = two_ref[t, 3:13]
            pack[at + 42 : at + 50] = low_high_ref[t, pl.ds(56 * last, 8)]
            pack[at + 50 : at + 58] = one_high_ref[t, pl.ds(2 + 20 * last, 8)]
        for j in range(9):
            pack[EDGES + 8 * j : EDGES + 8 * j + 8] = high_ref[j, pl.ds(56 * last, 8)]
    for t in range(wide // 128):
        s = slice(128 * t, 128 * t + 128)
        x_ref[0:8, s], x_ref[8:16, s] = low_low_ref[t, 0:8], low_low_ref[t, 56:64]
        x_ref[16:24, s], x_ref[24:32, s] = one_ref[t, 2:10], one_ref[t, 22:30]
        x_ref[32:42, s] = two_ref[t, 3:13]
    spread(y_ref, slice(None), split_lanes(2, x_ref[...])[0])
    below = (row % 4 < 2).astype(jnp.int32)
    for pack, last in ((for_even_far, below), (for_odd_far, 1 - below)):
        for t in range(WIDE[2] // 128):
            at = FAR_PIECE * t
            pack[at : at + 8] = y_ref[t, pl.ds(8 * last, 8)]
            pack[at + 8 : at + 16] = y_ref[t, pl.ds(16 + 8 * last, 8)]
            pack[at + 16 : at + 25] = y_ref[t, pl.ds(32 + last, 9)]


PIECE, EDGES, PACK = 58, 296, 368
FAR_PIECE, FAR_PACK = 25, 80


def plain_low(ref, t, tall):
    near = (lambda x: pltpu.roll(x, 1, 0)), (lambda x: pltpu.roll(x, tall - 1, 0))
    return forward_lift(ref[t, pl.ds(0, tall, stride=2)], ref[t, pl.ds(1, tall, stride=2)], near)[0]


def sides(flag, odd_ref, even_ref):
    def above(*at):
        return jnp.where(flag, odd_ref[at], even_ref[at])

    def under(*at):
        return jnp.where(flag, even_ref[at], odd_ref[at])

    return above, under


def halves_of(ref, t, tall):
    return ref[t, pl.ds(0, tall, stride=2)], ref[t, pl.ds(1, tall, stride=2)]


def lifted(ref, t, tall, begin, own):
    row, count = lax.axis_index("rows"), lax.axis_size("rows")
    starts, stops = [(begin, row == 0)], [(begin + own - 1, row == count - 1)]
    if begin >= own:
        starts.append((begin - own, row == 1))
        stops.append((begin + 2 * own - 1, row == count - 2))
    return forward_lift(*halves_of(ref, t, tall), neighbours(0, starts, stops))


def across(level, low, high):
    _, at_start, at_end = ends("cols")
    halves = lift_lanes(low, high, EDGE[level], 1024 >> level, at_start, at_end, inverse=True)
    return merge_pairs(*halves)


def split_lanes(level, band):
    _, at_start, at_end = ends("cols")
    wide = WIDE[level]
    pad = jnp.zeros((band.shape[0], 2 * wide - band.shape[1]), jnp.float32)
    halves = split_pairs(jnp.concatenate([band, pad], 1))
    return lift_lanes(*halves, EDGE[level], 1024 >> level, at_start, at_end)


def limited(limits, level, kind, coeffs):
    at = 3 * level + kind
    return soften(coeffs, limits[at : at + 1, :])


def near_kernel(
    limits, own_low, own_high, own_low_low, own_low_high, odd_ref, even_ref,
    ah0_ref, vh0_ref, ah1_ref, vh1_ref, ah2_ref, vh2_ref, next_ref, edge_ref,
    l_ref, h_ref, b_ref, x_ref, lh_ref, hh_ref, hl_ref,
):
    above, under = sides(lax.axis_index("rows") % 2 == 0, odd_ref, even_ref)
    for t in range(WIDE[1] // 128):
        at = PIECE * t
        s = slice(128 * t, 128 * t + 128)

        def part(offset, size=8, at=at):
            return slice(at + offset, at + offset + size)

        x_ref[0, 0:8], x_ref[0, 8:72], x_ref[0, 72:80] = above(part(8)), own_low_low[t], under(part(0))
        x_ref[1, 0:8], x_ref[1, 8:72], x_ref[1, 72:80] = above(part(42)), own_low_high[t], under(part(42))
        l_ref[t, 8:48] = lifted(x_ref, 0, 40, 4, 32)[0]
        l_ref[t, 2:10], l_ref[t, 46:54] = above(part(24)), under(part(16))
        h_ref[t, 8:48] = lifted(x_ref, 1, 40, 4, 32)[0]
        h_ref[t, 2:10], h_ref[t, 46:54] = above(part(50)), under(part(50))
        low, high = lifted(l_ref, t, 32, 6, 16)
        lh_ref[0:24, s] = limited(limits, 1, 1, high[2:26])
        b_ref[3:13, s], b_ref[13:35, s], b_ref[35:45, s] = above(part(32, 10)), low[3:25], under(part(32, 10))
        b_ref[48:56, s], b_ref[56:64, s] = above(part(0)), under(part(8))
        b_ref[64:72, s], b_ref[72:80, s] = above(part(16)), under(part(24))
        low, high = lifted(h_ref, t, 32, 6, 16)
        hl_ref[0:24, s] = limited(limits, 1, 0, low[2:26])
        hh_ref[0:24, s] = limited(limits, 1, 2, high[2:26])
    ah1_ref[...] = across(1, None, hl_ref[0:24, :640])[:, :1152]
    vh1_ref[...] = across(1, lh_ref[0:24, :640], hh_ref[0:24, :640])[:, :1152]
    low, high = split_lanes(2, b_ref[...])
    spread(next_ref, slice(None), low[0:48])
    spread(edge_ref, slice(None), low[48:80])
    spread(h_ref, slice(0, 48), high[0:48])
    for t in range(WIDE[2] // 128):
        s = slice(128 * t, 128 * t + 128)
        high = lifted(next_ref, t, 24, 8, 8)[1]
        lh_ref[0:16, s] = limited(limits, 2, 1, high[4:20])
        low, high = lifted(h_ref, t, 24, 8, 8)
        hl_ref[0:16, s] = limited(limits, 2, 0, low[4:20])
        hh_ref[0:16, s] = limited(limits, 2, 2, high[4:20])
    ah2_ref[...] = across(2, None, hl_ref[0:16, :384])[:, :640]
    vh2_ref[...] = across(2, lh_ref[0:16, :384], hh_ref[0:16, :384])[:, :640]
    low, high = (
        jnp.concatenate(
            [
                jnp.concatenate([side(slice(PIECE * t + at, PIECE * t + at + 8)) for t in range(5)], 1)
                for side, at in sources
            ],
            0,
        )
        for sources in (((above, 8), (under, 0)), ((above, 42), (under, 42)))
    )
    lows = across(1, low, high)
    for j in range(9):
        x_ref[j, 0:8] = lows[0:8, 128 * j : 128 * j + 128]
        x_ref[j, 8:72] = own_low[j]
        x_ref[j, 72:80] = lows[8:16, 128 * j : 128 * j + 128]
        at = slice(EDGES + 8 * j, EDGES + 8 * j + 8)
        x_ref[j + 9, 0:8] = above(at)
        x_ref[j + 9, 8:72] = own_high[j]
        x_ref[j + 9, 72:80] = under(at)

    def lift(t, s):
        high = lifted(x_ref, t, 40, 4, 32)[1]
        lh_ref[:, s] = limited(limits, 0, 1, high)
        low, high = lifted(x_ref, t + 9, 40, 4, 32)
        hl_ref[:, s] = limited(limits, 0, 0, low)
        hh_ref[:, s] = limited(limits, 0, 2, high)

    tiles(WIDE[0], lift)
    ah0_ref[...] = across(0, None, hl_ref[...])[:, 128 : 128 + COLS]
    vh0_ref[...] = across(0, lh_ref[...], hh_ref[...])[:, 128 : 128 + COLS]


def far_kernel(
    limits, ah0_ref, vh0_ref, ah1_ref, vh1_ref, ah2_ref, vh2_ref, next_ref, edge_ref,
    odd_far, even_far, out_ref, f_ref, g_ref, l_ref, h_ref, b_ref, v_ref, r_ref, o_ref, sems,
):
    row, count = lax.axis_index("rows"), lax.axis_size("rows")
    above_far, under_far = sides(row % 4 < 2, odd_far, even_far)
    for t in range(WIDE[2] // 128):
        s = slice(128 * t, 128 * t + 128)

        def far_part(offset, size=8, at=FAR_PIECE * t):
            return slice(at + offset, at + offset + size)

        f_ref[t, 0:8], f_ref[t, 8:24], f_ref[t, 24:32] = (
            above_far(far_part(0)), edge_ref[t, 0:16], under_far(far_part(0))
        )
        near = neighbours(0, [(4, row == 1)], [(11, row == count - 2)])
        one = forward_lift(*halves_of(f_ref, t, 16), near)[0]
        g_ref[t, 10:14], g_ref[t, 42:46] = one[2:6], one[10:14]
        g_ref[t, 2:10], g_ref[t, 14:22] = above_far(far_part(8)), edge_ref[t, 16:24]
        g_ref[t, 34:42], g_ref[t, 46:54] = edge_ref[t, 24:32], under_far(far_part(8))
        near = neighbours(0, [(6, row == 1)], [(21, row == count - 2)])
        two = forward_lift(*halves_of(g_ref, t, 32), near)[0]
        l_ref[t, 0:9], l_ref[t, 9:15] = above_far(far_part(16, 9)), two[3:9]
        l_ref[t, 15:57] = next_ref[t, 3:45]
        l_ref[t, 57:63], l_ref[t, 63:72] = two[19:25], under_far(far_part(16, 9))
        b_ref[0:32, s] = lifted(l_ref, t, 40, 14, 8)[0][2:34]
    low, high = split_lanes(3, b_ref[0:32, :384])
    spread(l_ref, slice(0, 32), low)
    spread(h_ref, slice(0, 32), high)
    for t in range(WIDE[3] // 128):
        s = slice(128 * t, 128 * t + 128)
        low, high = lifted(l_ref, t, 16, 6, 4)
        v_ref[0:12, s] = low[2:14]
        v_ref[16:28, s] = limited(limits, 3, 1, high[2:14])
        low, high = lifted(h_ref, t, 16, 6, 4)
        r_ref[0:12, s] = limited(limits, 3, 0, low[2:14])
        r_ref[16:28, s] = limited(limits, 3, 2, high[2:14])
    both = across(3, v_ref[0:32, :256], r_ref[0:32, :256])[:, :384]
    low, high = both[0:16], both[16:32]
    _, at_start, at_end = ends("rows")
    for level in (3, 2, 1):
        own = OWN[level]
        long = max(own + 8, 16)
        near = neighbours(0, [(4, at_start)], [(3 + own, at_end)])
        for t in range(low.shape[1] // 128):
            s = slice(128 * t, 128 * t + 128)
            even, odd = inverse_lift(low[0:long, s], high[0:long, s], near)
            o_ref[t, pl.ds(0, long, stride=2)] = even
            o_ref[t, pl.ds(1, long, stride=2)] = odd
        size = OWN[level - 1] + 8
        low = joined(o_ref, slice(4, 4 + size), low.shape[1])
        added, high = ((ah0_ref, vh0_ref), (ah1_ref, vh1_ref), (ah2_ref, vh2_ref))[level - 1]
        low = across(level - 1, low, None)
        low = low[:, 128 : 128 + COLS] if level == 1 else low[:, : high.shape[1]]
        low = low + added[...]
    v_ref[...] = low
    near = neighbours(0, [(4, at_start)], [(35, at_end)])

    def finish(i, carry):
        for t in (2 * i, 2 * i + 1):
            s = pl.ds(pl.multiple_of(128 * t, 128), 128)
            even, odd = inverse_lift(v_ref[:, s], vh0_ref[:, s], near)
            o_ref[t, pl.ds(0, 40, stride=2)] = even
            o_ref[t, pl.ds(1, 40, stride=2)] = odd
            pltpu.make_async_copy(o_ref.at[t, 8:72], out_ref.at[:, s], sems.at[t]).start()
        return carry

    lax.fori_loop(0, COLS // 256, finish, 0)
    for t in range(COLS // 128):
        lanes = slice(128 * t, 128 * t + 128)
        pltpu.make_async_copy(o_ref.at[t, 8:72], out_ref.at[:, lanes], sems.at[t]).wait()


def swaps(axis, offset, apart):
    count = lax.axis_size(axis)
    pairs = []
    for block in range(offset, count, 2 * apart):
        for i in range(block, min(block + apart, count - apart)):
            pairs += [(i, i + apart), (i + apart, i)]
    return pairs


def exchange(for_even, for_odd, axis, apart=1):
    even = lax.ppermute(for_even, axis, swaps(axis, 0, apart))
    odd = lax.ppermute(for_odd, axis, swaps(axis, apart, apart))
    return odd, even


def f32(*shape):
    return jax.ShapeDtypeStruct(shape, jnp.float32)


def scratch(*shape):
    return pltpu.VMEM(shape, jnp.float32)


def call(kernel, outs, scratches, *args, scalars=0, space=pltpu.VMEM, out_space=pltpu.VMEM, cost=None):
    vmem = pl.BlockSpec(memory_space=pltpu.VMEM)
    smem = pl.BlockSpec(memory_space=pltpu.SMEM)
    return pl.pallas_call(
        kernel,
        out_shape=outs,
        in_specs=[smem] * scalars + [pl.BlockSpec(memory_space=space)] * (len(args) - scalars),
        out_specs=jax.tree.map(lambda _: pl.BlockSpec(memory_space=out_space), outs),
        scratch_shapes=scratches,
        compiler_params=pltpu.CompilerParams(vmem_limit_bytes=16 * 2**20),
        cost_estimate=cost,
    )(*args)


def local(micrograph, thresholds):
    for_even, for_odd = call(
        edges_kernel,
        (f32(ROWS, 128), f32(ROWS, 128)),
        [pltpu.SemaphoreType.DMA((2,))],
        micrograph,
        space=pltpu.HBM,
    )
    odd, even = exchange(for_even, for_odd, "cols")
    *inner, limits = call(
        inner_kernel,
        (f32(ROWS, 896), f32(ROWS, 896), f32(ROWS, 256), f32(16, 128)),
        [],
        thresholds,
        micrograph,
        scalars=1,
        cost=pl.CostEstimate(flops=2 * 10**9, bytes_accessed=4 * 10**6, transcendentals=0),
    )
    for_even, for_odd, for_even_far, for_odd_far, *own = call(
        columns_kernel,
        (f32(PACK, 128), f32(PACK, 128), f32(FAR_PACK, 128), f32(FAR_PACK, 128))
        + (f32(9, ROWS, 128), f32(9, ROWS, 128), f32(5, ROWS, 128), f32(5, ROWS, 128)),
        [scratch(5, 32, 128), scratch(5, 16, 128), scratch(5, 32, 128), scratch(48, 640), scratch(3, 48, 128)],
        *inner,
        odd,
        even,
    )
    near = exchange(for_even, for_odd, "rows")
    far = exchange(for_even_far, for_odd_far, "rows", 2)
    known = call(
        near_kernel,
        (f32(40, COLS), f32(40, COLS), f32(24, 1152), f32(24, 1152), f32(16, 640), f32(16, 640))
        + (f32(3, 48, 128), f32(3, 32, 128)),
        [scratch(5, 64, 128), scratch(5, 64, 128), scratch(80, 640), scratch(18, 80, 128)]
        + [scratch(40, 1152), scratch(40, 1152), scratch(40, 1152)],
        limits,
        *own,
        *near,
        cost=pl.CostEstimate(flops=2 * 10**9, bytes_accessed=4 * 10**6, transcendentals=0),
    )
    return call(
        far_kernel,
        f32(ROWS, COLS),
        [scratch(3, 32, 128), scratch(3, 64, 128), scratch(3, 80, 128), scratch(3, 80, 128)]
        + [scratch(32, 384), scratch(40, COLS), scratch(32, 256), scratch(16, 80, 128)]
        + [pltpu.SemaphoreType.DMA((16,))],
        limits,
        *known,
        *far,
        out_space=pl.ANY,
    )


def solution(mesh):
    placed = (P("rows", "cols"), P())
    return jax.shard_map(
        local, mesh=mesh, in_specs=placed, out_specs=P("rows", "cols"), check_vma=False
    )
```
